512 devices in a mesh: dp: 32 (over y_lo, z), ctx: 16 (over x, y_hi, core).
Axes of the slice: x: 4, y: 4 (y_hi: 2, y_lo: 2; y = y_hi * 2 + y_lo), z: 16, core: 2. Of those that a mesh axis runs over, the one named last changes fastest.
Arguments:
- hidden_in: bfloat16 [32, 2048, 8192], P('dp', 'ctx'), may hold values from -6 to 6
- query: bfloat16 [32, 2048, 1024], P('dp', 'ctx'), may hold values from -88 to 88
- key_value: bfloat16 [32, 2048, 256], P('dp', 'ctx'), may hold values from -4 to 4
- grad_out: bfloat16 [32, 2048, 1024], P('dp', 'ctx'), may hold values from -6 to 6
- lengths: int32 [32, 8], P('dp'), may hold values from 1 to 1792, 2048 in all within a row
- owner: int32 [64, 1], replicated, may hold values from 0 to 31; in each aligned block of 64 rows (0 to 63, 64 to 127, ...) at most 4 rows name the same one
Outputs:
- grad_query: bfloat16 [32, 2048, 1024], P('dp', 'ctx')
- grad_kv: bfloat16 [32, 2048, 256], P('dp', 'ctx')
- factors: float32 [32, 4, 2, 128, 128], P('dp')
The draws below stay inside these ranges and needn't reach their ends.
Inputs may be any that keep to these rules, and one draw needn't show every extreme that they name: `lengths`: each row sums to 2048; its longest document has exactly 1792 positions. No owner holds more than 4 tiles, one holds exactly 4, and every owner holds one or more.
All inputs are finite; a program needn't handle non-finite values.
Results may differ from the reference program's by a relative error of at most 0.017.
Values may be sent and summed in bfloat16 or wider, within the bound.
No kernel may reach another device: no remote copies, remote signals or barrier semaphores. Data moves between devices by JAX's collectives and lax.ppermute only.
A program may use at most 64 MiB of HBM per device.

```python
import math
import jax
import jax.numpy as jnp
import numpy as np
from jax import lax

D = 8192
HEADS = 8
HD = 128
TILE = 128
DOCS = 8
SEQ = 2048
BATCH = 32
DOC_MOST = 1792
TILES = 64
CAP = 4
N_DP = 32


def shared_keys(key):
    base = jnp.clip(jax.random.normal(jax.random.fold_in(key, 11), (BATCH, SEQ, HD), jnp.float32), -4.0, 4.0)
    keys = base
    return keys


def draw_query(key, part):
    key = jax.random.fold_in(key, 1)
    base = 2.5 * jnp.clip(jax.random.normal(key, (BATCH, SEQ, HEADS, HD), jnp.float32), -4.0, 4.0)
    mixed = base
    return mixed.reshape(BATCH, SEQ, HEADS * HD).astype(jnp.bfloat16)


def draw_key_value(key, part):
    keys = shared_keys(key)
    key = jax.random.fold_in(key, 2)
    values = jnp.clip(jax.random.normal(key, (BATCH, SEQ, HD), jnp.float32), -4.0, 4.0)
    return jnp.concatenate([keys, values], axis=2).astype(jnp.bfloat16)


def block_levels(stream_key, shape, cuts, least, top_value):
    loudness, own = 1.0, jax.random.fold_in(stream_key, 6)
    for dim, parts in cuts:
        heights = jnp.exp(jax.random.uniform(jax.random.fold_in(own, dim), (parts,), jnp.float32, least / len(cuts), top_value / len(cuts)))
        loudness = loudness * jnp.repeat(heights, shape[dim] // parts).reshape([-1 if axis == dim else 1 for axis in range(len(shape))])
    return loudness


def profile(count, total, most, skew):
    weights = [(1 << 20) // math.isqrt(grade ** skew) + 1 for grade in range(2, count + 1)]
    spare, holding = total - most - (count - 1), [1] * (count - 1)
    while spare > 0:
        candidates = [i for i in range(count - 1) if holding[i] < most]
        mass, left = sum([weights[i] for i in candidates]), spare
        for i in candidates:
            extra = min(most - holding[i], max(1, left * weights[i] // mass), spare)
            holding[i] = holding[i] + extra
            spare = spare - extra
    return np.array([most] + holding)


def ragged_sizes(rng, count, total, bound, skew):
    if count == 2:
        one = jax.random.randint(rng, (), max(1, total - bound), min(bound, total - 1) + 1)
        return jnp.stack([one, total - one])
    sizes = jnp.asarray(profile(count, total, bound, skew), jnp.int32)
    couples = (count - 1) // 2
    donor, sink = sizes[1:1 + 2 * couples:2], sizes[2:2 + 2 * couples:2]
    margin = jnp.minimum(donor - 1, bound - sink)
    moved = jax.random.randint(jax.random.fold_in(rng, 1), (couples,), 0, 1 << 20) % (margin + 1)
    sizes = sizes.at[1:1 + 2 * couples:2].set(donor - moved).at[2:2 + 2 * couples:2].set(sink + moved)
    return sizes[jax.random.permutation(jax.random.fold_in(rng, 2), count)]


def assign_block(rng, own, number, rows, number_of, top, bound, slope):
    ranking = jax.random.permutation(rng, number_of)
    packed, usual = shares(number_of, rows * top, bound, slope, True), shares(number_of, rows * top, bound, slope, False)
    places = jnp.arange(number_of)

    def named(tallies, turn):
        used = int((tallies > 0).sum())
        fixed = max(1, used // 4)
        moved = fixed + (places - fixed + turn * (used - fixed)) % max(1, number_of - fixed)
        return jnp.zeros((number_of,), jnp.int32).at[ranking[jnp.where(places < fixed, places, moved)]].set(jnp.asarray(tallies, jnp.int32))

    tallies = jnp.where(number % 4 == 0, named(packed, number // 4), named(usual, number - number // 4 - 1))
    mixed = jax.random.permutation(jax.random.fold_in(own, 3), number_of)
    giver, receiver = mixed[0:number_of // 2 * 2:2], mixed[1:number_of // 2 * 2:2]
    margin = jnp.minimum(tallies[giver] - 1, bound - tallies[receiver]) // 2
    margin = jnp.where((giver == ranking[0]) | (receiver == ranking[0]) | (tallies[receiver] == 0), 0, jnp.maximum(margin, 0))
    moved = jax.random.randint(jax.random.fold_in(own, 4), (number_of // 2,), 0, 1 << 20) % (margin + 1)
    tallies = tallies.at[giver].add(-moved).at[receiver].add(moved)
    items = jnp.searchsorted(jnp.cumsum(tallies), jnp.arange(rows * top), side="right").astype(jnp.int32)
    table = items.reshape(top, rows).T
    table = table[jax.random.permutation(jax.random.fold_in(own, 1), rows)]
    turn = jax.random.randint(jax.random.fold_in(own, 2), (rows, 1), 0, top)
    return jnp.take_along_axis(table, (jnp.arange(top)[None, :] + turn) % top, axis=1)


def shares(amount, total, most, slope, full):
    portions = [(1 << 20) // math.isqrt(rank ** slope) + 1 for rank in range(1, amount + 1)]
    largest = most if full else min(most, max(-(-total // amount), total * portions[0] // sum(portions)))
    least = 1 if total - largest >= amount - 1 else 0
    counts, spare = [largest] + [least] * (amount - 1), total - largest - least * (amount - 1)
    while spare > 0:
        movable = [i for i in range(1, amount) if counts[i] < largest] or [i for i in range(1, amount) if counts[i] < most]
        whole, budget = sum([portions[i] for i in movable]), spare
        for i in movable:
            more = min(most - counts[i], max(1, budget * portions[i] // whole), spare)
            counts[i] = counts[i] + more
            spare = spare - more
    return np.array(counts)


def centred(rng, extent, scale, most, cuts=(), kind=jnp.bfloat16):
    values = jax.random.normal(rng, extent, jnp.float32) * scale
    if len(cuts) > 0:
        values = block_levels(rng, extent, cuts, -0.22, 0.18) * values
    return jnp.clip(values, min=-most, max=most).astype(kind)


def setup_inputs(seed: int = 0) -> dict:
    streams_of = jax.random.split(jax.random.key(seed), 7)
    hidden_in = centred(streams_of[0], (BATCH, SEQ, D), 1.0, 6.0, ((0, 32), (1, 16)))
    query = draw_query(jax.random.fold_in(streams_of[6], 71), 0)
    key_value = draw_key_value(jax.random.fold_in(streams_of[6], 71), 0)
    grad_out = centred(streams_of[3], (BATCH, SEQ, HEADS * HD), 1.0, 6.0, ((0, 32), (1, 16)))
    lengths = jax.vmap(lambda own: ragged_sizes(own, DOCS, SEQ, DOC_MOST, 2))(jax.random.split(streams_of[4], BATCH)).reshape((BATCH, DOCS)).astype(jnp.int32)
    owner_keys = jax.random.split(jax.random.fold_in(streams_of[5], 1), TILES // TILES)
    owner_turns = jax.random.permutation(jax.random.fold_in(streams_of[5], 3), TILES // TILES)
    owner = jax.vmap(lambda own, number: assign_block(jax.random.fold_in(streams_of[5], 2), own, number, TILES, N_DP, 1, CAP, 2))(owner_keys, owner_turns).reshape((TILES, 1))
    return {"hidden_in": hidden_in, "query": query, "key_value": key_value, "grad_out": grad_out, "lengths": lengths, "owner": owner}


masked_value = -1e+30

def doc_of(positions, doc_ends):
    return lax.optimization_barrier(jnp.sum((positions[:, None] >= doc_ends[None, :]).astype(jnp.int32), axis=1)).astype(jnp.int32)

def owner_slots(owner_col, owner_count, slot_count):
    tile_count = owner_col.shape[0]
    tile_order = jnp.arange(tile_count, dtype=jnp.int32)
    same_owner = owner_col[:, None] == owner_col[None, :]
    owner_rank = lax.optimization_barrier(jnp.sum((same_owner & (tile_order[None, :] < tile_order[:, None])).astype(jnp.int32), axis=1)).astype(jnp.int32)
    owner_ids = jnp.arange(owner_count, dtype=jnp.int32)
    slot_ids = jnp.arange(slot_count, dtype=jnp.int32)
    slot_table = (owner_col[None, None, :] == owner_ids[:, None, None]) & (owner_rank[None, None, :] == slot_ids[None, :, None])
    return slot_table.astype(jnp.float32)

def lowered(values):
    return lax.optimization_barrier(values.astype(jnp.bfloat16)).astype(jnp.float32)

def sequence_backward(query_seq, kv_seq, grad_seq, length_row):
    score_scale = 1.0 / math.sqrt(HD)
    key_rows = kv_seq[:, :HD].astype(jnp.float32)
    value_rows = kv_seq[:, HD:].astype(jnp.float32)
    doc_ends = jnp.cumsum(length_row).astype(jnp.int32)
    key_pos = jnp.arange(SEQ, dtype=jnp.int32)
    key_doc = doc_of(key_pos, doc_ends)
    query_block = min(256, SEQ)
    query_blocks = SEQ // query_block
    queries = query_seq.reshape(query_blocks, query_block, HEADS, HD)
    out_grads = grad_seq.reshape(query_blocks, query_block, HEADS, HD)

    def query_step(kv_grad, block_index):
        block_q = lax.dynamic_index_in_dim(queries, block_index, 0, keepdims=False).astype(jnp.float32)
        block_grads = lax.dynamic_index_in_dim(out_grads, block_index, 0, keepdims=False).astype(jnp.float32)
        query_pos = block_index * query_block + jnp.arange(query_block, dtype=jnp.int32)
        visible = (doc_of(query_pos, doc_ends)[:, None] == key_doc[None, :]) & (key_pos[None, :] <= query_pos[:, None])
        visible = visible[:, None, :]
        raw_scores = jnp.einsum('thd,kd->thk', block_q, key_rows) * score_scale
        masked = jnp.where(visible, raw_scores, masked_value)
        row_top = lax.optimization_barrier(jnp.max(masked, axis=2))
        weights = jnp.where(visible, jnp.exp(masked - row_top[..., None]), 0.0)
        weights = weights / lax.optimization_barrier(jnp.sum(weights, axis=2))[..., None]
        low_weights = lowered(weights)
        output = jnp.einsum('thk,kd->thd', low_weights, value_rows)
        row_delta = lax.optimization_barrier(jnp.sum(block_grads * output, axis=2))
        prob_grad = jnp.einsum('thd,kd->thk', block_grads, value_rows)
        score_grad = lowered(weights * (prob_grad - row_delta[..., None]))
        query_grad = (jnp.einsum('thk,kd->thd', score_grad, key_rows) * score_scale).astype(jnp.bfloat16)
        key_grad = jnp.einsum('thk,thd->kd', score_grad, block_q) * score_scale
        value_grad = jnp.einsum('thk,thd->kd', low_weights, block_grads)
        return (kv_grad + jnp.concatenate([key_grad, value_grad], axis=1), query_grad)
    kv_grad, query_grad = lax.scan(query_step, jnp.zeros((SEQ, 2 * HD), jnp.float32), jnp.arange(query_blocks, dtype=jnp.int32))
    return (kv_grad, query_grad.reshape(SEQ, HEADS * HD))

def reference(hidden_in, query, key_value, grad_out, lengths, owner):

    def per_sequence(weight_sum, sequence):
        hidden_seq, query_seq, kv_seq, grad_seq, length_row = sequence
        kv_grad, query_grad = sequence_backward(query_seq, kv_seq, grad_seq, length_row)
        kv_low = kv_grad.astype(jnp.bfloat16)
        weight = jnp.dot(hidden_seq.T, kv_low[:, :HD], preferred_element_type=jnp.float32)
        return (weight_sum + weight, (query_grad, kv_low))
    weight_grad, (grad_query, grad_kv) = lax.scan(per_sequence, jnp.zeros((D, HD), jnp.float32), (hidden_in, query, key_value, grad_out, lengths))
    gradient = weight_grad * (1.0 / math.sqrt(BATCH * SEQ))
    pieces = gradient.reshape(D // TILE, TILE, HD // TILE, TILE).transpose(0, 2, 1, 3).reshape(TILES, TILE, TILE)
    slot_table = owner_slots(owner[:, 0], N_DP, CAP)
    owned = jnp.einsum('ost,tab->osab', slot_table, pieces, precision=lax.Precision.HIGHEST)
    left_factor = jnp.einsum('osab,oscb->osac', owned, owned, precision=lax.Precision.HIGHEST) / TILE
    right_factor = jnp.einsum('osab,osac->osbc', owned, owned, precision=lax.Precision.HIGHEST) / TILE
    factors = jnp.stack([left_factor, right_factor], axis=2)
    return (grad_query, grad_kv, factors)
```

```python
import math

import jax
import jax.numpy as jnp
from jax import lax
from jax.experimental import pallas as pl
from jax.experimental.pallas import tpu as pltpu
from jax.sharding import Mesh
from jax.sharding import PartitionSpec as P

HEADS = 8
HD = 128
TILE = 128
ROWS = 128
CHIPS = 8
SEQ = 2048
TILES = 64
CAP = 4
N_DP = 32
MODEL = 8192
PAIR = 2 * ROWS
HIDDEN_NEG = -1e30
SCALE = 1.0 / math.sqrt(HD)
EXP2_SCALE = SCALE * math.log2(math.e)
F32 = jnp.float32
BF16 = jnp.bfloat16


def attention_kernel(
    lengths_ref, q_ref, go_ref, mine_ref, other_ref,
    dq_ref, dmine_ref, dother_ref,
    q_t, go_t, q_rows, go_rows, scores, prob_grads, ds_buf, w_buf, top, total, delta, dq_t,
):
    chip = lax.axis_index("chip")
    core = lax.axis_index("core")
    first = (2 * chip + core) * ROWS
    for h in range(HEADS):
        cols = pl.ds(h * HD, HD)
        qh = q_ref[:, cols]
        gh = go_ref[:, cols]
        q_t[:, cols] = qh.T
        go_t[:, cols] = gh.T
        q_rows[cols, :] = qh
        go_rows[cols, :] = gh
    row_pos = first + lax.broadcasted_iota(jnp.int32, (1, ROWS), 1)
    row_low = jnp.zeros((1, ROWS), jnp.int32)
    first_low = jnp.int32(0)
    end = jnp.int32(0)
    for d in range(lengths_ref.shape[1]):
        end = end + lengths_ref[0, d]
        row_low = jnp.maximum(row_low, jnp.where(row_pos >= end, end, 0))
        first_low = jnp.maximum(first_low, jnp.where(first >= end, end, 0))
    low_block = first_low // PAIR
    high_block = chip + 1
    top[...] = jnp.full(top.shape, HIDDEN_NEG, F32)
    total[...] = jnp.zeros(total.shape, F32)
    delta[...] = jnp.zeros(delta.shape, F32)
    dq_t[...] = jnp.zeros(dq_t.shape, F32)
    dmine_ref[...] = jnp.zeros(dmine_ref.shape, dmine_ref.dtype)
    dother_ref[...] = jnp.zeros(dother_ref.shape, dother_ref.dtype)

    def rows_of(j):
        return pl.ds(pl.multiple_of(j * PAIR, PAIR), PAIR)

    def sides(j):
        return ((mine_ref, core, 0), (other_ref, 1 - core, ROWS))

    def score_step(j, carry):
        base = pl.multiple_of(j * PAIR, PAIR)
        for ref, side, offset in sides(j):
            pos = (2 * j + side) * ROWS + lax.broadcasted_iota(jnp.int32, (ROWS, ROWS), 0)
            seen = (pos >= row_low) & (pos <= row_pos)
            keys = ref[j, :, :HD]
            for h in range(HEADS):
                cols = pl.ds(h * HD, HD)
                s = jnp.dot(keys, q_t[:, cols], preferred_element_type=F32)
                s = jnp.where(seen, s, HIDDEN_NEG)
                scores[pl.ds(base + offset, ROWS), cols] = s
                best = jnp.max(s.reshape(ROWS // 8, 8, ROWS), axis=0)
                top[:, cols] = jnp.maximum(top[:, cols], best)
        return carry

    lax.fori_loop(low_block, high_block, score_step, 0)
    top[0:1, :] = jnp.max(top[...], axis=0, keepdims=True)

    def weight_step(j, carry):
        base = pl.multiple_of(j * PAIR, PAIR)
        for ref, side, offset in sides(j):
            values = ref[j, :, HD:]
            for h in range(HEADS):
                cols = pl.ds(h * HD, HD)
                rows = pl.ds(base + offset, ROWS)
                p = jnp.exp2((scores[rows, cols] - top[0:1, cols]) * EXP2_SCALE)
                pg = jnp.dot(values, go_t[:, cols], preferred_element_type=F32)
                scores[rows, cols] = p
                prob_grads[rows, cols] = pg
                total[:, cols] += jnp.sum(p.reshape(ROWS // 8, 8, ROWS), axis=0)
                delta[:, cols] += jnp.sum((p * pg).reshape(ROWS // 8, 8, ROWS), axis=0)
        return carry

    lax.fori_loop(low_block, high_block, weight_step, 0)
    inverse = 1.0 / jnp.sum(total[...], axis=0, keepdims=True)
    total[0:1, :] = inverse
    delta[0:1, :] = jnp.sum(delta[...], axis=0, keepdims=True) * inverse

    def back_step(j, carry):
        base = pl.multiple_of(j * PAIR, PAIR)
        for h in range(HEADS):
            cols = pl.ds(h * HD, HD)
            rows = pl.ds(base, PAIR)
            w = scores[rows, cols] * total[0:1, cols]
            w_buf[:, cols] = w.astype(BF16)
            ds_buf[:, cols] = (w * (prob_grads[rows, cols] - delta[0:1, cols])).astype(BF16)
        ds = ds_buf[...]
        dk = jnp.dot(ds, q_rows[...], preferred_element_type=F32) * SCALE
        dv = jnp.dot(w_buf[...], go_rows[...], preferred_element_type=F32)
        dmine_ref[j, :, :HD] = dk[:ROWS]
        dmine_ref[j, :, HD:] = dv[:ROWS]
        dother_ref[j, :, :HD] = dk[ROWS:].astype(BF16)
        dother_ref[j, :, HD:] = dv[ROWS:].astype(BF16)
        keys = jnp.concatenate([mine_ref[j, :, :HD], other_ref[j, :, :HD]], axis=0)
        dq_t[...] += lax.dot_general(
            keys, ds, (((0,), (0,)), ((), ())), preferred_element_type=F32
        )
        return carry

    lax.fori_loop(low_block, high_block, back_step, 0)
    for h in range(HEADS):
        cols = pl.ds(h * HD, HD)
        dq_ref[:, cols] = (dq_t[:, cols].T * SCALE).astype(BF16)


def attention(lengths, query, grad_out, mine, other):
    vmem = pl.BlockSpec(memory_space=pltpu.VMEM)
    wide = HEADS * HD
    return pl.pallas_call(
        attention_kernel,
        out_shape=(
            jax.ShapeDtypeStruct((ROWS, wide), BF16),
            jax.ShapeDtypeStruct((CHIPS, ROWS, 2 * HD), F32),
            jax.ShapeDtypeStruct((CHIPS, ROWS, 2 * HD), BF16),
        ),
        in_specs=[pl.BlockSpec(memory_space=pltpu.SMEM), vmem, vmem, vmem, vmem],
        out_specs=(vmem, vmem, vmem),
        scratch_shapes=[
            pltpu.VMEM((HD, wide), BF16),
            pltpu.VMEM((HD, wide), BF16),
            pltpu.VMEM((wide, HD), BF16),
            pltpu.VMEM((wide, HD), BF16),
            pltpu.VMEM((SEQ, wide), F32),
            pltpu.VMEM((SEQ, wide), F32),
            pltpu.VMEM((PAIR, wide), BF16),
            pltpu.VMEM((PAIR, wide), BF16),
            pltpu.VMEM((8, wide), F32),
            pltpu.VMEM((8, wide), F32),
            pltpu.VMEM((8, wide), F32),
            pltpu.VMEM((HD, wide), F32),
        ],
        compiler_params=pltpu.CompilerParams(vmem_limit_bytes=44 * 1024 * 1024),
        name="attention_backward",
    )(lengths, query, grad_out, mine, other)


STEP_TILES = 8


def weight_kernel(parts_ref, hidden_ref, kv_ref, mine_ref, other_ref, k_t):
    core = lax.axis_index("core")

    @pl.when(pl.program_id(0) == 0)
    def _():
        low = jnp.sum(parts_ref[...].astype(F32), axis=0).astype(BF16)
        kv_ref[...] = low
        k_t[...] = low[:, :HD].T

    grad_t = jnp.dot(k_t[...], hidden_ref[...], preferred_element_type=F32)
    for pair in range(STEP_TILES // 2):
        even = grad_t[:, (2 * pair) * TILE : (2 * pair + 1) * TILE].reshape(CHIPS, 2, 8, TILE)
        odd = grad_t[:, (2 * pair + 1) * TILE : (2 * pair + 2) * TILE].reshape(CHIPS, 2, 8, TILE)
        both = [jnp.concatenate([even[:, c], odd[:, c]], axis=1) for c in range(2)]
        rows = pl.ds(pair * 16, 16)
        here = jnp.where(core == 0, both[0], both[1])
        there = jnp.where(core == 0, both[1], both[0])
        mine_ref[:, rows, :] = here
        other_ref[:, rows, :] = there.astype(BF16)


def weight_terms(parts, hidden):
    steps = TILES // STEP_TILES
    rows = STEP_TILES * 8
    return pl.pallas_call(
        weight_kernel,
        grid=(steps,),
        out_shape=(
            jax.ShapeDtypeStruct((ROWS, 2 * HD), BF16),
            jax.ShapeDtypeStruct((CHIPS, TILES * 8, TILE), F32),
            jax.ShapeDtypeStruct((CHIPS, TILES * 8, TILE), BF16),
        ),
        in_specs=[
            pl.BlockSpec((CHIPS, ROWS, 2 * HD), lambda i: (0, 0, 0)),
            pl.BlockSpec((ROWS, STEP_TILES * TILE), lambda i: (0, i)),
        ],
        out_specs=(
            pl.BlockSpec((ROWS, 2 * HD), lambda i: (0, 0)),
            pl.BlockSpec((CHIPS, rows, TILE), lambda i: (0, i, 0)),
            pl.BlockSpec((CHIPS, rows, TILE), lambda i: (0, i, 0)),
        ),
        scratch_shapes=[pltpu.VMEM((HD, ROWS), BF16)],
        compiler_params=pltpu.CompilerParams(vmem_limit_bytes=32 * 1024 * 1024),
        name="weight_gradient",
    )(parts, hidden)


def owner_kernel(owner_ref, parts_ref, out_ref, sums, placed, held):
    sums[...] = jnp.sum(parts_ref[...].astype(F32), axis=0)
    placed[...] = jnp.zeros(placed.shape, F32)
    for o in range(N_DP):
        held[o] = 0

    def place(t, carry):
        o = owner_ref[t, 0]
        slot = held[o]
        held[o] = slot + 1
        to = pl.multiple_of((o * CAP + slot) * 8, 8)
        placed[pl.ds(to, 8), :] = sums[pl.ds(pl.multiple_of(t * 8, 8), 8), :]
        return carry

    lax.fori_loop(0, TILES, place, 0)
    out_ref[...] = placed[...].astype(BF16).reshape(out_ref.shape)


def to_owners(owner, parts):
    vmem = pl.BlockSpec(memory_space=pltpu.VMEM)
    return pl.pallas_call(
        owner_kernel,
        out_shape=jax.ShapeDtypeStruct((N_DP, CAP * 8, TILE), BF16),
        in_specs=[pl.BlockSpec(memory_space=pltpu.SMEM), vmem],
        out_specs=vmem,
        scratch_shapes=[
            pltpu.VMEM((TILES * 8, TILE), F32),
            pltpu.VMEM((N_DP * CAP * 8, TILE), F32),
            pltpu.SMEM((N_DP,), jnp.int32),
        ],
        compiler_params=pltpu.CompilerParams(vmem_limit_bytes=32 * 1024 * 1024),
        name="owner_slots",
    )(owner, parts)


def sum_kernel(parts_ref, out_ref):
    gradient = jnp.sum(parts_ref[...].astype(F32), axis=0) * (1.0 / math.sqrt(N_DP * SEQ))
    out_ref[...] = jnp.broadcast_to(gradient.astype(BF16)[None], out_ref.shape)


def owned_sum(parts):
    vmem = pl.BlockSpec(memory_space=pltpu.VMEM)
    return pl.pallas_call(
        sum_kernel,
        out_shape=jax.ShapeDtypeStruct((2 * CHIPS, CAP * 8, TILE), BF16),
        in_specs=[vmem],
        out_specs=vmem,
        name="owned_sum",
    )(parts)


def factor_kernel(pieces_ref, out_ref):
    pieces = pieces_ref[...].astype(F32)
    for s in range(CAP):
        grad_t = pieces[:, s * 8 : (s + 1) * 8, :].reshape(TILE, TILE)
        low = grad_t.astype(BF16)
        low_t = grad_t.T.astype(BF16)
        out_ref[s, 0] = jnp.dot(low_t, low, preferred_element_type=F32) * (1.0 / TILE)
        out_ref[s, 1] = jnp.dot(low, low_t, preferred_element_type=F32) * (1.0 / TILE)


def factors_of(pieces):
    vmem = pl.BlockSpec(memory_space=pltpu.VMEM)
    return pl.pallas_call(
        factor_kernel,
        out_shape=jax.ShapeDtypeStruct((CAP, 2, TILE, TILE), F32),
        in_specs=[vmem],
        out_specs=vmem,
        name="factors",
    )(pieces)


SWAP = ((0, 1), (1, 0))


def body(hidden_in, query, key_value, grad_out, lengths, owner):
    mine = lax.all_to_all(
        jnp.broadcast_to(key_value, (CHIPS, ROWS, 2 * HD)), "chip", 0, 0, tiled=True
    )
    other = lax.ppermute(mine, "core", SWAP)
    grad_query, dkv_mine, dkv_other = attention(lengths, query[0], grad_out[0], mine, other)
    dkv = (dkv_mine + lax.ppermute(dkv_other, "core", SWAP).astype(F32)).astype(BF16)
    dkv = lax.all_to_all(dkv, "chip", 0, 0, tiled=True)
    grad_kv, wg_mine, wg_other = weight_terms(dkv, hidden_in[0])
    wg = (wg_mine + lax.ppermute(wg_other, "core", SWAP).astype(F32)).astype(BF16)
    wg = lax.all_to_all(wg, "chip", 0, 0, tiled=True)
    outgoing = to_owners(owner, wg)
    incoming = lax.all_to_all(outgoing, "dp", 0, 0, tiled=True)
    pieces = lax.all_to_all(owned_sum(incoming), ("chip", "core"), 0, 0, tiled=True)
    return grad_query[None], grad_kv[None], factors_of(pieces)[None]


def solution(mesh):
    fine = Mesh(mesh.devices.reshape(N_DP, CHIPS, 2), ("dp", "chip", "core"))
    ctx = ("chip", "core")
    return jax.shard_map(
        body,
        mesh=fine,
        in_specs=(
            P("dp", ctx, None),
            P("dp", ctx, None),
            P("dp", ctx, None),
            P("dp", ctx, None),
            P("dp", None),
            P(),
        ),
        out_specs=(P("dp", ctx, None), P("dp", ctx, None), P("dp", None, None, None, None)),
        check_vma=False,
    )
```

```python
import math

import jax
import jax.numpy as jnp
from jax import lax
from jax.experimental import pallas as pl
from jax.experimental.pallas import tpu as pltpu
from jax.sharding import Mesh
from jax.sharding import PartitionSpec as P

HEADS = 8
HD = 128
TILE = 128
ROWS = 128
CHIPS = 8
SEQ = 2048
TILES = 64
CAP = 4
N_DP = 32
MODEL = 8192
N_YL = 2
N_Z = 16
PLANE = N_YL * CHIPS
OWNED = N_YL * CAP * 4
BLOCK = 1024
GROUP = 2
HIDDEN_NEG = -1e30
SCALE = 1.0 / math.sqrt(HD)
EXP2_SCALE = SCALE * math.log2(math.e)
F32 = jnp.float32
BF16 = jnp.bfloat16


def attention_kernel(
    lengths_hbm, q_hbm, go_hbm, mine_ref, other_ref,
    dq_ref, dmine_ref, dother_ref,
    lengths_ref, q_ref, go_ref, q_rows, go_rows, k_all, v_all,
    scores, prob_grads, ds_buf, w_buf, top, total, delta, dq_t, sems,
):
    copies = [
        pltpu.make_async_copy(q_hbm, q_ref, sems.at[0]),
        pltpu.make_async_copy(go_hbm, go_ref, sems.at[1]),
        pltpu.make_async_copy(lengths_hbm, lengths_ref, sems.at[2]),
    ]
    for copy in copies:
        copy.start()
    chip = lax.axis_index("chip")
    core = lax.axis_index("core")
    first = (2 * chip + core) * ROWS
    for ref, side in ((mine_ref, core), (other_ref, 1 - core)):
        for j in range(CHIPS):
            rows = pl.ds(pl.multiple_of((2 * j + side) * ROWS, ROWS), ROWS)
            k_all[rows, :] = ref[j, :, :HD]
            v_all[rows, :] = ref[j, :, HD:]
    top[...] = jnp.full(top.shape, HIDDEN_NEG, F32)
    total[...] = jnp.zeros(total.shape, F32)
    delta[...] = jnp.zeros(delta.shape, F32)
    dq_t[...] = jnp.zeros(dq_t.shape, F32)
    dmine_ref[...] = jnp.zeros(dmine_ref.shape, dmine_ref.dtype)
    dother_ref[...] = jnp.zeros(dother_ref.shape, dother_ref.dtype)
    for copy in copies:
        copy.wait()
    for h in range(HEADS):
        cols = pl.ds(h * HD, HD)
        q_rows[cols, :] = q_ref[:, cols]
        go_rows[cols, :] = go_ref[:, cols]
    row_pos = first + lax.broadcasted_iota(jnp.int32, (1, ROWS), 1)
    row_low = jnp.zeros((1, ROWS), jnp.int32)
    first_low = jnp.int32(0)
    end = jnp.int32(0)
    for d in range(lengths_ref.shape[1]):
        end = end + lengths_ref[0, d]
        row_low = jnp.maximum(row_low, jnp.where(row_pos >= end, end, 0))
        first_low = jnp.maximum(first_low, jnp.where(first >= end, end, 0))
    low_block = first_low // BLOCK
    high_block = (first + ROWS - 1) // BLOCK + 1

    def fold(values, op):
        return op(values.reshape(values.shape[0] // 8, 8, values.shape[1]), axis=0)

    def against(rows, ref, cols):
        return lax.dot_general(
            rows, ref[cols, :], (((1,), (1,)), ((), ())), preferred_element_type=F32
        )

    def score_step(j, carry):
        rows = pl.ds(pl.multiple_of(j * BLOCK, BLOCK), BLOCK)
        pos = j * BLOCK + lax.broadcasted_iota(jnp.int32, (BLOCK, ROWS), 0)
        seen = (pos >= row_low) & (pos <= row_pos)
        seen = jnp.concatenate([seen] * GROUP, axis=1)
        keys = k_all[rows, :]
        for g in range(HEADS // GROUP):
            cols = pl.ds(g * GROUP * HD, GROUP * HD)
            s = jnp.where(seen, against(keys, q_rows, cols), HIDDEN_NEG)
            scores[rows, cols] = s
            top[:, cols] = jnp.maximum(top[:, cols], fold(s, jnp.max))
        return carry

    lax.fori_loop(low_block, high_block, score_step, 0)
    top[0:1, :] = jnp.max(top[...], axis=0, keepdims=True)

    def weight_step(j, carry):
        rows = pl.ds(pl.multiple_of(j * BLOCK, BLOCK), BLOCK)
        values = v_all[rows, :]
        for g in range(HEADS // GROUP):
            cols = pl.ds(g * GROUP * HD, GROUP * HD)
            pg = against(values, go_rows, cols)
            p = jnp.exp2((scores[rows, cols] - top[0:1, cols]) * EXP2_SCALE)
            scores[rows, cols] = p
            prob_grads[rows, cols] = pg
            total[:, cols] += fold(p, jnp.sum)
            delta[:, cols] += fold(p * pg, jnp.sum)
        return carry

    lax.fori_loop(low_block, high_block, weight_step, 0)
    inverse = 1.0 / jnp.sum(total[...], axis=0, keepdims=True)
    total[0:1, :] = inverse
    delta[0:1, :] = jnp.sum(delta[...], axis=0, keepdims=True) * inverse

    def back_step(j, carry):
        rows = pl.ds(pl.multiple_of(j * BLOCK, BLOCK), BLOCK)
        for g in range(HEADS // GROUP):
            cols = pl.ds(g * GROUP * HD, GROUP * HD)
            w = scores[rows, cols] * total[0:1, cols]
            w_buf[:, cols] = w.astype(BF16)
            ds_buf[:, cols] = (w * (prob_grads[rows, cols] - delta[0:1, cols])).astype(BF16)
        ds = ds_buf[...]
        dk = jnp.dot(ds, q_rows[...], preferred_element_type=F32) * SCALE
        dv = jnp.dot(w_buf[...], go_rows[...], preferred_element_type=F32)
        dq_t[...] += lax.dot_general(
            k_all[rows, :], ds, (((0,), (0,)), ((), ())), preferred_element_type=F32
        )
        for i in range(BLOCK // ROWS):
            here = slice(i * ROWS, (i + 1) * ROWS)
            pair = j * (BLOCK // (2 * ROWS)) + i // 2

            @pl.when(core == i % 2)
            def _():
                dmine_ref[pair, :, :HD] = dk[here]
                dmine_ref[pair, :, HD:] = dv[here]

            @pl.when(core != i % 2)
            def _():
                dother_ref[pair, :, :HD] = dk[here].astype(BF16)
                dother_ref[pair, :, HD:] = dv[here].astype(BF16)

        return carry

    lax.fori_loop(low_block, high_block, back_step, 0)
    for h in range(HEADS):
        cols = pl.ds(h * HD, HD)
        dq_ref[:, cols] = (dq_t[:, cols].T * SCALE).astype(BF16)


VMEM = pl.BlockSpec(memory_space=pltpu.VMEM)


def in_hbm(x):
    return pltpu.with_memory_space_constraint(x, pltpu.HBM)


def limit(mib):
    return pltpu.CompilerParams(vmem_limit_bytes=mib * 1024 * 1024)


def attention(lengths, query, grad_out, mine, other):
    hbm = pl.BlockSpec(memory_space=pltpu.HBM)
    wide = HEADS * HD
    return pl.pallas_call(
        attention_kernel,
        out_shape=(
            jax.ShapeDtypeStruct((ROWS, wide), BF16),
            jax.ShapeDtypeStruct((CHIPS, ROWS, 2 * HD), F32),
            jax.ShapeDtypeStruct((CHIPS, ROWS, 2 * HD), BF16),
        ),
        in_specs=[hbm, hbm, hbm, VMEM, VMEM],
        out_specs=(VMEM, VMEM, VMEM),
        scratch_shapes=[
            pltpu.SMEM((1, 8), jnp.int32),
            pltpu.VMEM((ROWS, wide), BF16),
            pltpu.VMEM((ROWS, wide), BF16),
            pltpu.VMEM((wide, HD), BF16),
            pltpu.VMEM((wide, HD), BF16),
            pltpu.VMEM((SEQ, HD), BF16),
            pltpu.VMEM((SEQ, HD), BF16),
            pltpu.VMEM((SEQ, wide), F32),
            pltpu.VMEM((SEQ, wide), F32),
            pltpu.VMEM((BLOCK, wide), BF16),
            pltpu.VMEM((BLOCK, wide), BF16),
            pltpu.VMEM((8, wide), F32),
            pltpu.VMEM((8, wide), F32),
            pltpu.VMEM((8, wide), F32),
            pltpu.VMEM((HD, wide), F32),
            pltpu.SemaphoreType.DMA((3,)),
        ],
        compiler_params=limit(44),
        name="attention_backward",
    )(in_hbm(lengths), in_hbm(query), in_hbm(grad_out), mine, other)


STEP_TILES = 8


def low_half(shape, axis):
    return lax.broadcasted_iota(jnp.int32, shape, axis) < 4


def weight_kernel(parts_ref, hidden_ref, kv_ref, mine_ref, other_ref, k_t):
    core = lax.axis_index("core")
    shape = (PLANE, 8, TILE)

    @pl.when(pl.program_id(0) == 0)
    def _():
        low = jnp.sum(parts_ref[...].astype(F32), axis=0).astype(BF16)
        kv_ref[...] = low
        key_t = low[:, :HD].astype(F32).T.reshape(shape)
        key_t = jnp.where(core == 0, key_t, pltpu.roll(key_t, 4, axis=1))
        k_t[...] = key_t.reshape(HD, ROWS).astype(BF16)

    grad_t = jnp.dot(k_t[...], hidden_ref[...], preferred_element_type=F32)
    low = low_half(shape, 1)

    def pieces(pair):
        even = grad_t[:, (2 * pair) * TILE : (2 * pair + 1) * TILE].reshape(shape)
        odd = grad_t[:, (2 * pair + 1) * TILE : (2 * pair + 2) * TILE].reshape(shape)
        here = jnp.where(low, even, pltpu.roll(odd, 4, axis=1))
        there = jnp.where(low, pltpu.roll(even, 4, axis=1), odd)
        return here, there

    for quad in range(STEP_TILES // 4):
        first, second = pieces(2 * quad), pieces(2 * quad + 1)
        rows = pl.ds(quad * 16, 16)
        mine_ref[:, rows, :] = jnp.concatenate([first[0], second[0]], axis=1)
        other_ref[:, rows, :] = jnp.concatenate([first[1], second[1]], axis=1).astype(BF16)


def weight_terms(parts, hidden):
    steps = TILES // STEP_TILES
    rows = STEP_TILES * 4
    return pl.pallas_call(
        weight_kernel,
        grid=(steps,),
        out_shape=(
            jax.ShapeDtypeStruct((ROWS, 2 * HD), BF16),
            jax.ShapeDtypeStruct((PLANE, TILES * 4, TILE), F32),
            jax.ShapeDtypeStruct((PLANE, TILES * 4, TILE), BF16),
        ),
        in_specs=[
            pl.BlockSpec((CHIPS, ROWS, 2 * HD), lambda i: (0, 0, 0)),
            pl.BlockSpec((ROWS, STEP_TILES * TILE), lambda i: (0, i)),
        ],
        out_specs=(
            pl.BlockSpec((ROWS, 2 * HD), lambda i: (0, 0)),
            pl.BlockSpec((PLANE, rows, TILE), lambda i: (0, i, 0)),
            pl.BlockSpec((PLANE, rows, TILE), lambda i: (0, i, 0)),
        ),
        scratch_shapes=[pltpu.VMEM((HD, ROWS), BF16)],
        compiler_params=limit(16),
        name="weight_gradient",
    )(parts, hidden)


def owner_kernel(owner_ref, parts_ref, out_ref, sums, placed, held):
    rows = TILES * 4
    own = jnp.sum(parts_ref[...].astype(F32), axis=0)
    sums[:rows, :] = own
    sums[rows:, :] = pltpu.roll(own.reshape(rows // 8, 8, TILE), 4, axis=1).reshape(rows, TILE)
    placed[...] = jnp.zeros(placed.shape, F32)
    for o in range(N_DP):
        held[o] = 0
    low = low_half((8, TILE), 0)
    for t in range(TILES):
        o = owner_ref[0, t]
        slot = held[o]
        held[o] = slot + 1
        half = slot & 1
        block = ((o & (N_Z - 1)) * N_YL + o // N_Z) * (CAP // 2) + slot // 2
        at = pl.ds(pl.multiple_of(block * 8, 8), 8)
        source = pl.multiple_of((half ^ (t & 1)) * rows + (t // 2) * 8, 8)
        placed[at, :] = jnp.where(low == (half == 0), sums[pl.ds(source, 8), :], placed[at, :])
    out_ref[...] = placed[...].astype(BF16).reshape(out_ref.shape)


def to_owners(owner, parts):
    return pl.pallas_call(
        owner_kernel,
        out_shape=jax.ShapeDtypeStruct((N_Z, OWNED, TILE), BF16),
        in_specs=[pl.BlockSpec(memory_space=pltpu.SMEM), VMEM],
        out_specs=VMEM,
        scratch_shapes=[
            pltpu.VMEM((2 * TILES * 4, TILE), F32),
            pltpu.VMEM((N_Z * OWNED, TILE), F32),
            pltpu.SMEM((N_DP,), jnp.int32),
        ],
        compiler_params=limit(12),
        name="owner_slots",
    )(owner, parts)


def sum_kernel(parts_ref, out_ref):
    gradient = jnp.sum(parts_ref[...].astype(F32), axis=0) * (1.0 / math.sqrt(N_DP * SEQ))
    gradient = gradient.astype(BF16)
    rows = OWNED // N_YL
    for yl in range(N_YL):
        piece = gradient[yl * rows : (yl + 1) * rows]
        out_ref[yl * PLANE : (yl + 1) * PLANE] = jnp.broadcast_to(piece[None], (PLANE, rows, TILE))


def owned_sum(parts):
    return pl.pallas_call(
        sum_kernel,
        out_shape=jax.ShapeDtypeStruct((2 * PLANE, OWNED // N_YL, TILE), BF16),
        in_specs=[VMEM],
        out_specs=VMEM,
        compiler_params=limit(8),
        name="owned_sum",
    )(parts)


def factor_kernel(pieces_ref, out_ref):
    pieces = pieces_ref[...].astype(F32)
    low = low_half((PLANE, 8, TILE), 1)
    for two in range(CAP // 2):
        pair = pieces[:, two * 8 : (two + 1) * 8, :].reshape(PLANE, 2, 8, TILE)
        even, odd = pair[:, 0], pair[:, 1]
        both = (
            jnp.where(low, even, pltpu.roll(odd, 4, axis=1)),
            jnp.where(low, pltpu.roll(even, 4, axis=1), odd),
        )
        for i in range(2):
            grad_t = both[i].reshape(TILE, TILE)
            flat = grad_t.astype(BF16)
            flat_t = grad_t.T.astype(BF16)
            s = 2 * two + i
            out_ref[s, 0] = jnp.dot(flat_t, flat, preferred_element_type=F32) * (1.0 / TILE)
            out_ref[s, 1] = jnp.dot(flat, flat_t, preferred_element_type=F32) * (1.0 / TILE)


def factors_of(pieces):
    return pl.pallas_call(
        factor_kernel,
        out_shape=jax.ShapeDtypeStruct((CAP, 2, TILE, TILE), F32),
        in_specs=[VMEM],
        out_specs=VMEM,
        compiler_params=limit(8),
        name="factors",
    )(pieces)


SWAP = ((0, 1), (1, 0))


def body(hidden_in, query, key_value, grad_out, lengths, owner):
    mine = lax.all_to_all(
        jnp.broadcast_to(key_value, (CHIPS, ROWS, 2 * HD)), "chip", 0, 0, tiled=True
    )
    other = lax.ppermute(mine, "core", SWAP)
    grad_query, dkv_mine, dkv_other = attention(lengths, query[0], grad_out[0], mine, other)
    dkv = (dkv_mine + lax.ppermute(dkv_other, "core", SWAP).astype(F32)).astype(BF16)
    dkv = lax.all_to_all(dkv, "chip", 0, 0, tiled=True)
    grad_kv, wg_mine, wg_other = weight_terms(dkv, hidden_in[0])
    wg = (wg_mine + lax.ppermute(wg_other, "core", SWAP).astype(F32)).astype(BF16)
    wg = lax.all_to_all(wg, ("yl", "chip"), 0, 0, tiled=True)
    outgoing = to_owners(owner.reshape(1, TILES), wg)
    incoming = lax.all_to_all(outgoing, "z", 0, 0, tiled=True)
    pieces = lax.all_to_all(owned_sum(incoming), ("yl", "chip", "core"), 0, 0, tiled=True)
    return grad_query[None], grad_kv[None], factors_of(pieces)[None]


def solution(mesh):
    fine = Mesh(mesh.devices.reshape(N_YL, N_Z, CHIPS, 2), ("yl", "z", "chip", "core"))
    dp, ctx = ("yl", "z"), ("chip", "core")
    split = P(dp, ctx, None)
    return jax.shard_map(
        body,
        mesh=fine,
        in_specs=(split, split, split, split, P(dp, None), P()),
        out_specs=(split, split, P(dp, None, None, None, None)),
        check_vma=False,
    )
```

```python
import math

import jax
import jax.numpy as jnp
from jax import lax
from jax.experimental import pallas as pl
from jax.experimental.pallas import tpu as pltpu
from jax.sharding import Mesh
from jax.sharding import PartitionSpec as P

HEADS = 8
HD = 128
TILE = 128
ROWS = 128
CHIPS = 8
SEQ = 2048
TILES = 64
CAP = 4
N_DP = 32
MODEL = 8192
N_YL = 2
N_Z = 16
PLANE = N_YL * CHIPS
OWNED = N_YL * CAP * 4
BLOCK = 1024
GROUP = 2
HIDDEN_NEG = -1e30
SCALE = 1.0 / math.sqrt(HD)
EXP2_SCALE = SCALE * math.log2(math.e)
F32 = jnp.float32
BF16 = jnp.bfloat16


def attention_kernel(
    lengths_hbm, q_hbm, go_hbm, mine_ref, other_ref,
    dq_ref, keep_ref, send_ref,
    lengths_ref, q_ref, go_ref, q_rows, go_rows, k_all, v_all,
    scores, prob_grads, ds_buf, w_buf, top, total, delta, dq_t, sems,
):
    copies = [
        pltpu.make_async_copy(q_hbm, q_ref, sems.at[0]),
        pltpu.make_async_copy(go_hbm, go_ref, sems.at[1]),
        pltpu.make_async_copy(lengths_hbm, lengths_ref, sems.at[2]),
    ]
    for copy in copies:
        copy.start()
    chip = lax.axis_index("chip")
    core = lax.axis_index("core")
    first = (2 * chip + core) * ROWS
    for ref, side in ((mine_ref, core), (other_ref, 1 - core)):
        for j in range(CHIPS):
            rows = pl.ds(pl.multiple_of((2 * j + side) * ROWS, ROWS), ROWS)
            k_all[rows, :] = ref[j, :, :HD]
            v_all[rows, :] = ref[j, :, HD:]
    top[...] = jnp.full(top.shape, HIDDEN_NEG, F32)
    total[...] = jnp.zeros(total.shape, F32)
    delta[...] = jnp.zeros(delta.shape, F32)
    dq_t[...] = jnp.zeros(dq_t.shape, F32)
    keep_ref[...] = jnp.zeros(keep_ref.shape, keep_ref.dtype)
    send_ref[...] = jnp.zeros(send_ref.shape, send_ref.dtype)
    for copy in copies:
        copy.wait()
    for h in range(HEADS):
        cols = pl.ds(h * HD, HD)
        q_rows[cols, :] = q_ref[:, cols]
        go_rows[cols, :] = go_ref[:, cols]
    row_pos = first + lax.broadcasted_iota(jnp.int32, (1, ROWS), 1)
    row_low = jnp.zeros((1, ROWS), jnp.int32)
    first_low = jnp.int32(0)
    end = jnp.int32(0)
    for d in range(lengths_ref.shape[1]):
        end = end + lengths_ref[0, d]
        row_low = jnp.maximum(row_low, jnp.where(row_pos >= end, end, 0))
        first_low = jnp.maximum(first_low, jnp.where(first >= end, end, 0))
    low_block = first_low // BLOCK
    high_block = (first + ROWS - 1) // BLOCK + 1

    def fold(values, op):
        return op(values.reshape(values.shape[0] // 8, 8, values.shape[1]), axis=0)

    def against(rows, ref, cols):
        return lax.dot_general(
            rows, ref[cols, :], (((1,), (1,)), ((), ())), preferred_element_type=F32
        )

    def score_step(j, carry):
        rows = pl.ds(pl.multiple_of(j * BLOCK, BLOCK), BLOCK)
        pos = j * BLOCK + lax.broadcasted_iota(jnp.int32, (BLOCK, ROWS), 0)
        seen = (pos >= row_low) & (pos <= row_pos)
        seen = jnp.concatenate([seen] * GROUP, axis=1)
        keys = k_all[rows, :]
        for g in range(HEADS // GROUP):
            cols = pl.ds(g * GROUP * HD, GROUP * HD)
            s = jnp.where(seen, against(keys, q_rows, cols), HIDDEN_NEG)
            scores[rows, cols] = s
            top[:, cols] = jnp.maximum(top[:, cols], fold(s, jnp.max))
        return carry

    lax.fori_loop(low_block, high_block, score_step, 0)
    top[0:1, :] = jnp.max(top[...], axis=0, keepdims=True)

    def weight_step(j, carry):
        rows = pl.ds(pl.multiple_of(j * BLOCK, BLOCK), BLOCK)
        values = v_all[rows, :]
        for g in range(HEADS // GROUP):
            cols = pl.ds(g * GROUP * HD, GROUP * HD)
            pg = against(values, go_rows, cols)
            p = jnp.exp2((scores[rows, cols] - top[0:1, cols]) * EXP2_SCALE)
            scores[rows, cols] = p
            prob_grads[rows, cols] = pg
            total[:, cols] += fold(p, jnp.sum)
            delta[:, cols] += fold(p * pg, jnp.sum)
        return carry

    lax.fori_loop(low_block, high_block, weight_step, 0)
    inverse = 1.0 / jnp.sum(total[...], axis=0, keepdims=True)
    total[0:1, :] = inverse
    delta[0:1, :] = jnp.sum(delta[...], axis=0, keepdims=True) * inverse

    def back_step(j, carry):
        rows = pl.ds(pl.multiple_of(j * BLOCK, BLOCK), BLOCK)
        for g in range(HEADS // GROUP):
            cols = pl.ds(g * GROUP * HD, GROUP * HD)
            w = scores[rows, cols] * total[0:1, cols]
            w_buf[:, cols] = w.astype(BF16)
            ds_buf[:, cols] = (w * (prob_grads[rows, cols] - delta[0:1, cols])).astype(BF16)
        ds = ds_buf[...]
        dk = jnp.dot(ds, q_rows[...], preferred_element_type=F32) * SCALE
        dv = jnp.dot(w_buf[...], go_rows[...], preferred_element_type=F32)
        dq_t[...] += lax.dot_general(
            k_all[rows, :], ds, (((0,), (0,)), ((), ())), preferred_element_type=F32
        )
        for i in range(BLOCK // ROWS):
            here = slice(i * ROWS, (i + 1) * ROWS)
            pair = j * (BLOCK // (2 * ROWS)) + i // 2
            at = pl.ds((i % 2) * ROWS, ROWS)
            keep_ref[pair, at, :] = dk[here]
            send_ref[pair, at, :] = dk[here].astype(BF16)

            @pl.when(core == i % 2)
            def _():
                keep_ref[pair, 2 * ROWS :, :] = dv[here]

            @pl.when(core != i % 2)
            def _():
                send_ref[pair, 2 * ROWS :, :] = dv[here].astype(BF16)

        return carry

    lax.fori_loop(low_block, high_block, back_step, 0)
    for h in range(HEADS):
        cols = pl.ds(h * HD, HD)
        dq_ref[:, cols] = (dq_t[:, cols].T * SCALE).astype(BF16)


VMEM = pl.BlockSpec(memory_space=pltpu.VMEM)


def in_hbm(x):
    return pltpu.with_memory_space_constraint(x, pltpu.HBM)


def limit(mib):
    return pltpu.CompilerParams(vmem_limit_bytes=mib * 1024 * 1024)


def attention(lengths, query, grad_out, mine, other):
    hbm = pl.BlockSpec(memory_space=pltpu.HBM)
    wide = HEADS * HD
    return pl.pallas_call(
        attention_kernel,
        out_shape=(
            jax.ShapeDtypeStruct((ROWS, wide), BF16),
            jax.ShapeDtypeStruct((CHIPS, 3 * ROWS, HD), F32),
            jax.ShapeDtypeStruct((CHIPS, 3 * ROWS, HD), BF16),
        ),
        in_specs=[hbm, hbm, hbm, VMEM, VMEM],
        out_specs=(VMEM, VMEM, VMEM),
        scratch_shapes=[
            pltpu.SMEM((1, 8), jnp.int32),
            pltpu.VMEM((ROWS, wide), BF16),
            pltpu.VMEM((ROWS, wide), BF16),
            pltpu.VMEM((wide, HD), BF16),
            pltpu.VMEM((wide, HD), BF16),
            pltpu.VMEM((SEQ, HD), BF16),
            pltpu.VMEM((SEQ, HD), BF16),
            pltpu.VMEM((SEQ, wide), F32),
            pltpu.VMEM((SEQ, wide), F32),
            pltpu.VMEM((BLOCK, wide), BF16),
            pltpu.VMEM((BLOCK, wide), BF16),
            pltpu.VMEM((8, wide), F32),
            pltpu.VMEM((8, wide), F32),
            pltpu.VMEM((8, wide), F32),
            pltpu.VMEM((HD, wide), F32),
            pltpu.SemaphoreType.DMA((3,)),
        ],
        compiler_params=limit(44),
        name="attention_backward",
    )(in_hbm(lengths), in_hbm(query), in_hbm(grad_out), mine, other)


def low_half(shape, axis):
    return lax.broadcasted_iota(jnp.int32, shape, axis) < 4


def weight_kernel(parts_ref, own_ref, other_ref, kv_ref, out_ref, k_t):
    core = lax.axis_index("core")
    sums = jnp.sum(parts_ref[...].astype(F32), axis=0).astype(BF16)
    keys = sums[: 2 * ROWS].astype(F32)
    first, second = keys[:ROWS], keys[ROWS:]
    own_keys = jnp.where(core == 0, first, second)
    other_keys = jnp.where(core == 0, second, first)
    kv_ref[:, :HD] = own_keys.astype(BF16)
    kv_ref[:, HD:] = sums[2 * ROWS :]
    for i, side in enumerate((own_keys, other_keys)):
        rows = side.T.reshape(PLANE // 2, 2, 8, ROWS)
        even, odd = rows[:, 0], rows[:, 1]
        low = low_half(even.shape, 1)
        here = jnp.where(low, even, pltpu.roll(odd, 4, axis=1))
        there = jnp.where(low, pltpu.roll(even, 4, axis=1), odd)
        mine = jnp.where(core == 0, here, there).reshape(HD // 2, ROWS)
        k_t[:, i * ROWS : (i + 1) * ROWS] = mine.astype(BF16)
    shape = (PLANE // 2, 8, TILE)
    low = low_half(shape, 1)
    for quad in range(TILES // 4):
        cols = pl.ds(quad * 4 * TILE, 4 * TILE)
        hidden = jnp.concatenate([own_ref[:, cols], other_ref[:, cols]], axis=0)
        grad_t = jnp.dot(k_t[...], hidden, preferred_element_type=F32)
        tiles = [grad_t[:, i * TILE : (i + 1) * TILE].reshape(shape) for i in range(4)]
        evens, odds = [], []
        for even, odd in (tiles[:2], tiles[2:]):
            evens.append(jnp.where(low, even, pltpu.roll(odd, 4, axis=1)))
            odds.append(jnp.where(low, pltpu.roll(even, 4, axis=1), odd))
        rows = pl.ds(quad * 16, 16)
        out_ref[:, 0, rows, :] = jnp.concatenate(evens, axis=1).astype(BF16)
        out_ref[:, 1, rows, :] = jnp.concatenate(odds, axis=1).astype(BF16)


def weight_terms(parts, own, other):
    grad_kv, terms = pl.pallas_call(
        weight_kernel,
        out_shape=(
            jax.ShapeDtypeStruct((ROWS, 2 * HD), BF16),
            jax.ShapeDtypeStruct((PLANE // 2, 2, TILES * 4, TILE), BF16),
        ),
        in_specs=[VMEM, VMEM, VMEM],
        out_specs=(VMEM, VMEM),
        scratch_shapes=[pltpu.VMEM((HD // 2, 2 * ROWS), BF16)],
        compiler_params=limit(16),
        name="weight_gradient",
    )(parts, own, other)
    return grad_kv, terms.reshape(PLANE, TILES * 4, TILE)


def owner_kernel(owner_ref, parts_ref, out_ref, sums, placed, held):
    rows = TILES * 4
    own = jnp.sum(parts_ref[...].astype(F32), axis=0)
    sums[:rows, :] = own
    sums[rows:, :] = pltpu.roll(own.reshape(rows // 8, 8, TILE), 4, axis=1).reshape(rows, TILE)
    placed[...] = jnp.zeros(placed.shape, F32)
    for o in range(N_DP):
        held[o] = 0
    low = low_half((8, TILE), 0)
    for t in range(TILES):
        o = owner_ref[0, t]
        slot = held[o]
        held[o] = slot + 1
        half = slot & 1
        block = ((o & (N_Z - 1)) * N_YL + o // N_Z) * (CAP // 2) + slot // 2
        at = pl.ds(pl.multiple_of(block * 8, 8), 8)
        source = pl.multiple_of((half ^ (t & 1)) * rows + (t // 2) * 8, 8)
        placed[at, :] = jnp.where(low == (half == 0), sums[pl.ds(source, 8), :], placed[at, :])
    out_ref[...] = placed[...].astype(BF16).reshape(out_ref.shape)


def to_owners(owner, parts):
    return pl.pallas_call(
        owner_kernel,
        out_shape=jax.ShapeDtypeStruct((N_Z, OWNED, TILE), BF16),
        in_specs=[pl.BlockSpec(memory_space=pltpu.SMEM), VMEM],
        out_specs=VMEM,
        scratch_shapes=[
            pltpu.VMEM((2 * TILES * 4, TILE), F32),
            pltpu.VMEM((N_Z * OWNED, TILE), F32),
            pltpu.SMEM((N_DP,), jnp.int32),
        ],
        compiler_params=limit(12),
        name="owner_slots",
    )(owner, parts)


def sum_kernel(parts_ref, out_ref):
    gradient = jnp.sum(parts_ref[...].astype(F32), axis=0) * (1.0 / math.sqrt(N_DP * SEQ))
    gradient = gradient.astype(BF16)
    rows = OWNED // N_YL
    for yl in range(N_YL):
        piece = gradient[yl * rows : (yl + 1) * rows]
        out_ref[yl * PLANE : (yl + 1) * PLANE] = jnp.broadcast_to(piece[None], (PLANE, rows, TILE))


def owned_sum(parts):
    return pl.pallas_call(
        sum_kernel,
        out_shape=jax.ShapeDtypeStruct((2 * PLANE, OWNED // N_YL, TILE), BF16),
        in_specs=[VMEM],
        out_specs=VMEM,
        compiler_params=limit(8),
        name="owned_sum",
    )(parts)


def factor_kernel(pieces_ref, out_ref):
    pieces = pieces_ref[...].astype(F32)
    low = low_half((PLANE, 8, TILE), 1)
    for two in range(CAP // 2):
        pair = pieces[:, two * 8 : (two + 1) * 8, :].reshape(PLANE, 2, 8, TILE)
        even, odd = pair[:, 0], pair[:, 1]
        both = (
            jnp.where(low, even, pltpu.roll(odd, 4, axis=1)),
            jnp.where(low, pltpu.roll(even, 4, axis=1), odd),
        )
        for i in range(2):
            grad_t = both[i].reshape(TILE, TILE)
            flat = grad_t.astype(BF16)
            flat_t = grad_t.T.astype(BF16)
            s = 2 * two + i
            out_ref[s, 0] = jnp.dot(flat_t, flat, preferred_element_type=F32) * (1.0 / TILE)
            out_ref[s, 1] = jnp.dot(flat, flat_t, preferred_element_type=F32) * (1.0 / TILE)


def factors_of(pieces):
    return pl.pallas_call(
        factor_kernel,
        out_shape=jax.ShapeDtypeStruct((CAP, 2, TILE, TILE), F32),
        in_specs=[VMEM],
        out_specs=VMEM,
        compiler_params=limit(8),
        name="factors",
    )(pieces)


SWAP = ((0, 1), (1, 0))


def body(hidden_in, query, key_value, grad_out, lengths, owner):
    hidden = hidden_in[0]
    hidden_other = lax.ppermute(hidden, "core", SWAP)
    mine = lax.all_to_all(
        jnp.broadcast_to(key_value, (CHIPS, ROWS, 2 * HD)), "chip", 0, 0, tiled=True
    )
    other = lax.ppermute(mine, "core", SWAP)
    grad_query, keep, send = attention(lengths, query[0], grad_out[0], mine, other)
    dkv = (keep + lax.ppermute(send, "core", SWAP).astype(F32)).astype(BF16)
    dkv = lax.all_to_all(dkv, "chip", 0, 0, tiled=True)
    grad_kv, wg = weight_terms(dkv, hidden, hidden_other)
    wg = lax.all_to_all(wg, ("yl", "chip"), 0, 0, tiled=True)
    outgoing = to_owners(owner.reshape(1, TILES), wg)
    incoming = lax.all_to_all(outgoing, "z", 0, 0, tiled=True)
    pieces = lax.all_to_all(owned_sum(incoming), ("yl", "chip", "core"), 0, 0, tiled=True)
    return grad_query[None], grad_kv[None], factors_of(pieces)[None]


def solution(mesh):
    fine = Mesh(mesh.devices.reshape(N_YL, N_Z, CHIPS, 2), ("yl", "z", "chip", "core"))
    dp, ctx = ("yl", "z"), ("chip", "core")
    split = P(dp, ctx, None)
    return jax.shard_map(
        body,
        mesh=fine,
        in_specs=(split, split, split, split, P(dp, None), P()),
        out_specs=(split, split, P(dp, None, None, None, None)),
        check_vma=False,
    )
```

```python
import math

import jax
import jax.numpy as jnp
from jax import lax
from jax.experimental import pallas as pl
from jax.experimental.pallas import tpu as pltpu
from jax.sharding import Mesh
from jax.sharding import PartitionSpec as P

HEADS = 8
HD = 128
TILE = 128
ROWS = 128
CHIPS = 8
SEQ = 2048
TILES = 64
CAP = 4
N_DP = 32
MODEL = 8192
N_YL = 2
N_Z = 16
PLANE = N_YL * CHIPS
OWNED = N_YL * CAP * 4
GROUP = 2
HIDDEN_NEG = -1e30
SCALE = 1.0 / math.sqrt(HD)
EXP2_SCALE = SCALE * math.log2(math.e)
F32 = jnp.float32
BF16 = jnp.bfloat16


def prepare_kernel(
    lengths_hbm, q_hbm, go_hbm, q_rows, go_rows, low_ref, lengths_ref, q_ref, go_ref, sems
):
    copies = [
        pltpu.make_async_copy(lengths_hbm, lengths_ref, sems.at[0]),
        pltpu.make_async_copy(q_hbm, q_ref, sems.at[1]),
        pltpu.make_async_copy(go_hbm, go_ref, sems.at[2]),
    ]
    for copy in copies:
        copy.start()
    first = (2 * lax.axis_index("chip") + lax.axis_index("core")) * ROWS
    row_pos = first + lax.broadcasted_iota(jnp.int32, low_ref.shape, 1)
    row_low = jnp.zeros(low_ref.shape, jnp.int32)
    end = jnp.int32(0)
    copies[0].wait()
    for d in range(lengths_ref.shape[1]):
        end = end + lengths_ref[0, d]
        row_low = jnp.maximum(row_low, jnp.where(row_pos >= end, end, 0))
    low_ref[...] = row_low
    for copy, rows, ref in ((copies[1], q_rows, q_ref), (copies[2], go_rows, go_ref)):
        copy.wait()
        for h in range(HEADS):
            cols = pl.ds(h * HD, HD)
            rows[cols, :] = ref[:, cols]


def attention_kernel(
    q_rows, go_rows, low_ref, mine_ref, other_ref,
    dq_t, keep_ref, send_ref,
    k_all, v_all, scores, prob_grads, ds_buf, w_buf, top, total, delta,
):
    chip = lax.axis_index("chip")
    core = lax.axis_index("core")
    first = (2 * chip + core) * ROWS
    for ref, side in ((mine_ref, core), (other_ref, 1 - core)):
        for j in range(CHIPS):
            rows = pl.ds(pl.multiple_of((2 * j + side) * ROWS, ROWS), ROWS)
            k_all[rows, :] = ref[j, :, :HD]
            v_all[rows, :] = ref[j, :, HD:]
    row_pos = first + lax.broadcasted_iota(jnp.int32, (1, ROWS), 1)
    row_low = low_ref[0:1, :]

    def fold(values, op):
        return op(values.reshape(values.shape[0] // 8, 8, values.shape[1]), axis=0)

    def against(rows, ref, cols):
        return lax.dot_general(
            rows, ref[cols, :], (((1,), (1,)), ((), ())), preferred_element_type=F32
        )

    pos = lax.broadcasted_iota(jnp.int32, (SEQ, ROWS), 0)
    seen = (pos >= row_low) & (pos <= row_pos)
    seen = jnp.concatenate([seen] * GROUP, axis=1)
    keys = k_all[...]
    groups = [pl.ds(g * GROUP * HD, GROUP * HD) for g in range(HEADS // GROUP)]
    for cols in groups:
        s = jnp.where(seen, against(keys, q_rows, cols), HIDDEN_NEG)
        scores[:, cols] = s
        top[:, cols] = fold(s, jnp.max)
    top[0:1, :] = jnp.max(top[...], axis=0, keepdims=True)
    values = v_all[...]
    for cols in groups:
        pg = against(values, go_rows, cols)
        p = jnp.exp2((scores[:, cols] - top[0:1, cols]) * EXP2_SCALE)
        scores[:, cols] = p
        prob_grads[:, cols] = pg
        total[:, cols] = fold(p, jnp.sum)
        delta[:, cols] = fold(p * pg, jnp.sum)
    inverse = 1.0 / jnp.sum(total[...], axis=0, keepdims=True)
    total[0:1, :] = inverse
    delta[0:1, :] = jnp.sum(delta[...], axis=0, keepdims=True) * inverse
    for cols in groups:
        w = scores[:, cols] * total[0:1, cols]
        w_buf[:, cols] = w.astype(BF16)
        ds_buf[:, cols] = (w * (prob_grads[:, cols] - delta[0:1, cols])).astype(BF16)
    ds = ds_buf[...]
    dk = jnp.dot(ds, q_rows[...], preferred_element_type=F32) * SCALE
    dv = jnp.dot(w_buf[...], go_rows[...], preferred_element_type=F32)
    dq_t[...] = lax.dot_general(
        keys, ds, (((0,), (0,)), ((), ())), preferred_element_type=F32
    )
    for pair in range(CHIPS):
        for cols, grads in ((slice(0, HD), dk), (slice(HD, 2 * HD), dv)):
            even = grads[2 * pair * ROWS : (2 * pair + 1) * ROWS]
            odd = grads[(2 * pair + 1) * ROWS : (2 * pair + 2) * ROWS]
            keep_ref[pair, :, cols] = jnp.where(core == 0, even, odd)
            send_ref[pair, :, cols] = jnp.where(core == 0, odd, even).astype(BF16)


def query_kernel(dq_t, dq_ref):
    for h in range(HEADS):
        cols = pl.ds(h * HD, HD)
        dq_ref[:, cols] = (dq_t[:, cols].T * SCALE).astype(BF16)


VMEM = pl.BlockSpec(memory_space=pltpu.VMEM)


def in_hbm(x):
    return pltpu.with_memory_space_constraint(x, pltpu.HBM)


def limit(mib):
    return pltpu.CompilerParams(vmem_limit_bytes=mib * 1024 * 1024)


def prepare(lengths, query, grad_out):
    hbm = pl.BlockSpec(memory_space=pltpu.HBM)
    wide = HEADS * HD
    return pl.pallas_call(
        prepare_kernel,
        out_shape=(
            jax.ShapeDtypeStruct((wide, HD), BF16),
            jax.ShapeDtypeStruct((wide, HD), BF16),
            jax.ShapeDtypeStruct((8, ROWS), jnp.int32),
        ),
        in_specs=[hbm, hbm, hbm],
        out_specs=(VMEM, VMEM, VMEM),
        scratch_shapes=[
            pltpu.SMEM((1, 8), jnp.int32),
            pltpu.VMEM((ROWS, wide), BF16),
            pltpu.VMEM((ROWS, wide), BF16),
            pltpu.SemaphoreType.DMA((3,)),
        ],
        compiler_params=limit(8),
        name="prepare_rows",
    )(in_hbm(lengths), in_hbm(query), in_hbm(grad_out))


def attention(q_rows, go_rows, row_low, mine, other):
    wide = HEADS * HD
    return pl.pallas_call(
        attention_kernel,
        out_shape=(
            jax.ShapeDtypeStruct((HD, wide), F32),
            jax.ShapeDtypeStruct((CHIPS, ROWS, 2 * HD), F32),
            jax.ShapeDtypeStruct((CHIPS, ROWS, 2 * HD), BF16),
        ),
        in_specs=[VMEM] * 5,
        out_specs=(VMEM, VMEM, VMEM),
        scratch_shapes=[
            pltpu.VMEM((SEQ, HD), BF16),
            pltpu.VMEM((SEQ, HD), BF16),
            pltpu.VMEM((SEQ, wide), F32),
            pltpu.VMEM((SEQ, wide), F32),
            pltpu.VMEM((SEQ, wide), BF16),
            pltpu.VMEM((SEQ, wide), BF16),
            pltpu.VMEM((8, wide), F32),
            pltpu.VMEM((8, wide), F32),
            pltpu.VMEM((8, wide), F32),
        ],
        compiler_params=limit(36),
        name="attention_backward",
    )(q_rows, go_rows, row_low, mine, other)


def query_gradient(dq_t):
    return pl.pallas_call(
        query_kernel,
        out_shape=jax.ShapeDtypeStruct((ROWS, HEADS * HD), BF16),
        in_specs=[VMEM],
        out_specs=VMEM,
        compiler_params=limit(8),
        name="query_gradient",
    )(dq_t)


def low_half(shape, axis):
    return lax.broadcasted_iota(jnp.int32, shape, axis) < 4


def halves(keys):
    rows = keys.T.reshape(PLANE // 2, 2, 8, ROWS)
    even, odd = rows[:, 0], rows[:, 1]
    low = low_half(even.shape, 1)
    first = jnp.where(low, even, pltpu.roll(odd, 4, axis=1))
    second = jnp.where(low, pltpu.roll(even, 4, axis=1), odd)
    return first.reshape(HD // 2, ROWS), second.reshape(HD // 2, ROWS)


def half_tiles(k_t, hidden_ref, out_ref):
    shape = (PLANE // 2, 8, TILE)
    low = low_half(shape, 1)
    for quad in range(TILES // 4):
        hidden = hidden_ref[:, pl.ds(quad * 4 * TILE, 4 * TILE)]
        grad_t = jnp.dot(k_t, hidden, preferred_element_type=F32)
        tiles = [grad_t[:, i * TILE : (i + 1) * TILE].reshape(shape) for i in range(4)]
        evens, odds = [], []
        for even, odd in (tiles[:2], tiles[2:]):
            evens.append(jnp.where(low, even, pltpu.roll(odd, 4, axis=1)))
            odds.append(jnp.where(low, pltpu.roll(even, 4, axis=1), odd))
        rows = pl.ds(quad * 16, 16)
        out_ref[:, 0, rows, :] = jnp.concatenate(evens, axis=1).astype(out_ref.dtype)
        out_ref[:, 1, rows, :] = jnp.concatenate(odds, axis=1).astype(out_ref.dtype)


def weight_send_kernel(parts_ref, hidden_ref, kv_ref, k_ref, out_ref):
    core = lax.axis_index("core")
    low = jnp.sum(parts_ref[...].astype(F32), axis=0).astype(BF16)
    kv_ref[...] = low
    first, second = halves(low[:, :HD].astype(F32))
    k_ref[...] = jnp.where(core == 0, first, second).astype(BF16)
    half_tiles(jnp.where(core == 0, second, first).astype(BF16), hidden_ref, out_ref)


def weight_keep_kernel(k_ref, hidden_ref, out_ref):
    half_tiles(k_ref[...], hidden_ref, out_ref)


def weight_send(parts, hidden):
    return pl.pallas_call(
        weight_send_kernel,
        out_shape=(
            jax.ShapeDtypeStruct((ROWS, 2 * HD), BF16),
            jax.ShapeDtypeStruct((HD // 2, ROWS), BF16),
            jax.ShapeDtypeStruct((PLANE // 2, 2, TILES * 4, TILE), BF16),
        ),
        in_specs=[VMEM, VMEM],
        out_specs=(VMEM, VMEM, VMEM),
        compiler_params=limit(10),
        name="weight_tiles_to_send",
    )(parts, hidden)


def weight_keep(k_t, hidden):
    return pl.pallas_call(
        weight_keep_kernel,
        out_shape=jax.ShapeDtypeStruct((PLANE // 2, 2, TILES * 4, TILE), F32),
        in_specs=[VMEM, VMEM],
        out_specs=VMEM,
        compiler_params=limit(10),
        name="weight_tiles_to_keep",
    )(k_t, hidden)


def owner_kernel(owner_ref, parts_ref, out_ref, sums, placed, held):
    rows = TILES * 4
    own = jnp.sum(parts_ref[...].astype(F32), axis=0)
    sums[:rows, :] = own
    sums[rows:, :] = pltpu.roll(own.reshape(rows // 8, 8, TILE), 4, axis=1).reshape(rows, TILE)
    placed[...] = jnp.zeros(placed.shape, F32)
    for o in range(N_DP):
        held[o] = 0
    low = low_half((8, TILE), 0)
    for t in range(TILES):
        o = owner_ref[0, t]
        slot = held[o]
        held[o] = slot + 1
        half = slot & 1
        block = ((o & (N_Z - 1)) * N_YL + o // N_Z) * (CAP // 2) + slot // 2
        at = pl.ds(pl.multiple_of(block * 8, 8), 8)
        source = pl.multiple_of((half ^ (t & 1)) * rows + (t // 2) * 8, 8)
        placed[at, :] = jnp.where(low == (half == 0), sums[pl.ds(source, 8), :], placed[at, :])
    out_ref[...] = placed[...].astype(BF16).reshape(out_ref.shape)


def to_owners(owner, parts):
    return pl.pallas_call(
        owner_kernel,
        out_shape=jax.ShapeDtypeStruct((N_Z, OWNED, TILE), BF16),
        in_specs=[pl.BlockSpec(memory_space=pltpu.SMEM), VMEM],
        out_specs=VMEM,
        scratch_shapes=[
            pltpu.VMEM((2 * TILES * 4, TILE), F32),
            pltpu.VMEM((N_Z * OWNED, TILE), F32),
            pltpu.SMEM((N_DP,), jnp.int32),
        ],
        compiler_params=limit(12),
        name="owner_slots",
    )(owner, parts)


def sum_kernel(parts_ref, out_ref):
    gradient = jnp.sum(parts_ref[...].astype(F32), axis=0) * (1.0 / math.sqrt(N_DP * SEQ))
    gradient = gradient.astype(BF16)
    rows = OWNED // N_YL
    for yl in range(N_YL):
        piece = gradient[yl * rows : (yl + 1) * rows]
        out_ref[yl * PLANE : (yl + 1) * PLANE] = jnp.broadcast_to(piece[None], (PLANE, rows, TILE))


def owned_sum(parts):
    return pl.pallas_call(
        sum_kernel,
        out_shape=jax.ShapeDtypeStruct((2 * PLANE, OWNED // N_YL, TILE), BF16),
        in_specs=[VMEM],
        out_specs=VMEM,
        compiler_params=limit(8),
        name="owned_sum",
    )(parts)


def factor_kernel(pieces_ref, out_ref):
    pieces = pieces_ref[...].astype(F32)
    low = low_half((PLANE, 8, TILE), 1)
    for two in range(CAP // 2):
        pair = pieces[:, two * 8 : (two + 1) * 8, :].reshape(PLANE, 2, 8, TILE)
        even, odd = pair[:, 0], pair[:, 1]
        both = (
            jnp.where(low, even, pltpu.roll(odd, 4, axis=1)),
            jnp.where(low, pltpu.roll(even, 4, axis=1), odd),
        )
        for i in range(2):
            grad_t = both[i].reshape(TILE, TILE)
            flat = grad_t.astype(BF16)
            flat_t = grad_t.T.astype(BF16)
            s = 2 * two + i
            out_ref[s, 0] = jnp.dot(flat_t, flat, preferred_element_type=F32) * (1.0 / TILE)
            out_ref[s, 1] = jnp.dot(flat, flat_t, preferred_element_type=F32) * (1.0 / TILE)


def factors_of(pieces):
    return pl.pallas_call(
        factor_kernel,
        out_shape=jax.ShapeDtypeStruct((CAP, 2, TILE, TILE), F32),
        in_specs=[VMEM],
        out_specs=VMEM,
        compiler_params=limit(8),
        name="factors",
    )(pieces)


SWAP = ((0, 1), (1, 0))


def body(hidden_in, query, key_value, grad_out, lengths, owner):
    mine = lax.all_to_all(
        jnp.broadcast_to(key_value, (CHIPS, ROWS, 2 * HD)), "chip", 0, 0, tiled=True
    )
    other = lax.ppermute(mine, "core", SWAP)
    q_rows, go_rows, row_low = prepare(lengths, query[0], grad_out[0])
    dq_t, keep, send = attention(q_rows, go_rows, row_low, mine, other)
    dkv = (keep + lax.ppermute(send, "core", SWAP).astype(F32)).astype(BF16)
    grad_query = query_gradient(dq_t)
    dkv = lax.all_to_all(dkv, "chip", 0, 0, tiled=True)
    hidden = hidden_in[0]
    grad_kv, k_t, send = weight_send(dkv, hidden)
    arrived = lax.ppermute(send, "core", SWAP)
    keep = weight_keep(k_t, hidden)
    wg = (keep + arrived.astype(F32)).astype(BF16).reshape(PLANE, TILES * 4, TILE)
    wg = lax.all_to_all(wg, ("yl", "chip"), 0, 0, tiled=True)
    outgoing = to_owners(owner.reshape(1, TILES), wg)
    incoming = lax.all_to_all(outgoing, "z", 0, 0, tiled=True)
    pieces = lax.all_to_all(owned_sum(incoming), ("yl", "chip", "core"), 0, 0, tiled=True)
    return grad_query[None], grad_kv[None], factors_of(pieces)[None]


def solution(mesh):
    fine = Mesh(mesh.devices.reshape(N_YL, N_Z, CHIPS, 2), ("yl", "z", "chip", "core"))
    dp, ctx = ("yl", "z"), ("chip", "core")
    split = P(dp, ctx, None)
    return jax.shard_map(
        body,
        mesh=fine,
        in_specs=(split, split, split, split, P(dp, None), P()),
        out_specs=(split, split, P(dp, None, None, None, None)),
        check_vma=False,
    )
```

```python
import math

import jax
import jax.numpy as jnp
from jax import lax
from jax.experimental import pallas as pl
from jax.experimental.pallas import tpu as pltpu
from jax.sharding import Mesh
from jax.sharding import PartitionSpec as P

HEADS = 8
HD = 128
TILE = 128
ROWS = 128
CHIPS = 8
SEQ = 2048
HALF = SEQ // 2
TILES = 64
CAP = 4
N_DP = 32
MODEL = 8192
N_YL = 2
N_Z = 16
PLANE = N_YL * CHIPS
OWNED = N_YL * CAP * 4
GROUP = 2
HIDDEN_NEG = -1e30
SCALE = 1.0 / math.sqrt(HD)
EXP2_SCALE = SCALE * math.log2(math.e)
F32 = jnp.float32
BF16 = jnp.bfloat16


def prepare_kernel(
    lengths_hbm, q_hbm, go_hbm, q_rows, go_rows, low_ref, lengths_ref, q_ref, go_ref, sems
):
    copies = [
        pltpu.make_async_copy(lengths_hbm, lengths_ref, sems.at[0]),
        pltpu.make_async_copy(q_hbm, q_ref, sems.at[1]),
        pltpu.make_async_copy(go_hbm, go_ref, sems.at[2]),
    ]
    for copy in copies:
        copy.start()
    first = (2 * lax.axis_index("chip") + lax.axis_index("core")) * ROWS
    row_pos = first + lax.broadcasted_iota(jnp.int32, low_ref.shape, 1)
    row_low = jnp.zeros(low_ref.shape, jnp.int32)
    end = jnp.int32(0)
    copies[0].wait()
    for d in range(lengths_ref.shape[1]):
        end = end + lengths_ref[0, d]
        row_low = jnp.maximum(row_low, jnp.where(row_pos >= end, end, 0))
    low_ref[...] = row_low
    for copy, rows, ref in ((copies[1], q_rows, q_ref), (copies[2], go_rows, go_ref)):
        copy.wait()
        for h in range(HEADS):
            cols = pl.ds(h * HD, HD)
            rows[cols, :] = ref[:, cols]


def side_of(ref, part):
    return ref[:, :, part * HD : (part + 1) * HD].reshape(HALF, HD)


def products(w, ds, q_rows, go_rows, ref):
    dk = jnp.dot(ds[...], q_rows[...], preferred_element_type=F32) * SCALE
    dv = jnp.dot(w[...], go_rows[...], preferred_element_type=F32)
    dq_t = lax.dot_general(
        side_of(ref, 0), ds[...], (((0,), (0,)), ((), ())), preferred_element_type=F32
    )
    return dk.reshape(CHIPS, ROWS, HD), dv.reshape(CHIPS, ROWS, HD), dq_t


def attention_kernel(
    q_rows, go_rows, low_ref, mine_ref, other_ref,
    send_ref, dq_t, w_mine, ds_mine,
    w_other, ds_other, scores, prob_grads, top, total, delta,
):
    core = lax.axis_index("core")
    first = (2 * lax.axis_index("chip") + core) * ROWS
    row_pos = first + lax.broadcasted_iota(jnp.int32, (1, ROWS), 1)
    row_low = low_ref[0:1, :]
    groups = [pl.ds(g * GROUP * HD, GROUP * HD) for g in range(HEADS // GROUP)]
    sides = ((0, other_ref, 1 - core), (1, mine_ref, core))

    def fold(values, op):
        return op(values.reshape(values.shape[0] // 8, 8, values.shape[1]), axis=0)

    def against(rows, ref, cols):
        return lax.dot_general(
            rows, ref[cols, :], (((1,), (1,)), ((), ())), preferred_element_type=F32
        )

    for i, ref, side in sides:
        rows = pl.ds(i * HALF, HALF)
        shape = (CHIPS, ROWS, ROWS)
        chip = lax.broadcasted_iota(jnp.int32, shape, 0)
        pos = (2 * chip + side) * ROWS + lax.broadcasted_iota(jnp.int32, shape, 1)
        pos = pos.reshape(HALF, ROWS)
        seen = (pos >= row_low) & (pos <= row_pos)
        seen = jnp.concatenate([seen] * GROUP, axis=1)
        keys = side_of(ref, 0)
        for cols in groups:
            s = jnp.where(seen, against(keys, q_rows, cols), HIDDEN_NEG)
            scores[rows, cols] = s
            best = fold(s, jnp.max)
            top[:, cols] = best if i == 0 else jnp.maximum(top[:, cols], best)
    top[0:1, :] = jnp.max(top[...], axis=0, keepdims=True)
    for i, ref, side in sides:
        rows = pl.ds(i * HALF, HALF)
        values = side_of(ref, 1)
        for cols in groups:
            pg = against(values, go_rows, cols)
            p = jnp.exp2((scores[rows, cols] - top[0:1, cols]) * EXP2_SCALE)
            scores[rows, cols] = p
            prob_grads[rows, cols] = pg
            p_sum, pg_sum = fold(p, jnp.sum), fold(p * pg, jnp.sum)
            total[:, cols] = p_sum if i == 0 else total[:, cols] + p_sum
            delta[:, cols] = pg_sum if i == 0 else delta[:, cols] + pg_sum
    inverse = 1.0 / jnp.sum(total[...], axis=0, keepdims=True)
    total[0:1, :] = inverse
    delta[0:1, :] = jnp.sum(delta[...], axis=0, keepdims=True) * inverse
    for i, w_ref, ds_ref in ((0, w_other, ds_other), (1, w_mine, ds_mine)):
        rows = pl.ds(i * HALF, HALF)
        for cols in groups:
            w = scores[rows, cols] * total[0:1, cols]
            w_ref[:, cols] = w.astype(BF16)
            ds_ref[:, cols] = (w * (prob_grads[rows, cols] - delta[0:1, cols])).astype(BF16)
    dk, dv, dq = products(w_other, ds_other, q_rows, go_rows, other_ref)
    send_ref[:, :, :HD] = dk.astype(BF16)
    send_ref[:, :, HD:] = dv.astype(BF16)
    dq_t[...] = dq


def own_kernel(q_rows, go_rows, mine_ref, dq_in, w_mine, ds_mine, keep_ref, dq_t):
    dk, dv, dq = products(w_mine, ds_mine, q_rows, go_rows, mine_ref)
    keep_ref[:, :, :HD] = dk
    keep_ref[:, :, HD:] = dv
    dq_t[...] = dq_in[...] + dq


VMEM = pl.BlockSpec(memory_space=pltpu.VMEM)


def in_hbm(x):
    return pltpu.with_memory_space_constraint(x, pltpu.HBM)


def limit(mib):
    return pltpu.CompilerParams(vmem_limit_bytes=mib * 1024 * 1024)


def prepare(lengths, query, grad_out):
    hbm = pl.BlockSpec(memory_space=pltpu.HBM)
    wide = HEADS * HD
    return pl.pallas_call(
        prepare_kernel,
        out_shape=(
            jax.ShapeDtypeStruct((wide, HD), BF16),
            jax.ShapeDtypeStruct((wide, HD), BF16),
            jax.ShapeDtypeStruct((8, ROWS), jnp.int32),
        ),
        in_specs=[hbm, hbm, hbm],
        out_specs=(VMEM, VMEM, VMEM),
        scratch_shapes=[
            pltpu.SMEM((1, 8), jnp.int32),
            pltpu.VMEM((ROWS, wide), BF16),
            pltpu.VMEM((ROWS, wide), BF16),
            pltpu.SemaphoreType.DMA((3,)),
        ],
        compiler_params=limit(8),
        name="prepare_rows",
    )(in_hbm(lengths), in_hbm(query), in_hbm(grad_out))


def attention(q_rows, go_rows, row_low, mine, other):
    wide = HEADS * HD
    return pl.pallas_call(
        attention_kernel,
        out_shape=(
            jax.ShapeDtypeStruct((CHIPS, ROWS, 2 * HD), BF16),
            jax.ShapeDtypeStruct((HD, wide), F32),
            jax.ShapeDtypeStruct((HALF, wide), BF16),
            jax.ShapeDtypeStruct((HALF, wide), BF16),
        ),
        in_specs=[VMEM] * 5,
        out_specs=(VMEM,) * 4,
        scratch_shapes=[
            pltpu.VMEM((HALF, wide), BF16),
            pltpu.VMEM((HALF, wide), BF16),
            pltpu.VMEM((SEQ, wide), F32),
            pltpu.VMEM((SEQ, wide), F32),
            pltpu.VMEM((8, wide), F32),
            pltpu.VMEM((8, wide), F32),
            pltpu.VMEM((8, wide), F32),
        ],
        compiler_params=limit(30),
        name="attention_backward",
    )(q_rows, go_rows, row_low, mine, other)


def own_keys(q_rows, go_rows, mine, dq_t, w, ds):
    return pl.pallas_call(
        own_kernel,
        out_shape=(
            jax.ShapeDtypeStruct((CHIPS, ROWS, 2 * HD), F32),
            jax.ShapeDtypeStruct((HD, HEADS * HD), F32),
        ),
        in_specs=[VMEM] * 6,
        out_specs=(VMEM, VMEM),
        compiler_params=limit(12),
        name="own_keys",
    )(q_rows, go_rows, mine, dq_t, w, ds)


def low_half(shape, axis):
    return lax.broadcasted_iota(jnp.int32, shape, axis) < 4


def halves(keys):
    rows = keys.T.reshape(PLANE // 2, 2, 8, ROWS)
    even, odd = rows[:, 0], rows[:, 1]
    low = low_half(even.shape, 1)
    first = jnp.where(low, even, pltpu.roll(odd, 4, axis=1))
    second = jnp.where(low, pltpu.roll(even, 4, axis=1), odd)
    return first.reshape(HD // 2, ROWS), second.reshape(HD // 2, ROWS)


def half_tiles(k_t, hidden_ref, out_ref):
    shape = (PLANE // 2, 8, TILE)
    low = low_half(shape, 1)
    for quad in range(TILES // 4):
        hidden = hidden_ref[:, pl.ds(quad * 4 * TILE, 4 * TILE)]
        grad_t = jnp.dot(k_t, hidden, preferred_element_type=F32)
        tiles = [grad_t[:, i * TILE : (i + 1) * TILE].reshape(shape) for i in range(4)]
        evens, odds = [], []
        for even, odd in (tiles[:2], tiles[2:]):
            evens.append(jnp.where(low, even, pltpu.roll(odd, 4, axis=1)))
            odds.append(jnp.where(low, pltpu.roll(even, 4, axis=1), odd))
        rows = pl.ds(quad * 16, 16)
        out_ref[:, 0, rows, :] = jnp.concatenate(evens, axis=1).astype(out_ref.dtype)
        out_ref[:, 1, rows, :] = jnp.concatenate(odds, axis=1).astype(out_ref.dtype)


def weight_send_kernel(parts_ref, hidden_ref, kv_ref, k_ref, out_ref):
    core = lax.axis_index("core")
    low = jnp.sum(parts_ref[...].astype(F32), axis=0).astype(BF16)
    kv_ref[...] = low
    first, second = halves(low[:, :HD].astype(F32))
    k_ref[...] = jnp.where(core == 0, first, second).astype(BF16)
    half_tiles(jnp.where(core == 0, second, first).astype(BF16), hidden_ref, out_ref)


def weight_keep_kernel(
    owner_ref, k_ref, hidden_ref, dq_t, out_ref, dq_ref, place_ref, held
):
    for o in range(N_DP):
        held[o] = 0
    for t in range(TILES):
        o = owner_ref[0, t]
        slot = held[o]
        held[o] = slot + 1
        place_ref[0, t] = ((o & (N_Z - 1)) * N_YL + o // N_Z) * CAP + slot
    half_tiles(k_ref[...], hidden_ref, out_ref)
    for h in range(HEADS):
        cols = pl.ds(h * HD, HD)
        dq_ref[:, cols] = (dq_t[:, cols].T * SCALE).astype(BF16)


def weight_send(parts, hidden):
    return pl.pallas_call(
        weight_send_kernel,
        out_shape=(
            jax.ShapeDtypeStruct((ROWS, 2 * HD), BF16),
            jax.ShapeDtypeStruct((HD // 2, ROWS), BF16),
            jax.ShapeDtypeStruct((PLANE // 2, 2, TILES * 4, TILE), BF16),
        ),
        in_specs=[VMEM, VMEM],
        out_specs=(VMEM, VMEM, VMEM),
        compiler_params=limit(10),
        name="weight_tiles_to_send",
    )(parts, hidden)


def weight_keep(owner, k_t, hidden, dq_t):
    smem = pl.BlockSpec(memory_space=pltpu.SMEM)
    return pl.pallas_call(
        weight_keep_kernel,
        out_shape=(
            jax.ShapeDtypeStruct((PLANE // 2, 2, TILES * 4, TILE), F32),
            jax.ShapeDtypeStruct((ROWS, HEADS * HD), BF16),
            jax.ShapeDtypeStruct((1, TILES), jnp.int32),
        ),
        in_specs=[smem, VMEM, VMEM, VMEM],
        out_specs=(VMEM, VMEM, smem),
        scratch_shapes=[pltpu.SMEM((N_DP,), jnp.int32)],
        compiler_params=limit(10),
        name="weight_tiles_to_keep",
    )(owner, k_t, hidden, dq_t)


def owner_kernel(place_ref, parts_ref, out_ref, sums, placed):
    rows = TILES * 4
    own = jnp.sum(parts_ref[...].astype(F32), axis=0)
    sums[:rows, :] = own
    sums[rows:, :] = pltpu.roll(own.reshape(rows // 8, 8, TILE), 4, axis=1).reshape(rows, TILE)
    placed[...] = jnp.zeros(placed.shape, F32)
    low = low_half((8, TILE), 0)
    for t in range(TILES):
        place = place_ref[0, t]
        half = place & 1
        at = pl.ds(pl.multiple_of((place >> 1) * 8, 8), 8)
        source = pl.multiple_of((half ^ (t & 1)) * rows + (t // 2) * 8, 8)
        placed[at, :] = jnp.where(low == (half == 0), sums[pl.ds(source, 8), :], placed[at, :])
    out_ref[...] = placed[...].astype(BF16).reshape(out_ref.shape)


def to_owners(place, parts):
    return pl.pallas_call(
        owner_kernel,
        out_shape=jax.ShapeDtypeStruct((N_Z, OWNED, TILE), BF16),
        in_specs=[pl.BlockSpec(memory_space=pltpu.SMEM), VMEM],
        out_specs=VMEM,
        scratch_shapes=[
            pltpu.VMEM((2 * TILES * 4, TILE), F32),
            pltpu.VMEM((N_Z * OWNED, TILE), F32),
        ],
        compiler_params=limit(12),
        name="owner_slots",
    )(place, parts)


def sum_kernel(parts_ref, out_ref):
    gradient = jnp.sum(parts_ref[...].astype(F32), axis=0) * (1.0 / math.sqrt(N_DP * SEQ))
    gradient = gradient.astype(BF16)
    rows = OWNED // N_YL
    for yl in range(N_YL):
        piece = gradient[yl * rows : (yl + 1) * rows]
        out_ref[yl * PLANE : (yl + 1) * PLANE] = jnp.broadcast_to(piece[None], (PLANE, rows, TILE))


def owned_sum(parts):
    return pl.pallas_call(
        sum_kernel,
        out_shape=jax.ShapeDtypeStruct((2 * PLANE, OWNED // N_YL, TILE), BF16),
        in_specs=[VMEM],
        out_specs=VMEM,
        compiler_params=limit(8),
        name="owned_sum",
    )(parts)


def factor_kernel(pieces_ref, out_ref):
    pieces = pieces_ref[...].astype(F32)
    low = low_half((PLANE, 8, TILE), 1)
    for two in range(CAP // 2):
        pair = pieces[:, two * 8 : (two + 1) * 8, :].reshape(PLANE, 2, 8, TILE)
        even, odd = pair[:, 0], pair[:, 1]
        both = (
            jnp.where(low, even, pltpu.roll(odd, 4, axis=1)),
            jnp.where(low, pltpu.roll(even, 4, axis=1), odd),
        )
        for i in range(2):
            grad_t = both[i].reshape(TILE, TILE)
            flat = grad_t.astype(BF16)
            flat_t = grad_t.T.astype(BF16)
            s = 2 * two + i
            out_ref[s, 0] = jnp.dot(flat_t, flat, preferred_element_type=F32) * (1.0 / TILE)
            out_ref[s, 1] = jnp.dot(flat, flat_t, preferred_element_type=F32) * (1.0 / TILE)


def factors_of(pieces):
    return pl.pallas_call(
        factor_kernel,
        out_shape=jax.ShapeDtypeStruct((CAP, 2, TILE, TILE), F32),
        in_specs=[VMEM],
        out_specs=VMEM,
        compiler_params=limit(8),
        name="factors",
    )(pieces)


SWAP = ((0, 1), (1, 0))


def body(hidden_in, query, key_value, grad_out, lengths, owner):
    mine = lax.all_to_all(
        jnp.broadcast_to(key_value, (CHIPS, ROWS, 2 * HD)), "chip", 0, 0, tiled=True
    )
    other = lax.ppermute(mine, "core", SWAP)
    q_rows, go_rows, row_low = prepare(lengths, query[0], grad_out[0])
    send, dq_t, w, ds = attention(q_rows, go_rows, row_low, mine, other)
    arrived = lax.ppermute(send, "core", SWAP)
    keep, dq_t = own_keys(q_rows, go_rows, mine, dq_t, w, ds)
    dkv = (keep + arrived.astype(F32)).astype(BF16)
    dkv = lax.all_to_all(dkv, "chip", 0, 0, tiled=True)
    hidden = hidden_in[0]
    grad_kv, k_t, send = weight_send(dkv, hidden)
    arrived = lax.ppermute(send, "core", SWAP)
    keep, grad_query, place = weight_keep(owner.reshape(1, TILES), k_t, hidden, dq_t)
    wg = (keep + arrived.astype(F32)).astype(BF16).reshape(PLANE, TILES * 4, TILE)
    wg = lax.all_to_all(wg, ("yl", "chip"), 0, 0, tiled=True)
    outgoing = to_owners(place, wg)
    incoming = lax.all_to_all(outgoing, "z", 0, 0, tiled=True)
    pieces = lax.all_to_all(owned_sum(incoming), ("yl", "chip", "core"), 0, 0, tiled=True)
    return grad_query[None], grad_kv[None], factors_of(pieces)[None]


def solution(mesh):
    fine = Mesh(mesh.devices.reshape(N_YL, N_Z, CHIPS, 2), ("yl", "z", "chip", "core"))
    dp, ctx = ("yl", "z"), ("chip", "core")
    split = P(dp, ctx, None)
    return jax.shard_map(
        body,
        mesh=fine,
        in_specs=(split, split, split, split, P(dp, None), P()),
        out_specs=(split, split, P(dp, None, None, None, None)),
        check_vma=False,
    )
```

```python
import math

import jax
import jax.numpy as jnp
from jax import lax
from jax.experimental import pallas as pl
from jax.experimental.pallas import tpu as pltpu
from jax.sharding import Mesh
from jax.sharding import PartitionSpec as P

HEADS = 8
HD = 128
TILE = 128
ROWS = 128
CHIPS = 8
SEQ = 2048
HALF = SEQ // 2
TILES = 64
CAP = 4
N_DP = 32
MODEL = 8192
N_YL = 2
N_Z = 16
PLANE = N_YL * CHIPS
OWNED = N_YL * CAP * 4
GROUP = 2
HIDDEN_NEG = -1e30
SCALE = 1.0 / math.sqrt(HD)
EXP2_SCALE = SCALE * math.log2(math.e)
F32 = jnp.float32
BF16 = jnp.bfloat16


def prepare_kernel(
    lengths_hbm, q_hbm, go_hbm, q_rows, go_rows, low_ref, lengths_ref, q_ref, go_ref, sems
):
    copies = [
        pltpu.make_async_copy(lengths_hbm, lengths_ref, sems.at[0]),
        pltpu.make_async_copy(q_hbm, q_ref, sems.at[1]),
        pltpu.make_async_copy(go_hbm, go_ref, sems.at[2]),
    ]
    for copy in copies:
        copy.start()
    first = (2 * lax.axis_index("chip") + lax.axis_index("core")) * ROWS
    row_pos = first + lax.broadcasted_iota(jnp.int32, low_ref.shape, 1)
    row_low = jnp.zeros(low_ref.shape, jnp.int32)
    end = jnp.int32(0)
    copies[0].wait()
    for d in range(lengths_ref.shape[1]):
        end = end + lengths_ref[0, d]
        row_low = jnp.maximum(row_low, jnp.where(row_pos >= end, end, 0))
    low_ref[...] = row_low
    for copy, rows, ref in ((copies[1], q_rows, q_ref), (copies[2], go_rows, go_ref)):
        copy.wait()
        for h in range(HEADS):
            cols = pl.ds(h * HD, HD)
            rows[cols, :] = ref[:, cols]


def side_of(ref, part):
    return ref[:, :, part * HD : (part + 1) * HD].reshape(HALF, HD)


def products(w, ds, q_rows, go_rows):
    dk = jnp.dot(ds[...], q_rows[...], preferred_element_type=F32) * SCALE
    dv = jnp.dot(w[...], go_rows[...], preferred_element_type=F32)
    return dk.reshape(CHIPS, ROWS, HD), dv.reshape(CHIPS, ROWS, HD)


def attention_kernel(
    q_rows, go_rows, low_ref, mine_ref, other_ref,
    send_ref, w_mine, ds_mine, ds_other,
    w_other, probs, top, total, delta,
):
    core = lax.axis_index("core")
    first = (2 * lax.axis_index("chip") + core) * ROWS
    row_pos = first + lax.broadcasted_iota(jnp.int32, (1, ROWS), 1)
    row_low = low_ref[0:1, :]
    groups = [pl.ds(g * GROUP * HD, GROUP * HD) for g in range(HEADS // GROUP)]
    sides = (
        (0, other_ref, 1 - core, w_other, ds_other),
        (1, mine_ref, core, w_mine, ds_mine),
    )

    def fold(values, op):
        return op(values.reshape(values.shape[0] // 8, 8, values.shape[1]), axis=0)

    def against(rows, ref, cols):
        return lax.dot_general(
            rows, ref[cols, :], (((1,), (1,)), ((), ())), preferred_element_type=F32
        )

    def scores_of(ref, side):
        shape = (CHIPS, ROWS, ROWS)
        chip = lax.broadcasted_iota(jnp.int32, shape, 0)
        pos = (2 * chip + side) * ROWS + lax.broadcasted_iota(jnp.int32, shape, 1)
        pos = pos.reshape(HALF, ROWS)
        seen = (pos >= row_low) & (pos <= row_pos)
        seen = jnp.concatenate([seen] * GROUP, axis=1)
        keys = side_of(ref, 0)
        return lambda cols: jnp.where(seen, against(keys, q_rows, cols), HIDDEN_NEG)

    for i, ref, side, _, _ in sides:
        scores = scores_of(ref, side)
        for cols in groups:
            best = fold(scores(cols), jnp.max)
            top[:, cols] = best if i == 0 else jnp.maximum(top[:, cols], best)
    top[0:1, :] = jnp.max(top[...], axis=0, keepdims=True)
    for i, ref, side, _, _ in sides:
        scores = scores_of(ref, side)
        values = side_of(ref, 1)
        for cols in groups:
            pg = against(values, go_rows, cols)
            p = jnp.exp2((scores(cols) - top[0:1, cols]) * EXP2_SCALE)
            probs[pl.ds(i * HALF, HALF), cols] = p
            p_sum, pg_sum = fold(p, jnp.sum), fold(p * pg, jnp.sum)
            total[:, cols] = p_sum if i == 0 else total[:, cols] + p_sum
            delta[:, cols] = pg_sum if i == 0 else delta[:, cols] + pg_sum
    inverse = 1.0 / jnp.sum(total[...], axis=0, keepdims=True)
    total[0:1, :] = inverse
    delta[0:1, :] = jnp.sum(delta[...], axis=0, keepdims=True) * inverse
    for i, ref, _, w_ref, ds_ref in sides:
        values = side_of(ref, 1)
        for cols in groups:
            w = probs[pl.ds(i * HALF, HALF), cols] * total[0:1, cols]
            w_ref[:, cols] = w.astype(BF16)
            pg = against(values, go_rows, cols)
            ds_ref[:, cols] = (w * (pg - delta[0:1, cols])).astype(BF16)
    dk, dv = products(w_other, ds_other, q_rows, go_rows)
    send_ref[:, :, :HD] = dk.astype(BF16)
    send_ref[:, :, HD:] = dv.astype(BF16)


def own_kernel(q_rows, go_rows, w_mine, ds_mine, keep_ref):
    dk, dv = products(w_mine, ds_mine, q_rows, go_rows)
    keep_ref[:, :, :HD] = dk
    keep_ref[:, :, HD:] = dv


VMEM = pl.BlockSpec(memory_space=pltpu.VMEM)


def in_hbm(x):
    return pltpu.with_memory_space_constraint(x, pltpu.HBM)


def limit(mib):
    return pltpu.CompilerParams(vmem_limit_bytes=mib * 1024 * 1024)


def prepare(lengths, query, grad_out):
    hbm = pl.BlockSpec(memory_space=pltpu.HBM)
    wide = HEADS * HD
    return pl.pallas_call(
        prepare_kernel,
        out_shape=(
            jax.ShapeDtypeStruct((wide, HD), BF16),
            jax.ShapeDtypeStruct((wide, HD), BF16),
            jax.ShapeDtypeStruct((8, ROWS), jnp.int32),
        ),
        in_specs=[hbm, hbm, hbm],
        out_specs=(VMEM, VMEM, VMEM),
        scratch_shapes=[
            pltpu.SMEM((1, 8), jnp.int32),
            pltpu.VMEM((ROWS, wide), BF16),
            pltpu.VMEM((ROWS, wide), BF16),
            pltpu.SemaphoreType.DMA((3,)),
        ],
        compiler_params=limit(8),
        name="prepare_rows",
    )(in_hbm(lengths), in_hbm(query), in_hbm(grad_out))


SMEM = pl.BlockSpec(memory_space=pltpu.SMEM)


def attention(q_rows, go_rows, row_low, mine, other):
    wide = HEADS * HD
    half = jax.ShapeDtypeStruct((HALF, wide), BF16)
    return pl.pallas_call(
        attention_kernel,
        out_shape=(jax.ShapeDtypeStruct((CHIPS, ROWS, 2 * HD), BF16), half, half, half),
        in_specs=[VMEM] * 5,
        out_specs=(VMEM,) * 4,
        scratch_shapes=[
            pltpu.VMEM((HALF, wide), BF16),
            pltpu.VMEM((SEQ, wide), F32),
            pltpu.VMEM((8, wide), F32),
            pltpu.VMEM((8, wide), F32),
            pltpu.VMEM((8, wide), F32),
        ],
        compiler_params=limit(24),
        name="attention_backward",
    )(q_rows, go_rows, row_low, mine, other)


def own_keys(q_rows, go_rows, w, ds):
    return pl.pallas_call(
        own_kernel,
        out_shape=jax.ShapeDtypeStruct((CHIPS, ROWS, 2 * HD), F32),
        in_specs=[VMEM] * 4,
        out_specs=VMEM,
        compiler_params=limit(12),
        name="own_keys",
    )(q_rows, go_rows, w, ds)


def low_half(shape, axis):
    return lax.broadcasted_iota(jnp.int32, shape, axis) < 4


def halves(keys):
    rows = keys.T.reshape(PLANE // 2, 2, 8, ROWS)
    even, odd = rows[:, 0], rows[:, 1]
    low = low_half(even.shape, 1)
    first = jnp.where(low, even, pltpu.roll(odd, 4, axis=1))
    second = jnp.where(low, pltpu.roll(even, 4, axis=1), odd)
    return first.reshape(HD // 2, ROWS), second.reshape(HD // 2, ROWS)


def half_tiles(k_t, hidden_ref, out_ref):
    shape = (PLANE // 2, 8, TILE)
    low = low_half(shape, 1)
    for quad in range(TILES // 4):
        hidden = hidden_ref[:, pl.ds(quad * 4 * TILE, 4 * TILE)]
        grad_t = jnp.dot(k_t, hidden, preferred_element_type=F32)
        tiles = [grad_t[:, i * TILE : (i + 1) * TILE].reshape(shape) for i in range(4)]
        evens, odds = [], []
        for even, odd in (tiles[:2], tiles[2:]):
            evens.append(jnp.where(low, even, pltpu.roll(odd, 4, axis=1)))
            odds.append(jnp.where(low, pltpu.roll(even, 4, axis=1), odd))
        rows = pl.ds(quad * 16, 16)
        out_ref[:, 0, rows, :] = jnp.concatenate(evens, axis=1).astype(out_ref.dtype)
        out_ref[:, 1, rows, :] = jnp.concatenate(odds, axis=1).astype(out_ref.dtype)


def weight_send_kernel(parts_ref, hidden_ref, kv_ref, k_ref, out_ref):
    core = lax.axis_index("core")
    low = jnp.sum(parts_ref[...].astype(F32), axis=0).astype(BF16)
    kv_ref[...] = low
    first, second = halves(low[:, :HD].astype(F32))
    k_ref[...] = jnp.where(core == 0, first, second).astype(BF16)
    half_tiles(jnp.where(core == 0, second, first).astype(BF16), hidden_ref, out_ref)


def slot_table(owner_ref, place_ref):
    held = [jnp.int32(0)] * 4
    for t in range(TILES):
        o = owner_ref[0, t]
        word, shift = o >> 3, (o & 7) * 4
        count = jnp.int32(0)
        for i in range(4):
            count = jnp.where(word == i, held[i], count)
            held[i] = held[i] + jnp.where(word == i, 1 << shift, 0)
        slot = (count >> shift) & 15
        place_ref[0, t] = ((o & (N_Z - 1)) * N_YL + o // N_Z) * CAP + slot


def weight_keep_kernel(
    owner_ref, k_ref, hidden_ref, mine_ref, other_ref, ds_mine, ds_other,
    out_ref, dq_ref, place_ref,
):
    slot_table(owner_ref, place_ref)
    half_tiles(k_ref[...], hidden_ref, out_ref)
    dq_t = sum(
        lax.dot_general(
            side_of(ref, 0), ds[...], (((0,), (0,)), ((), ())), preferred_element_type=F32
        )
        for ref, ds in ((mine_ref, ds_mine), (other_ref, ds_other))
    )
    for h in range(HEADS):
        cols = slice(h * HD, (h + 1) * HD)
        dq_ref[:, cols] = (dq_t[:, cols].T * SCALE).astype(BF16)


def weight_send(parts, hidden):
    return pl.pallas_call(
        weight_send_kernel,
        out_shape=(
            jax.ShapeDtypeStruct((ROWS, 2 * HD), BF16),
            jax.ShapeDtypeStruct((HD // 2, ROWS), BF16),
            jax.ShapeDtypeStruct((PLANE // 2, 2, TILES * 4, TILE), BF16),
        ),
        in_specs=[VMEM, VMEM],
        out_specs=(VMEM, VMEM, VMEM),
        compiler_params=limit(10),
        name="weight_tiles_to_send",
    )(parts, hidden)


def weight_keep(owner, k_t, hidden, mine, other, ds_mine, ds_other):
    return pl.pallas_call(
        weight_keep_kernel,
        out_shape=(
            jax.ShapeDtypeStruct((PLANE // 2, 2, TILES * 4, TILE), F32),
            jax.ShapeDtypeStruct((ROWS, HEADS * HD), BF16),
            jax.ShapeDtypeStruct((1, TILES), jnp.int32),
        ),
        in_specs=[SMEM] + [VMEM] * 6,
        out_specs=(VMEM, VMEM, SMEM),
        compiler_params=limit(12),
        name="weight_tiles_to_keep",
    )(owner, k_t, hidden, mine, other, ds_mine, ds_other)


def owner_kernel(place_ref, parts_ref, out_ref, sums, placed):
    rows = TILES * 4
    own = jnp.sum(parts_ref[...].astype(F32), axis=0)
    sums[:rows, :] = own
    sums[rows:, :] = pltpu.roll(own.reshape(rows // 8, 8, TILE), 4, axis=1).reshape(rows, TILE)
    placed[...] = jnp.zeros(placed.shape, F32)
    low = low_half((8, TILE), 0)
    for t in range(TILES):
        place = place_ref[0, t]
        half = place & 1
        at = pl.ds(pl.multiple_of((place >> 1) * 8, 8), 8)
        source = pl.multiple_of((half ^ (t & 1)) * rows + (t // 2) * 8, 8)
        placed[at, :] = jnp.where(low == (half == 0), sums[pl.ds(source, 8), :], placed[at, :])
    out_ref[...] = placed[...].astype(BF16).reshape(out_ref.shape)


def to_owners(place, parts):
    return pl.pallas_call(
        owner_kernel,
        out_shape=jax.ShapeDtypeStruct((N_Z, OWNED, TILE), BF16),
        in_specs=[pl.BlockSpec(memory_space=pltpu.SMEM), VMEM],
        out_specs=VMEM,
        scratch_shapes=[
            pltpu.VMEM((2 * TILES * 4, TILE), F32),
            pltpu.VMEM((N_Z * OWNED, TILE), F32),
        ],
        compiler_params=limit(12),
        name="owner_slots",
    )(place, parts)


def sum_kernel(parts_ref, out_ref):
    gradient = jnp.sum(parts_ref[...].astype(F32), axis=0) * (1.0 / math.sqrt(N_DP * SEQ))
    gradient = gradient.astype(BF16)
    rows = OWNED // N_YL
    for yl in range(N_YL):
        piece = gradient[yl * rows : (yl + 1) * rows]
        out_ref[yl * PLANE : (yl + 1) * PLANE] = jnp.broadcast_to(piece[None], (PLANE, rows, TILE))


def owned_sum(parts):
    return pl.pallas_call(
        sum_kernel,
        out_shape=jax.ShapeDtypeStruct((2 * PLANE, OWNED // N_YL, TILE), BF16),
        in_specs=[VMEM],
        out_specs=VMEM,
        compiler_params=limit(8),
        name="owned_sum",
    )(parts)


def factor_kernel(pieces_ref, out_ref):
    pieces = pieces_ref[...].astype(F32)
    low = low_half((PLANE, 8, TILE), 1)
    for two in range(CAP // 2):
        pair = pieces[:, two * 8 : (two + 1) * 8, :].reshape(PLANE, 2, 8, TILE)
        even, odd = pair[:, 0], pair[:, 1]
        both = (
            jnp.where(low, even, pltpu.roll(odd, 4, axis=1)),
            jnp.where(low, pltpu.roll(even, 4, axis=1), odd),
        )
        for i in range(2):
            grad_t = both[i].reshape(TILE, TILE)
            flat = grad_t.astype(BF16)
            flat_t = grad_t.T.astype(BF16)
            s = 2 * two + i
            out_ref[s, 0] = jnp.dot(flat_t, flat, preferred_element_type=F32) * (1.0 / TILE)
            out_ref[s, 1] = jnp.dot(flat, flat_t, preferred_element_type=F32) * (1.0 / TILE)


def factors_of(pieces):
    return pl.pallas_call(
        factor_kernel,
        out_shape=jax.ShapeDtypeStruct((CAP, 2, TILE, TILE), F32),
        in_specs=[VMEM],
        out_specs=VMEM,
        compiler_params=limit(8),
        name="factors",
    )(pieces)


SWAP = ((0, 1), (1, 0))


def body(hidden_in, query, key_value, grad_out, lengths, owner):
    mine = lax.all_to_all(
        jnp.broadcast_to(key_value, (CHIPS, ROWS, 2 * HD)), "chip", 0, 0, tiled=True
    )
    other = lax.ppermute(mine, "core", SWAP)
    q_rows, go_rows, row_low = prepare(lengths, query[0], grad_out[0])
    send, w, ds_mine, ds_other = attention(q_rows, go_rows, row_low, mine, other)
    arrived = lax.ppermute(send, "core", SWAP)
    keep = own_keys(q_rows, go_rows, w, ds_mine)
    dkv = (keep + arrived.astype(F32)).astype(BF16)
    dkv = lax.all_to_all(dkv, "chip", 0, 0, tiled=True)
    hidden = hidden_in[0]
    grad_kv, k_t, send = weight_send(dkv, hidden)
    arrived = lax.ppermute(send, "core", SWAP)
    keep, grad_query, place = weight_keep(
        owner.reshape(1, TILES), k_t, hidden, mine, other, ds_mine, ds_other
    )
    wg = (keep + arrived.astype(F32)).astype(BF16).reshape(PLANE, TILES * 4, TILE)
    wg = lax.all_to_all(wg, ("yl", "chip"), 0, 0, tiled=True)
    outgoing = to_owners(place, wg)
    incoming = lax.all_to_all(outgoing, "z", 0, 0, tiled=True)
    pieces = lax.all_to_all(owned_sum(incoming), ("yl", "chip", "core"), 0, 0, tiled=True)
    return grad_query[None], grad_kv[None], factors_of(pieces)[None]


def solution(mesh):
    fine = Mesh(mesh.devices.reshape(N_YL, N_Z, CHIPS, 2), ("yl", "z", "chip", "core"))
    dp, ctx = ("yl", "z"), ("chip", "core")
    split = P(dp, ctx, None)
    return jax.shard_map(
        body,
        mesh=fine,
        in_specs=(split, split, split, split, P(dp, None), P()),
        out_specs=(split, split, P(dp, None, None, None, None)),
        check_vma=False,
    )
```

```python
import math

import jax
import jax.numpy as jnp
from jax import lax
from jax.experimental import pallas as pl
from jax.experimental.pallas import tpu as pltpu
from jax.sharding import Mesh
from jax.sharding import PartitionSpec as P

HEADS = 8
HD = 128
TILE = 128
ROWS = 128
CHIPS = 8
SEQ = 2048
HALF = SEQ // 2
TILES = 64
CAP = 4
N_DP = 32
MODEL = 8192
N_YL = 2
N_Z = 16
N_X = 4
N_YH = 2
PLANE = N_YL * CHIPS
OWNED = N_YL * CAP * 4
GROUP = 2
HIDDEN_NEG = -1e30
SCALE = 1.0 / math.sqrt(HD)
EXP2_SCALE = SCALE * math.log2(math.e)
F32 = jnp.float32
BF16 = jnp.bfloat16


def first_position():
    chip = N_YH * lax.axis_index("x") + lax.axis_index("yh")
    return (2 * chip + lax.axis_index("core")) * ROWS


def prepare_kernel(
    lengths_hbm, q_hbm, go_hbm, q_rows, go_rows, low_ref, lengths_ref, q_ref, go_ref, sems
):
    copies = [
        pltpu.make_async_copy(lengths_hbm, lengths_ref, sems.at[0]),
        pltpu.make_async_copy(q_hbm, q_ref, sems.at[1]),
        pltpu.make_async_copy(go_hbm, go_ref, sems.at[2]),
    ]
    for copy in copies:
        copy.start()
    first = first_position()
    row_pos = first + lax.broadcasted_iota(jnp.int32, low_ref.shape, 1)
    row_low = jnp.zeros(low_ref.shape, jnp.int32)
    end = jnp.int32(0)
    copies[0].wait()
    for d in range(lengths_ref.shape[1]):
        end = end + lengths_ref[0, d]
        row_low = jnp.maximum(row_low, jnp.where(row_pos >= end, end, 0))
    low_ref[...] = row_low
    for copy, rows, ref in ((copies[1], q_rows, q_ref), (copies[2], go_rows, go_ref)):
        copy.wait()
        for h in range(HEADS):
            cols = pl.ds(h * HD, HD)
            rows[cols, :] = ref[:, cols]


def side_of(ref, part):
    return ref[:, :, part * HD : (part + 1) * HD].reshape(HALF, HD)


def products(w, ds, q_rows, go_rows, ref):
    dk = jnp.dot(ds[...], q_rows[...], preferred_element_type=F32) * SCALE
    dv = jnp.dot(w[...], go_rows[...], preferred_element_type=F32)
    dq_t = lax.dot_general(
        side_of(ref, 0), ds[...], (((0,), (0,)), ((), ())), preferred_element_type=F32
    )
    return dk.reshape(CHIPS, ROWS, HD), dv.reshape(CHIPS, ROWS, HD), dq_t


def attention_kernel(
    q_rows, go_rows, low_ref, mine_ref, other_ref,
    send_ref, dq_t, w_mine, ds_mine,
    w_other, ds_other, probs, top, total, delta,
):
    core = lax.axis_index("core")
    first = first_position()
    row_pos = first + lax.broadcasted_iota(jnp.int32, (1, ROWS), 1)
    row_low = low_ref[0:1, :]
    groups = [pl.ds(g * GROUP * HD, GROUP * HD) for g in range(HEADS // GROUP)]
    sides = (
        (0, other_ref, 1 - core, w_other, ds_other),
        (1, mine_ref, core, w_mine, ds_mine),
    )

    def fold(values, op):
        return op(values.reshape(values.shape[0] // 8, 8, values.shape[1]), axis=0)

    def against(rows, ref, cols):
        return lax.dot_general(
            rows, ref[cols, :], (((1,), (1,)), ((), ())), preferred_element_type=F32
        )

    def scores_of(ref, side):
        shape = (CHIPS, ROWS, ROWS)
        place = lax.broadcasted_iota(jnp.int32, shape, 0)
        chip = N_YH * (place & (N_X - 1)) + place // N_X
        pos = (2 * chip + side) * ROWS + lax.broadcasted_iota(jnp.int32, shape, 1)
        pos = pos.reshape(HALF, ROWS)
        seen = (pos >= row_low) & (pos <= row_pos)
        seen = jnp.concatenate([seen] * GROUP, axis=1)
        keys = side_of(ref, 0)
        return lambda cols: jnp.where(seen, against(keys, q_rows, cols), HIDDEN_NEG)

    for i, ref, side, _, _ in sides:
        scores = scores_of(ref, side)
        for cols in groups:
            best = fold(scores(cols), jnp.max)
            top[:, cols] = best if i == 0 else jnp.maximum(top[:, cols], best)
    top[0:1, :] = jnp.max(top[...], axis=0, keepdims=True)
    for i, ref, side, _, _ in sides:
        scores = scores_of(ref, side)
        values = side_of(ref, 1)
        for cols in groups:
            pg = against(values, go_rows, cols)
            p = jnp.exp2((scores(cols) - top[0:1, cols]) * EXP2_SCALE)
            probs[pl.ds(i * HALF, HALF), cols] = p
            p_sum, pg_sum = fold(p, jnp.sum), fold(p * pg, jnp.sum)
            total[:, cols] = p_sum if i == 0 else total[:, cols] + p_sum
            delta[:, cols] = pg_sum if i == 0 else delta[:, cols] + pg_sum
    inverse = 1.0 / jnp.sum(total[...], axis=0, keepdims=True)
    total[0:1, :] = inverse
    delta[0:1, :] = jnp.sum(delta[...], axis=0, keepdims=True) * inverse
    for i, ref, _, w_ref, ds_ref in sides:
        values = side_of(ref, 1)
        for cols in groups:
            w = probs[pl.ds(i * HALF, HALF), cols] * total[0:1, cols]
            w_ref[:, cols] = w.astype(BF16)
            pg = against(values, go_rows, cols)
            ds_ref[:, cols] = (w * (pg - delta[0:1, cols])).astype(BF16)
    dk, dv, dq = products(w_other, ds_other, q_rows, go_rows, other_ref)
    send_ref[:, :, :HD] = dk.astype(BF16)
    send_ref[:, :, HD:] = dv.astype(BF16)
    dq_t[...] = dq


def own_kernel(q_rows, go_rows, mine_ref, dq_in, w_mine, ds_mine, keep_ref, dq_t):
    dk, dv, dq = products(w_mine, ds_mine, q_rows, go_rows, mine_ref)
    keep_ref[:, :, :HD] = dk
    keep_ref[:, :, HD:] = dv
    dq_t[...] = dq_in[...] + dq


VMEM = pl.BlockSpec(memory_space=pltpu.VMEM)


def in_hbm(x):
    return pltpu.with_memory_space_constraint(x, pltpu.HBM)


def limit(mib):
    return pltpu.CompilerParams(vmem_limit_bytes=mib * 1024 * 1024)


def prepare(lengths, query, grad_out):
    hbm = pl.BlockSpec(memory_space=pltpu.HBM)
    wide = HEADS * HD
    return pl.pallas_call(
        prepare_kernel,
        out_shape=(
            jax.ShapeDtypeStruct((wide, HD), BF16),
            jax.ShapeDtypeStruct((wide, HD), BF16),
            jax.ShapeDtypeStruct((8, ROWS), jnp.int32),
        ),
        in_specs=[hbm, hbm, hbm],
        out_specs=(VMEM, VMEM, VMEM),
        scratch_shapes=[
            pltpu.SMEM((1, 8), jnp.int32),
            pltpu.VMEM((ROWS, wide), BF16),
            pltpu.VMEM((ROWS, wide), BF16),
            pltpu.SemaphoreType.DMA((3,)),
        ],
        compiler_params=limit(8),
        name="prepare_rows",
    )(in_hbm(lengths), in_hbm(query), in_hbm(grad_out))


SMEM = pl.BlockSpec(memory_space=pltpu.SMEM)


def attention(q_rows, go_rows, row_low, mine, other):
    wide = HEADS * HD
    half = jax.ShapeDtypeStruct((HALF, wide), BF16)
    return pl.pallas_call(
        attention_kernel,
        out_shape=(
            jax.ShapeDtypeStruct((CHIPS, ROWS, 2 * HD), BF16),
            jax.ShapeDtypeStruct((HD, wide), F32),
            half,
            half,
        ),
        in_specs=[VMEM] * 5,
        out_specs=(VMEM,) * 4,
        scratch_shapes=[
            pltpu.VMEM((HALF, wide), BF16),
            pltpu.VMEM((HALF, wide), BF16),
            pltpu.VMEM((SEQ, wide), F32),
            pltpu.VMEM((8, wide), F32),
            pltpu.VMEM((8, wide), F32),
            pltpu.VMEM((8, wide), F32),
        ],
        compiler_params=limit(24),
        name="attention_backward",
    )(q_rows, go_rows, row_low, mine, other)


def own_keys(q_rows, go_rows, mine, dq_t, w, ds):
    return pl.pallas_call(
        own_kernel,
        out_shape=(
            jax.ShapeDtypeStruct((CHIPS, ROWS, 2 * HD), F32),
            jax.ShapeDtypeStruct((HD, HEADS * HD), F32),
        ),
        in_specs=[VMEM] * 6,
        out_specs=(VMEM, VMEM),
        compiler_params=limit(12),
        name="own_keys",
    )(q_rows, go_rows, mine, dq_t, w, ds)


def low_half(shape, axis):
    return lax.broadcasted_iota(jnp.int32, shape, axis) < 4


def halves(keys):
    rows = keys.T.reshape(PLANE // 2, 2, 8, ROWS)
    even, odd = rows[:, 0], rows[:, 1]
    low = low_half(even.shape, 1)
    first = jnp.where(low, even, pltpu.roll(odd, 4, axis=1))
    second = jnp.where(low, pltpu.roll(even, 4, axis=1), odd)
    return first.reshape(HD // 2, ROWS), second.reshape(HD // 2, ROWS)


def half_tiles(k_t, hidden_ref, out_ref):
    shape = (PLANE // 2, 8, TILE)
    low = low_half(shape, 1)
    for quad in range(TILES // 4):
        hidden = hidden_ref[:, pl.ds(quad * 4 * TILE, 4 * TILE)]
        grad_t = jnp.dot(k_t, hidden, preferred_element_type=F32)
        tiles = [grad_t[:, i * TILE : (i + 1) * TILE].reshape(shape) for i in range(4)]
        evens, odds = [], []
        for even, odd in (tiles[:2], tiles[2:]):
            evens.append(jnp.where(low, even, pltpu.roll(odd, 4, axis=1)))
            odds.append(jnp.where(low, pltpu.roll(even, 4, axis=1), odd))
        rows = pl.ds(quad * 16, 16)
        out_ref[:, 0, rows, :] = jnp.concatenate(evens, axis=1).astype(out_ref.dtype)
        out_ref[:, 1, rows, :] = jnp.concatenate(odds, axis=1).astype(out_ref.dtype)


def weight_send_kernel(parts_ref, hidden_ref, kv_ref, k_ref, out_ref):
    core = lax.axis_index("core")
    low = jnp.sum(parts_ref[...].astype(F32), axis=0).astype(BF16)
    kv_ref[...] = low
    first, second = halves(low[:, :HD].astype(F32))
    k_ref[...] = jnp.where(core == 0, first, second).astype(BF16)
    half_tiles(jnp.where(core == 0, second, first).astype(BF16), hidden_ref, out_ref)


def slot_table(owner_ref, place_ref):
    held = [jnp.int32(0)] * 4
    for t in range(TILES):
        o = owner_ref[0, t]
        word, shift = o >> 3, (o & 7) * 4
        count = jnp.int32(0)
        for i in range(4):
            count = jnp.where(word == i, held[i], count)
            held[i] = held[i] + jnp.where(word == i, 1 << shift, 0)
        slot = (count >> shift) & 15
        place_ref[0, t] = ((o & (N_Z - 1)) * N_YL + o // N_Z) * CAP + slot


def weight_keep_kernel(owner_ref, k_ref, hidden_ref, dq_t, out_ref, dq_ref, place_ref):
    slot_table(owner_ref, place_ref)
    half_tiles(k_ref[...], hidden_ref, out_ref)
    for h in range(HEADS):
        cols = pl.ds(h * HD, HD)
        dq_ref[:, cols] = (dq_t[:, cols].T * SCALE).astype(BF16)


def weight_send(parts, hidden):
    return pl.pallas_call(
        weight_send_kernel,
        out_shape=(
            jax.ShapeDtypeStruct((ROWS, 2 * HD), BF16),
            jax.ShapeDtypeStruct((HD // 2, ROWS), BF16),
            jax.ShapeDtypeStruct((PLANE // 2, 2, TILES * 4, TILE), BF16),
        ),
        in_specs=[VMEM, VMEM],
        out_specs=(VMEM, VMEM, VMEM),
        compiler_params=limit(10),
        name="weight_tiles_to_send",
    )(parts, hidden)


def weight_keep(owner, k_t, hidden, dq_t):
    return pl.pallas_call(
        weight_keep_kernel,
        out_shape=(
            jax.ShapeDtypeStruct((PLANE // 2, 2, TILES * 4, TILE), F32),
            jax.ShapeDtypeStruct((ROWS, HEADS * HD), BF16),
            jax.ShapeDtypeStruct((1, TILES), jnp.int32),
        ),
        in_specs=[SMEM] + [VMEM] * 3,
        out_specs=(VMEM, VMEM, SMEM),
        compiler_params=limit(12),
        name="weight_tiles_to_keep",
    )(owner, k_t, hidden, dq_t)


def owner_kernel(place_ref, parts_ref, out_ref, sums, placed):
    rows = TILES * 4
    own = jnp.sum(parts_ref[...].astype(F32), axis=0)
    sums[:rows, :] = own
    sums[rows:, :] = pltpu.roll(own.reshape(rows // 8, 8, TILE), 4, axis=1).reshape(rows, TILE)
    placed[...] = jnp.zeros(placed.shape, F32)
    low = low_half((8, TILE), 0)
    for t in range(TILES):
        place = place_ref[0, t]
        half = place & 1
        at = pl.ds(pl.multiple_of((place >> 1) * 8, 8), 8)
        source = pl.multiple_of((half ^ (t & 1)) * rows + (t // 2) * 8, 8)
        placed[at, :] = jnp.where(low == (half == 0), sums[pl.ds(source, 8), :], placed[at, :])
    out_ref[...] = placed[...].astype(BF16).reshape(out_ref.shape)


def to_owners(place, parts):
    return pl.pallas_call(
        owner_kernel,
        out_shape=jax.ShapeDtypeStruct((N_Z, OWNED, TILE), BF16),
        in_specs=[pl.BlockSpec(memory_space=pltpu.SMEM), VMEM],
        out_specs=VMEM,
        scratch_shapes=[
            pltpu.VMEM((2 * TILES * 4, TILE), F32),
            pltpu.VMEM((N_Z * OWNED, TILE), F32),
        ],
        compiler_params=limit(12),
        name="owner_slots",
    )(place, parts)


def sum_kernel(parts_ref, out_ref):
    gradient = jnp.sum(parts_ref[...].astype(F32), axis=0) * (1.0 / math.sqrt(N_DP * SEQ))
    gradient = gradient.astype(BF16)
    rows = OWNED // N_YL
    some = 2 * N_YH
    for yl in range(N_YL):
        piece = gradient[yl * rows : (yl + 1) * rows]
        piece = jnp.broadcast_to(piece[None], (some, rows, TILE))
        for x in range(N_X):
            at = (x * N_YL + yl) * some
            out_ref[at : at + some] = piece


def owned_sum(parts):
    return pl.pallas_call(
        sum_kernel,
        out_shape=jax.ShapeDtypeStruct((2 * PLANE, OWNED // N_YL, TILE), BF16),
        in_specs=[VMEM],
        out_specs=VMEM,
        compiler_params=limit(8),
        name="owned_sum",
    )(parts)


def factor_kernel(pieces_ref, out_ref):
    pieces = pieces_ref[...].astype(F32)
    low = low_half((PLANE, 8, TILE), 1)
    for two in range(CAP // 2):
        pair = pieces[:, two * 8 : (two + 1) * 8, :].reshape(PLANE, 2, 8, TILE)
        even, odd = pair[:, 0], pair[:, 1]
        both = (
            jnp.where(low, even, pltpu.roll(odd, 4, axis=1)),
            jnp.where(low, pltpu.roll(even, 4, axis=1), odd),
        )
        for i in range(2):
            grad_t = both[i].reshape(TILE, TILE)
            flat = grad_t.astype(BF16)
            flat_t = grad_t.T.astype(BF16)
            s = 2 * two + i
            out_ref[s, 0] = jnp.dot(flat_t, flat, preferred_element_type=F32) * (1.0 / TILE)
            out_ref[s, 1] = jnp.dot(flat, flat_t, preferred_element_type=F32) * (1.0 / TILE)


def factors_of(pieces):
    return pl.pallas_call(
        factor_kernel,
        out_shape=jax.ShapeDtypeStruct((CAP, 2, TILE, TILE), F32),
        in_specs=[VMEM],
        out_specs=VMEM,
        compiler_params=limit(8),
        name="factors",
    )(pieces)


SWAP = ((0, 1), (1, 0))
CHIP_AXES = ("yh", "x")
PLANE_AXES = ("x", "yl", "yh")


def body(hidden_in, query, key_value, grad_out, lengths, owner):
    mine = lax.all_to_all(
        jnp.broadcast_to(key_value, (CHIPS, ROWS, 2 * HD)), CHIP_AXES, 0, 0, tiled=True
    )
    other = lax.ppermute(mine, "core", SWAP)
    q_rows, go_rows, row_low = prepare(lengths, query[0], grad_out[0])
    send, dq_t, w, ds = attention(q_rows, go_rows, row_low, mine, other)
    arrived = lax.ppermute(send, "core", SWAP)
    keep, dq_t = own_keys(q_rows, go_rows, mine, dq_t, w, ds)
    dkv = (keep + arrived.astype(F32)).astype(BF16)
    dkv = lax.all_to_all(dkv, CHIP_AXES, 0, 0, tiled=True)
    hidden = hidden_in[0]
    grad_kv, k_t, send = weight_send(dkv, hidden)
    arrived = lax.ppermute(send, "core", SWAP)
    keep, grad_query, place = weight_keep(owner.reshape(1, TILES), k_t, hidden, dq_t)
    wg = (keep + arrived.astype(F32)).astype(BF16).reshape(PLANE, TILES * 4, TILE)
    wg = lax.all_to_all(wg, PLANE_AXES, 0, 0, tiled=True)
    outgoing = to_owners(place, wg)
    incoming = lax.all_to_all(outgoing, "z", 0, 0, tiled=True)
    pieces = lax.all_to_all(owned_sum(incoming), PLANE_AXES + ("core",), 0, 0, tiled=True)
    return grad_query[None], grad_kv[None], factors_of(pieces)[None]


def solution(mesh):
    fine = Mesh(
        mesh.devices.reshape(N_YL, N_Z, N_X, N_YH, 2), ("yl", "z", "x", "yh", "core")
    )
    dp, ctx = ("yl", "z"), ("x", "yh", "core")
    split = P(dp, ctx, None)
    return jax.shard_map(
        body,
        mesh=fine,
        in_specs=(split, split, split, split, P(dp, None), P()),
        out_specs=(split, split, P(dp, None, None, None, None)),
        check_vma=False,
    )
```

```python
import math

import jax
import jax.numpy as jnp
from jax import lax
from jax.experimental import pallas as pl
from jax.experimental.pallas import tpu as pltpu
from jax.sharding import Mesh
from jax.sharding import PartitionSpec as P

HEADS = 8
HD = 128
TILE = 128
ROWS = 128
CHIPS = 8
SEQ = 2048
HALF = SEQ // 2
TILES = 64
CAP = 4
N_DP = 32
MODEL = 8192
N_YL = 2
N_Z = 16
N_X = 4
N_YH = 2
PLANE = N_YL * CHIPS
OWNED = N_YL * CAP * 4
GROUP = 2
HIDDEN_NEG = -1e30
SCALE = 1.0 / math.sqrt(HD)
EXP2_SCALE = SCALE * math.log2(math.e)
F32 = jnp.float32
BF16 = jnp.bfloat16


def first_position():
    chip = N_YH * lax.axis_index("x") + lax.axis_index("yh")
    return (2 * chip + lax.axis_index("core")) * ROWS


def slot_table(owner):
    across = jnp.broadcast_to(owner.astype(F32), (TILES, TILES))
    earlier = lax.broadcasted_iota(jnp.int32, (TILES, TILES), 0) < lax.broadcasted_iota(
        jnp.int32, (TILES, TILES), 1
    )
    same = jnp.where((across.T == across) & earlier, 1.0, 0.0)
    slot = jnp.sum(same, axis=0, keepdims=True).astype(jnp.int32)
    return ((owner & (N_Z - 1)) * N_YL + (owner >> 4)) * CAP + slot


def prepare_kernel(
    lengths_hbm, owner_hbm, q_hbm, go_hbm,
    q_rows, go_rows, low_ref, place_ref,
    lengths_ref, owner_ref, q_ref, go_ref, sems,
):
    copies = [
        pltpu.make_async_copy(lengths_hbm, lengths_ref, sems.at[0]),
        pltpu.make_async_copy(owner_hbm, owner_ref, sems.at[1]),
        pltpu.make_async_copy(q_hbm, q_ref, sems.at[2]),
        pltpu.make_async_copy(go_hbm, go_ref, sems.at[3]),
    ]
    for copy in copies:
        copy.start()
    first = first_position()
    row_pos = first + lax.broadcasted_iota(jnp.int32, low_ref.shape, 1)
    row_low = jnp.zeros(low_ref.shape, jnp.int32)
    end = jnp.int32(0)
    copies[0].wait()
    for d in range(lengths_ref.shape[1]):
        end = end + lengths_ref[0, d]
        row_low = jnp.maximum(row_low, jnp.where(row_pos >= end, end, 0))
    low_ref[...] = row_low
    copies[1].wait()
    place_ref[...] = slot_table(owner_ref[...])
    for copy, rows, ref in ((copies[2], q_rows, q_ref), (copies[3], go_rows, go_ref)):
        copy.wait()
        for h in range(HEADS):
            cols = pl.ds(h * HD, HD)
            rows[cols, :] = ref[:, cols]


def side_of(ref, part):
    return ref[:, :, part * HD : (part + 1) * HD].reshape(HALF, HD)


def products(w, ds, q_rows, go_rows, ref):
    dk = jnp.dot(ds[...], q_rows[...], preferred_element_type=F32) * SCALE
    dv = jnp.dot(w[...], go_rows[...], preferred_element_type=F32)
    dq_t = lax.dot_general(
        side_of(ref, 0), ds[...], (((0,), (0,)), ((), ())), preferred_element_type=F32
    )
    return dk.reshape(CHIPS, ROWS, HD), dv.reshape(CHIPS, ROWS, HD), dq_t


def attention_kernel(
    q_rows, go_rows, low_ref, mine_ref, other_ref,
    send_ref, dq_t, w_mine, ds_mine,
    w_other, ds_other, probs, top, total, delta,
):
    core = lax.axis_index("core")
    first = first_position()
    row_pos = first + lax.broadcasted_iota(jnp.int32, (1, ROWS), 1)
    row_low = low_ref[0:1, :]
    groups = [pl.ds(g * GROUP * HD, GROUP * HD) for g in range(HEADS // GROUP)]
    sides = (
        (0, other_ref, 1 - core, w_other, ds_other),
        (1, mine_ref, core, w_mine, ds_mine),
    )

    def fold(values, op):
        return op(values.reshape(values.shape[0] // 8, 8, values.shape[1]), axis=0)

    def against(rows, ref, cols):
        return lax.dot_general(
            rows, ref[cols, :], (((1,), (1,)), ((), ())), preferred_element_type=F32
        )

    def scores_of(ref, side):
        shape = (CHIPS, ROWS, ROWS)
        chip = lax.broadcasted_iota(jnp.int32, shape, 0)
        pos = (2 * chip + side) * ROWS + lax.broadcasted_iota(jnp.int32, shape, 1)
        pos = pos.reshape(HALF, ROWS)
        seen = (pos >= row_low) & (pos <= row_pos)
        seen = jnp.concatenate([seen] * GROUP, axis=1)
        keys = side_of(ref, 0)
        return lambda cols: jnp.where(seen, against(keys, q_rows, cols), HIDDEN_NEG)

    for i, ref, side, _, _ in sides:
        scores = scores_of(ref, side)
        for cols in groups:
            best = fold(scores(cols), jnp.max)
            top[:, cols] = best if i == 0 else jnp.maximum(top[:, cols], best)
    top[0:1, :] = jnp.max(top[...], axis=0, keepdims=True)
    for i, ref, side, _, _ in sides:
        scores = scores_of(ref, side)
        values = side_of(ref, 1)
        for cols in groups:
            pg = against(values, go_rows, cols)
            p = jnp.exp2((scores(cols) - top[0:1, cols]) * EXP2_SCALE)
            probs[pl.ds(i * HALF, HALF), cols] = p
            p_sum, pg_sum = fold(p, jnp.sum), fold(p * pg, jnp.sum)
            total[:, cols] = p_sum if i == 0 else total[:, cols] + p_sum
            delta[:, cols] = pg_sum if i == 0 else delta[:, cols] + pg_sum
    inverse = 1.0 / jnp.sum(total[...], axis=0, keepdims=True)
    total[0:1, :] = inverse
    delta[0:1, :] = jnp.sum(delta[...], axis=0, keepdims=True) * inverse
    for i, ref, _, w_ref, ds_ref in sides:
        values = side_of(ref, 1)
        for cols in groups:
            w = probs[pl.ds(i * HALF, HALF), cols] * total[0:1, cols]
            w_ref[:, cols] = w.astype(BF16)
            pg = against(values, go_rows, cols)
            ds_ref[:, cols] = (w * (pg - delta[0:1, cols])).astype(BF16)
    dk, dv, dq = products(w_other, ds_other, q_rows, go_rows, other_ref)
    send_ref[:, :, :HD] = dk.astype(BF16)
    send_ref[:, :, HD:] = dv.astype(BF16)
    dq_t[...] = dq


def own_kernel(q_rows, go_rows, mine_ref, dq_in, w_mine, ds_mine, keep_ref, dq_t):
    dk, dv, dq = products(w_mine, ds_mine, q_rows, go_rows, mine_ref)
    keep_ref[:, :, :HD] = dk
    keep_ref[:, :, HD:] = dv
    dq_t[...] = dq_in[...] + dq


VMEM = pl.BlockSpec(memory_space=pltpu.VMEM)
SMEM = pl.BlockSpec(memory_space=pltpu.SMEM)


def in_hbm(x):
    return pltpu.with_memory_space_constraint(x, pltpu.HBM)


def limit(mib):
    return pltpu.CompilerParams(vmem_limit_bytes=mib * 1024 * 1024)


def prepare(lengths, owner, query, grad_out):
    hbm = pl.BlockSpec(memory_space=pltpu.HBM)
    wide = HEADS * HD
    return pl.pallas_call(
        prepare_kernel,
        out_shape=(
            jax.ShapeDtypeStruct((wide, HD), BF16),
            jax.ShapeDtypeStruct((wide, HD), BF16),
            jax.ShapeDtypeStruct((8, ROWS), jnp.int32),
            jax.ShapeDtypeStruct((1, TILES), jnp.int32),
        ),
        in_specs=[hbm] * 4,
        out_specs=(VMEM,) * 4,
        scratch_shapes=[
            pltpu.SMEM((1, 8), jnp.int32),
            pltpu.VMEM((1, TILES), jnp.int32),
            pltpu.VMEM((ROWS, wide), BF16),
            pltpu.VMEM((ROWS, wide), BF16),
            pltpu.SemaphoreType.DMA((4,)),
        ],
        compiler_params=limit(8),
        name="prepare_rows",
    )(in_hbm(lengths), in_hbm(owner), in_hbm(query), in_hbm(grad_out))


def attention(q_rows, go_rows, row_low, mine, other):
    wide = HEADS * HD
    half = jax.ShapeDtypeStruct((HALF, wide), BF16)
    return pl.pallas_call(
        attention_kernel,
        out_shape=(
            jax.ShapeDtypeStruct((CHIPS, ROWS, 2 * HD), BF16),
            jax.ShapeDtypeStruct((HD, wide), F32),
            half,
            half,
        ),
        in_specs=[VMEM] * 5,
        out_specs=(VMEM,) * 4,
        scratch_shapes=[
            pltpu.VMEM((HALF, wide), BF16),
            pltpu.VMEM((HALF, wide), BF16),
            pltpu.VMEM((SEQ, wide), F32),
            pltpu.VMEM((8, wide), F32),
            pltpu.VMEM((8, wide), F32),
            pltpu.VMEM((8, wide), F32),
        ],
        compiler_params=limit(24),
        name="attention_backward",
    )(q_rows, go_rows, row_low, mine, other)


def own_keys(q_rows, go_rows, mine, dq_t, w, ds):
    return pl.pallas_call(
        own_kernel,
        out_shape=(
            jax.ShapeDtypeStruct((CHIPS, ROWS, 2 * HD), F32),
            jax.ShapeDtypeStruct((HD, HEADS * HD), F32),
        ),
        in_specs=[VMEM] * 6,
        out_specs=(VMEM, VMEM),
        compiler_params=limit(12),
        name="own_keys",
    )(q_rows, go_rows, mine, dq_t, w, ds)


def low_half(shape, axis):
    return lax.broadcasted_iota(jnp.int32, shape, axis) < 4


def halves(keys):
    rows = keys.T.reshape(PLANE // 2, 2, 8, ROWS)
    even, odd = rows[:, 0], rows[:, 1]
    low = low_half(even.shape, 1)
    first = jnp.where(low, even, pltpu.roll(odd, 4, axis=1))
    second = jnp.where(low, pltpu.roll(even, 4, axis=1), odd)
    return first.reshape(HD // 2, ROWS), second.reshape(HD // 2, ROWS)


def half_tiles(k_t, hidden_ref, out_ref):
    shape = (PLANE // 2, 8, TILE)
    low = low_half(shape, 1)
    for quad in range(TILES // 4):
        hidden = hidden_ref[:, pl.ds(quad * 4 * TILE, 4 * TILE)]
        grad_t = jnp.dot(k_t, hidden, preferred_element_type=F32)
        tiles = [grad_t[:, i * TILE : (i + 1) * TILE].reshape(shape) for i in range(4)]
        evens, odds = [], []
        for even, odd in (tiles[:2], tiles[2:]):
            evens.append(jnp.where(low, even, pltpu.roll(odd, 4, axis=1)))
            odds.append(jnp.where(low, pltpu.roll(even, 4, axis=1), odd))
        rows = pl.ds(quad * 16, 16)
        out_ref[:, 0, rows, :] = jnp.concatenate(evens, axis=1).astype(out_ref.dtype)
        out_ref[:, 1, rows, :] = jnp.concatenate(odds, axis=1).astype(out_ref.dtype)


def weight_send_kernel(parts_ref, hidden_ref, kv_ref, k_ref, out_ref):
    core = lax.axis_index("core")
    low = jnp.sum(parts_ref[...].astype(F32), axis=0).astype(BF16)
    kv_ref[...] = low
    first, second = halves(low[:, :HD].astype(F32))
    k_ref[...] = jnp.where(core == 0, first, second).astype(BF16)
    half_tiles(jnp.where(core == 0, second, first).astype(BF16), hidden_ref, out_ref)


def weight_keep_kernel(k_ref, hidden_ref, dq_t, out_ref, dq_ref):
    half_tiles(k_ref[...], hidden_ref, out_ref)
    for h in range(HEADS):
        cols = pl.ds(h * HD, HD)
        dq_ref[:, cols] = (dq_t[:, cols].T * SCALE).astype(BF16)


def weight_send(parts, hidden):
    return pl.pallas_call(
        weight_send_kernel,
        out_shape=(
            jax.ShapeDtypeStruct((ROWS, 2 * HD), BF16),
            jax.ShapeDtypeStruct((HD // 2, ROWS), BF16),
            jax.ShapeDtypeStruct((PLANE // 2, 2, TILES * 4, TILE), BF16),
        ),
        in_specs=[VMEM, VMEM],
        out_specs=(VMEM, VMEM, VMEM),
        compiler_params=limit(10),
        name="weight_tiles_to_send",
    )(parts, hidden)


def weight_keep(k_t, hidden, dq_t):
    return pl.pallas_call(
        weight_keep_kernel,
        out_shape=(
            jax.ShapeDtypeStruct((PLANE // 2, 2, TILES * 4, TILE), F32),
            jax.ShapeDtypeStruct((ROWS, HEADS * HD), BF16),
        ),
        in_specs=[VMEM] * 3,
        out_specs=(VMEM, VMEM),
        compiler_params=limit(12),
        name="weight_tiles_to_keep",
    )(k_t, hidden, dq_t)


def owner_kernel(place_ref, parts_ref, out_ref, sums, placed):
    rows = TILES * 4
    own = jnp.sum(parts_ref[...].astype(F32), axis=0)
    sums[:rows, :] = own
    sums[rows:, :] = pltpu.roll(own.reshape(rows // 8, 8, TILE), 4, axis=1).reshape(rows, TILE)
    placed[...] = jnp.zeros(placed.shape, F32)
    low = low_half((8, TILE), 0)
    for t in range(TILES):
        place = place_ref[0, t]
        half = place & 1
        at = pl.ds(pl.multiple_of((place >> 1) * 8, 8), 8)
        source = pl.multiple_of((half ^ (t & 1)) * rows + (t // 2) * 8, 8)
        placed[at, :] = jnp.where(low == (half == 0), sums[pl.ds(source, 8), :], placed[at, :])
    out_ref[...] = placed[...].astype(BF16).reshape(out_ref.shape)


def to_owners(place, parts):
    return pl.pallas_call(
        owner_kernel,
        out_shape=jax.ShapeDtypeStruct((N_Z, OWNED, TILE), BF16),
        in_specs=[pl.BlockSpec(memory_space=pltpu.SMEM), VMEM],
        out_specs=VMEM,
        scratch_shapes=[
            pltpu.VMEM((2 * TILES * 4, TILE), F32),
            pltpu.VMEM((N_Z * OWNED, TILE), F32),
        ],
        compiler_params=limit(12),
        name="owner_slots",
    )(place, parts)


def sum_kernel(parts_ref, out_ref):
    gradient = jnp.sum(parts_ref[...].astype(F32), axis=0) * (1.0 / math.sqrt(N_DP * SEQ))
    gradient = gradient.astype(BF16)
    rows = OWNED // N_YL
    some = 2 * N_YH
    for yl in range(N_YL):
        piece = gradient[yl * rows : (yl + 1) * rows]
        piece = jnp.broadcast_to(piece[None], (some, rows, TILE))
        for x in range(N_X):
            at = (x * N_YL + yl) * some
            out_ref[at : at + some] = piece


def owned_sum(parts):
    return pl.pallas_call(
        sum_kernel,
        out_shape=jax.ShapeDtypeStruct((2 * PLANE, OWNED // N_YL, TILE), BF16),
        in_specs=[VMEM],
        out_specs=VMEM,
        compiler_params=limit(8),
        name="owned_sum",
    )(parts)


def factor_kernel(pieces_ref, out_hbm, out_ref, sems):
    pieces = pieces_ref[...].astype(F32)
    low = low_half((PLANE, 8, TILE), 1)
    copies = []
    for two in range(CAP // 2):
        pair = pieces[:, two * 8 : (two + 1) * 8, :].reshape(PLANE, 2, 8, TILE)
        even, odd = pair[:, 0], pair[:, 1]
        both = (
            jnp.where(low, even, pltpu.roll(odd, 4, axis=1)),
            jnp.where(low, pltpu.roll(even, 4, axis=1), odd),
        )
        for i in range(2):
            grad_t = both[i].reshape(TILE, TILE)
            flat = grad_t.astype(BF16)
            flat_t = flat.T
            s = 2 * two + i
            out_ref[s, 0] = jnp.dot(flat_t, flat, preferred_element_type=F32) * (1.0 / TILE)
            out_ref[s, 1] = jnp.dot(flat, flat_t, preferred_element_type=F32) * (1.0 / TILE)
            copy = pltpu.make_async_copy(out_ref.at[s], out_hbm.at[s], sems.at[s])
            copy.start()
            copies.append(copy)
    for copy in copies:
        copy.wait()


def factors_of(pieces):
    return pl.pallas_call(
        factor_kernel,
        out_shape=jax.ShapeDtypeStruct((CAP, 2, TILE, TILE), F32),
        in_specs=[VMEM],
        out_specs=pl.BlockSpec(memory_space=pltpu.HBM),
        scratch_shapes=[
            pltpu.VMEM((CAP, 2, TILE, TILE), F32),
            pltpu.SemaphoreType.DMA((CAP,)),
        ],
        compiler_params=limit(8),
        name="factors",
    )(pieces)


SWAP = ((0, 1), (1, 0))
CHIP_AXES = ("x", "yh")
PLANE_AXES = ("x", "yl", "yh")


def body(hidden_in, query, key_value, grad_out, lengths, owner):
    mine = lax.all_to_all(
        jnp.broadcast_to(key_value, (CHIPS, ROWS, 2 * HD)), CHIP_AXES, 0, 0, tiled=True
    )
    other = lax.ppermute(mine, "core", SWAP)
    q_rows, go_rows, row_low, place = prepare(
        lengths, owner.reshape(1, TILES), query[0], grad_out[0]
    )
    send, dq_t, w, ds = attention(q_rows, go_rows, row_low, mine, other)
    arrived = lax.ppermute(send, "core", SWAP)
    keep, dq_t = own_keys(q_rows, go_rows, mine, dq_t, w, ds)
    dkv = (keep + arrived.astype(F32)).astype(BF16)
    dkv = lax.all_to_all(dkv, CHIP_AXES, 0, 0, tiled=True)
    hidden = hidden_in[0]
    grad_kv, k_t, send = weight_send(dkv, hidden)
    arrived = lax.ppermute(send, "core", SWAP)
    keep, grad_query = weight_keep(k_t, hidden, dq_t)
    wg = (keep + arrived.astype(F32)).astype(BF16).reshape(PLANE, TILES * 4, TILE)
    wg = lax.all_to_all(wg, PLANE_AXES, 0, 0, tiled=True)
    outgoing = to_owners(place, wg)
    incoming = lax.all_to_all(outgoing, "z", 0, 0, tiled=True)
    pieces = lax.all_to_all(owned_sum(incoming), PLANE_AXES + ("core",), 0, 0, tiled=True)
    return grad_query[None], grad_kv[None], factors_of(pieces)[None]


def solution(mesh):
    fine = Mesh(
        mesh.devices.reshape(N_YL, N_Z, N_X, N_YH, 2), ("yl", "z", "x", "yh", "core")
    )
    dp, ctx = ("yl", "z"), ("x", "yh", "core")
    split = P(dp, ctx, None)
    return jax.shard_map(
        body,
        mesh=fine,
        in_specs=(split, split, split, split, P(dp, None), P()),
        out_specs=(split, split, P(dp, None, None, None, None)),
        check_vma=False,
    )
```

```python
import math

import jax
import jax.numpy as jnp
from jax import lax
from jax.experimental import pallas as pl
from jax.experimental.pallas import tpu as pltpu
from jax.sharding import Mesh
from jax.sharding import PartitionSpec as P

HEADS = 8
HD = 128
TILE = 128
ROWS = 128
CHIPS = 8
SEQ = 2048
HALF = SEQ // 2
TILES = 64
CAP = 4
N_DP = 32
MODEL = 8192
N_YL = 2
N_Z = 16
N_X = 4
N_YH = 2
PLANE = N_YL * CHIPS
OWNED = N_YL * CAP * 4
GROUP = 2
HIDDEN_NEG = -1e30
SCALE = 1.0 / math.sqrt(HD)
EXP2_SCALE = SCALE * math.log2(math.e)
F32 = jnp.float32
BF16 = jnp.bfloat16


def first_position():
    chip = N_YH * lax.axis_index("x") + lax.axis_index("yh")
    return (2 * chip + lax.axis_index("core")) * ROWS


def slot_table(owner):
    across = jnp.broadcast_to(owner.astype(F32), (TILES, TILES))
    earlier = lax.broadcasted_iota(jnp.int32, (TILES, TILES), 0) < lax.broadcasted_iota(
        jnp.int32, (TILES, TILES), 1
    )
    same = jnp.where((across.T == across) & earlier, 1.0, 0.0)
    slot = jnp.sum(same, axis=0, keepdims=True).astype(jnp.int32)
    return ((owner & (N_Z - 1)) * N_YL + (owner >> 4)) * CAP + slot


def prepare_kernel(
    lengths_hbm, owner_hbm, q_hbm, go_hbm,
    q_rows, go_rows, low_ref, place_ref,
    lengths_ref, owner_ref, q_ref, go_ref, sems,
):
    copies = [
        pltpu.make_async_copy(lengths_hbm, lengths_ref, sems.at[0]),
        pltpu.make_async_copy(owner_hbm, owner_ref, sems.at[1]),
        pltpu.make_async_copy(q_hbm, q_ref, sems.at[2]),
        pltpu.make_async_copy(go_hbm, go_ref, sems.at[3]),
    ]
    for copy in copies:
        copy.start()
    first = first_position()
    row_pos = first + lax.broadcasted_iota(jnp.int32, low_ref.shape, 1)
    row_low = jnp.zeros(low_ref.shape, jnp.int32)
    end = jnp.int32(0)
    copies[0].wait()
    for d in range(lengths_ref.shape[1]):
        end = end + lengths_ref[0, d]
        row_low = jnp.maximum(row_low, jnp.where(row_pos >= end, end, 0))
    low_ref[...] = row_low
    copies[1].wait()
    place_ref[...] = slot_table(owner_ref[...])
    for copy, rows, ref in ((copies[2], q_rows, q_ref), (copies[3], go_rows, go_ref)):
        copy.wait()
        for h in range(HEADS):
            cols = pl.ds(h * HD, HD)
            rows[cols, :] = ref[:, cols]


def side_of(ref, part):
    return ref[:, :, part * HD : (part + 1) * HD].reshape(HALF, HD)


def products(w, ds, q_rows, go_rows):
    dk = jnp.dot(ds[...], q_rows[...], preferred_element_type=F32) * SCALE
    dv = jnp.dot(w[...], go_rows[...], preferred_element_type=F32)
    return dk.reshape(CHIPS, ROWS, HD), dv.reshape(CHIPS, ROWS, HD)


def query_part(ds, ref):
    return lax.dot_general(
        side_of(ref, 0), ds[...], (((0,), (0,)), ((), ())), preferred_element_type=F32
    )


def attention_kernel(
    q_rows, go_rows, low_ref, mine_ref, other_ref,
    send_ref, w_mine, ds_mine, ds_other,
    w_other, probs, top, total, delta,
):
    core = lax.axis_index("core")
    first = first_position()
    row_pos = first + lax.broadcasted_iota(jnp.int32, (1, ROWS), 1)
    row_low = low_ref[0:1, :]
    groups = [pl.ds(g * GROUP * HD, GROUP * HD) for g in range(HEADS // GROUP)]
    sides = (
        (0, other_ref, 1 - core, w_other, ds_other),
        (1, mine_ref, core, w_mine, ds_mine),
    )

    def fold(values, op):
        return op(values.reshape(values.shape[0] // 8, 8, values.shape[1]), axis=0)

    def against(rows, ref, cols):
        return lax.dot_general(
            rows, ref[cols, :], (((1,), (1,)), ((), ())), preferred_element_type=F32
        )

    def scores_of(ref, side):
        shape = (CHIPS, ROWS, ROWS)
        chip = lax.broadcasted_iota(jnp.int32, shape, 0)
        pos = (2 * chip + side) * ROWS + lax.broadcasted_iota(jnp.int32, shape, 1)
        pos = pos.reshape(HALF, ROWS)
        seen = (pos >= row_low) & (pos <= row_pos)
        seen = jnp.concatenate([seen] * GROUP, axis=1)
        keys = side_of(ref, 0)
        return lambda cols: jnp.where(seen, against(keys, q_rows, cols), HIDDEN_NEG)

    for i, ref, side, _, _ in sides:
        scores = scores_of(ref, side)
        for cols in groups:
            best = fold(scores(cols), jnp.max)
            top[:, cols] = best if i == 0 else jnp.maximum(top[:, cols], best)
    top[0:1, :] = jnp.max(top[...], axis=0, keepdims=True)
    for i, ref, side, _, _ in sides:
        scores = scores_of(ref, side)
        values = side_of(ref, 1)
        for cols in groups:
            pg = against(values, go_rows, cols)
            p = jnp.exp2((scores(cols) - top[0:1, cols]) * EXP2_SCALE)
            probs[pl.ds(i * HALF, HALF), cols] = p
            p_sum, pg_sum = fold(p, jnp.sum), fold(p * pg, jnp.sum)
            total[:, cols] = p_sum if i == 0 else total[:, cols] + p_sum
            delta[:, cols] = pg_sum if i == 0 else delta[:, cols] + pg_sum
    inverse = 1.0 / jnp.sum(total[...], axis=0, keepdims=True)
    total[0:1, :] = inverse
    delta[0:1, :] = jnp.sum(delta[...], axis=0, keepdims=True) * inverse
    for i, ref, _, w_ref, ds_ref in sides:
        values = side_of(ref, 1)
        for cols in groups:
            w = probs[pl.ds(i * HALF, HALF), cols] * total[0:1, cols]
            w_ref[:, cols] = w.astype(BF16)
            pg = against(values, go_rows, cols)
            ds_ref[:, cols] = (w * (pg - delta[0:1, cols])).astype(BF16)
    dk, dv = products(w_other, ds_other, q_rows, go_rows)
    send_ref[:, :, :HD] = dk.astype(BF16)
    send_ref[:, :, HD:] = dv.astype(BF16)


def own_kernel(q_rows, go_rows, mine_ref, w_mine, ds_mine, keep_ref, dq_t):
    dk, dv = products(w_mine, ds_mine, q_rows, go_rows)
    keep_ref[:, :, :HD] = dk
    keep_ref[:, :, HD:] = dv
    dq_t[...] = query_part(ds_mine, mine_ref)


VMEM = pl.BlockSpec(memory_space=pltpu.VMEM)
SMEM = pl.BlockSpec(memory_space=pltpu.SMEM)


def in_hbm(x):
    return pltpu.with_memory_space_constraint(x, pltpu.HBM)


def limit(mib):
    return pltpu.CompilerParams(vmem_limit_bytes=mib * 1024 * 1024)


def prepare(lengths, owner, query, grad_out):
    hbm = pl.BlockSpec(memory_space=pltpu.HBM)
    wide = HEADS * HD
    return pl.pallas_call(
        prepare_kernel,
        out_shape=(
            jax.ShapeDtypeStruct((wide, HD), BF16),
            jax.ShapeDtypeStruct((wide, HD), BF16),
            jax.ShapeDtypeStruct((8, ROWS), jnp.int32),
            jax.ShapeDtypeStruct((1, TILES), jnp.int32),
        ),
        in_specs=[hbm] * 4,
        out_specs=(VMEM,) * 4,
        scratch_shapes=[
            pltpu.SMEM((1, 8), jnp.int32),
            pltpu.VMEM((1, TILES), jnp.int32),
            pltpu.VMEM((ROWS, wide), BF16),
            pltpu.VMEM((ROWS, wide), BF16),
            pltpu.SemaphoreType.DMA((4,)),
        ],
        compiler_params=limit(8),
        name="prepare_rows",
    )(in_hbm(lengths), in_hbm(owner), in_hbm(query), in_hbm(grad_out))


def attention(q_rows, go_rows, row_low, mine, other):
    wide = HEADS * HD
    half = jax.ShapeDtypeStruct((HALF, wide), BF16)
    return pl.pallas_call(
        attention_kernel,
        out_shape=(
            jax.ShapeDtypeStruct((CHIPS, ROWS, 2 * HD), BF16),
            half,
            half,
            half,
        ),
        in_specs=[VMEM] * 5,
        out_specs=(VMEM,) * 4,
        scratch_shapes=[
            pltpu.VMEM((HALF, wide), BF16),
            pltpu.VMEM((SEQ, wide), F32),
            pltpu.VMEM((8, wide), F32),
            pltpu.VMEM((8, wide), F32),
            pltpu.VMEM((8, wide), F32),
        ],
        compiler_params=limit(24),
        name="attention_backward",
    )(q_rows, go_rows, row_low, mine, other)


def own_keys(q_rows, go_rows, mine, w, ds):
    return pl.pallas_call(
        own_kernel,
        out_shape=(
            jax.ShapeDtypeStruct((CHIPS, ROWS, 2 * HD), F32),
            jax.ShapeDtypeStruct((HD, HEADS * HD), F32),
        ),
        in_specs=[VMEM] * 5,
        out_specs=(VMEM, VMEM),
        compiler_params=limit(12),
        name="own_keys",
    )(q_rows, go_rows, mine, w, ds)


def low_half(shape, axis):
    return lax.broadcasted_iota(jnp.int32, shape, axis) < 4


def halves(keys):
    rows = keys.T.reshape(PLANE // 2, 2, 8, ROWS)
    even, odd = rows[:, 0], rows[:, 1]
    low = low_half(even.shape, 1)
    first = jnp.where(low, even, pltpu.roll(odd, 4, axis=1))
    second = jnp.where(low, pltpu.roll(even, 4, axis=1), odd)
    return first.reshape(HD // 2, ROWS), second.reshape(HD // 2, ROWS)


def half_tiles(k_t, hidden_ref, out_ref):
    shape = (PLANE // 2, 8, TILE)
    low = low_half(shape, 1)
    for quad in range(TILES // 4):
        hidden = hidden_ref[:, pl.ds(quad * 4 * TILE, 4 * TILE)]
        grad_t = jnp.dot(k_t, hidden, preferred_element_type=F32)
        tiles = [grad_t[:, i * TILE : (i + 1) * TILE].reshape(shape) for i in range(4)]
        evens, odds = [], []
        for even, odd in (tiles[:2], tiles[2:]):
            evens.append(jnp.where(low, even, pltpu.roll(odd, 4, axis=1)))
            odds.append(jnp.where(low, pltpu.roll(even, 4, axis=1), odd))
        rows = pl.ds(quad * 16, 16)
        out_ref[:, 0, rows, :] = jnp.concatenate(evens, axis=1).astype(out_ref.dtype)
        out_ref[:, 1, rows, :] = jnp.concatenate(odds, axis=1).astype(out_ref.dtype)


def position_sums(parts_ref, part):
    return jnp.sum(parts_ref[:, :, part * HD : (part + 1) * HD].astype(F32), axis=0).astype(BF16)


def weight_send_kernel(parts_ref, hidden_ref, low_ref, k_ref, out_ref):
    core = lax.axis_index("core")
    low = position_sums(parts_ref, 0)
    low_ref[...] = low
    first, second = halves(low.astype(F32))
    k_ref[...] = jnp.where(core == 0, first, second).astype(BF16)
    half_tiles(jnp.where(core == 0, second, first).astype(BF16), hidden_ref, out_ref)


def weight_keep_kernel(
    k_ref, hidden_ref, dq_t, ds_other, other_ref, low_ref, parts_ref, out_ref, dq_ref, kv_ref, dq_all
):
    kv_ref[:, :HD] = low_ref[...]
    kv_ref[:, HD:] = position_sums(parts_ref, 1)
    half_tiles(k_ref[...], hidden_ref, out_ref)
    dq_all[...] = dq_t[...] + query_part(ds_other, other_ref)
    for h in range(HEADS):
        cols = pl.ds(h * HD, HD)
        dq_ref[:, cols] = (dq_all[:, cols].T * SCALE).astype(BF16)


def weight_send(parts, hidden):
    return pl.pallas_call(
        weight_send_kernel,
        out_shape=(
            jax.ShapeDtypeStruct((ROWS, HD), BF16),
            jax.ShapeDtypeStruct((HD // 2, ROWS), BF16),
            jax.ShapeDtypeStruct((PLANE // 2, 2, TILES * 4, TILE), BF16),
        ),
        in_specs=[VMEM, VMEM],
        out_specs=(VMEM, VMEM, VMEM),
        compiler_params=limit(10),
        name="weight_tiles_to_send",
    )(parts, hidden)


def weight_keep(k_t, hidden, dq_t, ds_other, other, low, parts):
    return pl.pallas_call(
        weight_keep_kernel,
        out_shape=(
            jax.ShapeDtypeStruct((PLANE // 2, 2, TILES * 4, TILE), F32),
            jax.ShapeDtypeStruct((ROWS, HEADS * HD), BF16),
            jax.ShapeDtypeStruct((ROWS, 2 * HD), BF16),
        ),
        in_specs=[VMEM] * 7,
        out_specs=(VMEM,) * 3,
        scratch_shapes=[pltpu.VMEM((HD, HEADS * HD), F32)],
        compiler_params=limit(12),
        name="weight_tiles_to_keep",
    )(k_t, hidden, dq_t, ds_other, other, low, parts)


def owner_kernel(place_ref, parts_ref, out_ref, sums, placed):
    rows = TILES * 4
    own = jnp.sum(parts_ref[...].astype(F32), axis=0)
    sums[:rows, :] = own
    sums[rows:, :] = pltpu.roll(own.reshape(rows // 8, 8, TILE), 4, axis=1).reshape(rows, TILE)
    placed[...] = jnp.zeros(placed.shape, F32)
    low = low_half((8, TILE), 0)
    for t in range(TILES):
        place = place_ref[0, t]
        half = place & 1
        at = pl.ds(pl.multiple_of((place >> 1) * 8, 8), 8)
        source = pl.multiple_of((half ^ (t & 1)) * rows + (t // 2) * 8, 8)
        placed[at, :] = jnp.where(low == (half == 0), sums[pl.ds(source, 8), :], placed[at, :])
    out_ref[...] = placed[...].astype(BF16).reshape(out_ref.shape)


def to_owners(place, parts):
    return pl.pallas_call(
        owner_kernel,
        out_shape=jax.ShapeDtypeStruct((N_Z, OWNED, TILE), BF16),
        in_specs=[pl.BlockSpec(memory_space=pltpu.SMEM), VMEM],
        out_specs=VMEM,
        scratch_shapes=[
            pltpu.VMEM((2 * TILES * 4, TILE), F32),
            pltpu.VMEM((N_Z * OWNED, TILE), F32),
        ],
        compiler_params=limit(12),
        name="owner_slots",
    )(place, parts)


def sum_kernel(parts_ref, out_ref):
    gradient = jnp.sum(parts_ref[...].astype(F32), axis=0) * (1.0 / math.sqrt(N_DP * SEQ))
    gradient = gradient.astype(BF16)
    rows = OWNED // N_YL
    some = 2 * N_YH
    for yl in range(N_YL):
        piece = gradient[yl * rows : (yl + 1) * rows]
        piece = jnp.broadcast_to(piece[None], (some, rows, TILE))
        for x in range(N_X):
            at = (x * N_YL + yl) * some
            out_ref[at : at + some] = piece


def owned_sum(parts):
    return pl.pallas_call(
        sum_kernel,
        out_shape=jax.ShapeDtypeStruct((2 * PLANE, OWNED // N_YL, TILE), BF16),
        in_specs=[VMEM],
        out_specs=VMEM,
        compiler_params=limit(8),
        name="owned_sum",
    )(parts)


def factor_kernel(pieces_ref, out_hbm, out_ref, sems):
    pieces = pieces_ref[...].astype(F32)
    low = low_half((PLANE, 8, TILE), 1)
    copies = []
    for two in range(CAP // 2):
        pair = pieces[:, two * 8 : (two + 1) * 8, :].reshape(PLANE, 2, 8, TILE)
        even, odd = pair[:, 0], pair[:, 1]
        both = (
            jnp.where(low, even, pltpu.roll(odd, 4, axis=1)),
            jnp.where(low, pltpu.roll(even, 4, axis=1), odd),
        )
        for i in range(2):
            grad_t = both[i].reshape(TILE, TILE)
            flat = grad_t.astype(BF16)
            flat_t = flat.T
            s = 2 * two + i
            out_ref[s, 0] = jnp.dot(flat_t, flat, preferred_element_type=F32) * (1.0 / TILE)
            out_ref[s, 1] = jnp.dot(flat, flat_t, preferred_element_type=F32) * (1.0 / TILE)
            copy = pltpu.make_async_copy(out_ref.at[s], out_hbm.at[s], sems.at[s])
            copy.start()
            copies.append(copy)
    for copy in copies:
        copy.wait()


def factors_of(pieces):
    return pl.pallas_call(
        factor_kernel,
        out_shape=jax.ShapeDtypeStruct((CAP, 2, TILE, TILE), F32),
        in_specs=[VMEM],
        out_specs=pl.BlockSpec(memory_space=pltpu.HBM),
        scratch_shapes=[
            pltpu.VMEM((CAP, 2, TILE, TILE), F32),
            pltpu.SemaphoreType.DMA((CAP,)),
        ],
        compiler_params=limit(8),
        name="factors",
    )(pieces)


SWAP = ((0, 1), (1, 0))
CHIP_AXES = ("x", "yh")
PLANE_AXES = ("x", "yl", "yh")


def body(hidden_in, query, key_value, grad_out, lengths, owner):
    mine = lax.all_to_all(
        jnp.broadcast_to(key_value, (CHIPS, ROWS, 2 * HD)), CHIP_AXES, 0, 0, tiled=True
    )
    other = lax.ppermute(mine, "core", SWAP)
    q_rows, go_rows, row_low, place = prepare(
        lengths, owner.reshape(1, TILES), query[0], grad_out[0]
    )
    send, w, ds, ds_other = attention(q_rows, go_rows, row_low, mine, other)
    arrived = lax.ppermute(send, "core", SWAP)
    keep, dq_t = own_keys(q_rows, go_rows, mine, w, ds)
    dkv = (keep + arrived.astype(F32)).astype(BF16)
    dkv = lax.all_to_all(dkv, CHIP_AXES, 0, 0, tiled=True)
    hidden = hidden_in[0]
    low, k_t, send = weight_send(dkv, hidden)
    arrived = lax.ppermute(send, "core", SWAP)
    keep, grad_query, grad_kv = weight_keep(k_t, hidden, dq_t, ds_other, other, low, dkv)
    wg = (keep + arrived.astype(F32)).astype(BF16).reshape(PLANE, TILES * 4, TILE)
    wg = lax.all_to_all(wg, PLANE_AXES, 0, 0, tiled=True)
    outgoing = to_owners(place, wg)
    incoming = lax.all_to_all(outgoing, "z", 0, 0, tiled=True)
    pieces = lax.all_to_all(owned_sum(incoming), PLANE_AXES + ("core",), 0, 0, tiled=True)
    return grad_query[None], grad_kv[None], factors_of(pieces)[None]


def solution(mesh):
    fine = Mesh(
        mesh.devices.reshape(N_YL, N_Z, N_X, N_YH, 2), ("yl", "z", "x", "yh", "core")
    )
    dp, ctx = ("yl", "z"), ("x", "yh", "core")
    split = P(dp, ctx, None)
    return jax.shard_map(
        body,
        mesh=fine,
        in_specs=(split, split, split, split, P(dp, None), P()),
        out_specs=(split, split, P(dp, None, None, None, None)),
        check_vma=False,
    )
```

```python
import math

import jax
import jax.numpy as jnp
from jax import lax
from jax.experimental import pallas as pl
from jax.experimental.pallas import tpu as pltpu
from jax.sharding import Mesh
from jax.sharding import PartitionSpec as P

HEADS = 8
HD = 128
TILE = 128
ROWS = 128
CHIPS = 8
SEQ = 2048
HALF = SEQ // 2
TILES = 64
CAP = 4
N_DP = 32
MODEL = 8192
N_YL = 2
N_Z = 16
N_X = 4
N_YH = 2
PLANE = N_YL * CHIPS
OWNED = N_YL * CAP * 4
GROUP = 2
HIDDEN_NEG = -1e30
SCALE = 1.0 / math.sqrt(HD)
EXP2_SCALE = SCALE * math.log2(math.e)
F32 = jnp.float32
BF16 = jnp.bfloat16


def first_position():
    chip = N_YH * lax.axis_index("x") + lax.axis_index("yh")
    return (2 * chip + lax.axis_index("core")) * ROWS


def slot_table(owner):
    across = jnp.broadcast_to(owner.astype(F32), (TILES, TILES))
    earlier = lax.broadcasted_iota(jnp.int32, (TILES, TILES), 0) < lax.broadcasted_iota(
        jnp.int32, (TILES, TILES), 1
    )
    same = jnp.where((across.T == across) & earlier, 1.0, 0.0)
    slot = jnp.sum(same, axis=0, keepdims=True).astype(jnp.int32)
    return ((owner & (N_Z - 1)) * N_YL + (owner >> 4)) * CAP + slot


def prepare_kernel(
    lengths_hbm, owner_hbm, q_hbm, go_hbm,
    q_rows, go_rows, low_ref, place_ref,
    lengths_ref, owner_ref, q_ref, go_ref, sems,
):
    copies = [
        pltpu.make_async_copy(lengths_hbm, lengths_ref, sems.at[0]),
        pltpu.make_async_copy(owner_hbm, owner_ref, sems.at[1]),
        pltpu.make_async_copy(q_hbm, q_ref, sems.at[2]),
        pltpu.make_async_copy(go_hbm, go_ref, sems.at[3]),
    ]
    for copy in copies:
        copy.start()
    first = first_position()
    row_pos = first + lax.broadcasted_iota(jnp.int32, low_ref.shape, 1)
    row_low = jnp.zeros(low_ref.shape, jnp.int32)
    end = jnp.int32(0)
    copies[0].wait()
    for d in range(lengths_ref.shape[1]):
        end = end + lengths_ref[0, d]
        row_low = jnp.maximum(row_low, jnp.where(row_pos >= end, end, 0))
    low_ref[...] = row_low
    copies[1].wait()
    place_ref[...] = slot_table(owner_ref[...])
    for copy, rows, ref in ((copies[2], q_rows, q_ref), (copies[3], go_rows, go_ref)):
        copy.wait()
        for h in range(HEADS):
            cols = pl.ds(h * HD, HD)
            rows[cols, :] = ref[:, cols]


def side_of(ref, part):
    return ref[:, :, part * HD : (part + 1) * HD].reshape(HALF, HD)


def products(w, ds, q_rows, go_rows):
    dk = jnp.dot(ds[...], q_rows[...], preferred_element_type=F32) * SCALE
    dv = jnp.dot(w[...], go_rows[...], preferred_element_type=F32)
    return dk.reshape(CHIPS, ROWS, HD), dv.reshape(CHIPS, ROWS, HD)


def query_part(ds, ref):
    return lax.dot_general(
        side_of(ref, 0), ds[...], (((0,), (0,)), ((), ())), preferred_element_type=F32
    )


def attention_kernel(
    q_rows, go_rows, low_ref, mine_ref, other_ref,
    send_ref, w_mine, ds_mine, ds_other,
    w_other, probs, top, total, delta,
):
    core = lax.axis_index("core")
    first = first_position()
    row_pos = first + lax.broadcasted_iota(jnp.int32, (1, ROWS), 1)
    row_low = low_ref[0:1, :]
    groups = [pl.ds(g * GROUP * HD, GROUP * HD) for g in range(HEADS // GROUP)]
    sides = (
        (0, other_ref, 1 - core, w_other, ds_other),
        (1, mine_ref, core, w_mine, ds_mine),
    )

    def fold(values, op):
        return op(values.reshape(values.shape[0] // 8, 8, values.shape[1]), axis=0)

    def against(rows, ref, cols):
        return lax.dot_general(
            rows, ref[cols, :], (((1,), (1,)), ((), ())), preferred_element_type=F32
        )

    def scores_of(ref, side):
        shape = (CHIPS, ROWS, ROWS)
        chip = lax.broadcasted_iota(jnp.int32, shape, 0)
        pos = (2 * chip + side) * ROWS + lax.broadcasted_iota(jnp.int32, shape, 1)
        pos = pos.reshape(HALF, ROWS)
        seen = (pos >= row_low) & (pos <= row_pos)
        seen = jnp.concatenate([seen] * GROUP, axis=1)
        keys = side_of(ref, 0)
        return lambda cols: jnp.where(seen, against(keys, q_rows, cols), HIDDEN_NEG)

    for i, ref, side, _, _ in sides:
        scores = scores_of(ref, side)
        for cols in groups:
            best = fold(scores(cols), jnp.max)
            top[:, cols] = best if i == 0 else jnp.maximum(top[:, cols], best)
    top[0:1, :] = jnp.max(top[...], axis=0, keepdims=True)
    for i, ref, side, _, _ in sides:
        scores = scores_of(ref, side)
        values = side_of(ref, 1)
        for cols in groups:
            pg = against(values, go_rows, cols)
            p = jnp.exp2((scores(cols) - top[0:1, cols]) * EXP2_SCALE)
            probs[pl.ds(i * HALF, HALF), cols] = p
            p_sum, pg_sum = fold(p, jnp.sum), fold(p * pg, jnp.sum)
            total[:, cols] = p_sum if i == 0 else total[:, cols] + p_sum
            delta[:, cols] = pg_sum if i == 0 else delta[:, cols] + pg_sum
    inverse = 1.0 / jnp.sum(total[...], axis=0, keepdims=True)
    total[0:1, :] = inverse
    delta[0:1, :] = jnp.sum(delta[...], axis=0, keepdims=True) * inverse
    for i, ref, _, w_ref, ds_ref in sides:
        values = side_of(ref, 1)
        for cols in groups:
            w = probs[pl.ds(i * HALF, HALF), cols] * total[0:1, cols]
            w_ref[:, cols] = w.astype(BF16)
            pg = against(values, go_rows, cols)
            ds_ref[:, cols] = (w * (pg - delta[0:1, cols])).astype(BF16)
    dk, dv = products(w_other, ds_other, q_rows, go_rows)
    send_ref[:, :, :HD] = dk.astype(BF16)
    send_ref[:, :, HD:] = dv.astype(BF16)


def own_kernel(q_rows, go_rows, mine_ref, w_mine, ds_mine, keep_ref, dq_t):
    dk, dv = products(w_mine, ds_mine, q_rows, go_rows)
    keep_ref[:, :, :HD] = dk
    keep_ref[:, :, HD:] = dv
    dq_t[...] = query_part(ds_mine, mine_ref)


VMEM = pl.BlockSpec(memory_space=pltpu.VMEM)
SMEM = pl.BlockSpec(memory_space=pltpu.SMEM)


def in_hbm(x):
    return pltpu.with_memory_space_constraint(x, pltpu.HBM)


def limit(mib):
    return pltpu.CompilerParams(vmem_limit_bytes=mib * 1024 * 1024)


def prepare(lengths, owner, query, grad_out):
    hbm = pl.BlockSpec(memory_space=pltpu.HBM)
    wide = HEADS * HD
    return pl.pallas_call(
        prepare_kernel,
        out_shape=(
            jax.ShapeDtypeStruct((wide, HD), BF16),
            jax.ShapeDtypeStruct((wide, HD), BF16),
            jax.ShapeDtypeStruct((8, ROWS), jnp.int32),
            jax.ShapeDtypeStruct((1, TILES), jnp.int32),
        ),
        in_specs=[hbm] * 4,
        out_specs=(VMEM,) * 4,
        scratch_shapes=[
            pltpu.SMEM((1, 8), jnp.int32),
            pltpu.VMEM((1, TILES), jnp.int32),
            pltpu.VMEM((ROWS, wide), BF16),
            pltpu.VMEM((ROWS, wide), BF16),
            pltpu.SemaphoreType.DMA((4,)),
        ],
        compiler_params=limit(8),
        name="prepare_rows",
    )(in_hbm(lengths), in_hbm(owner), in_hbm(query), in_hbm(grad_out))


def attention(q_rows, go_rows, row_low, mine, other):
    wide = HEADS * HD
    half = jax.ShapeDtypeStruct((HALF, wide), BF16)
    return pl.pallas_call(
        attention_kernel,
        out_shape=(
            jax.ShapeDtypeStruct((CHIPS, ROWS, 2 * HD), BF16),
            half,
            half,
            half,
        ),
        in_specs=[VMEM] * 5,
        out_specs=(VMEM,) * 4,
        scratch_shapes=[
            pltpu.VMEM((HALF, wide), BF16),
            pltpu.VMEM((SEQ, wide), F32),
            pltpu.VMEM((8, wide), F32),
            pltpu.VMEM((8, wide), F32),
            pltpu.VMEM((8, wide), F32),
        ],
        compiler_params=limit(24),
        name="attention_backward",
    )(q_rows, go_rows, row_low, mine, other)


def own_keys(q_rows, go_rows, mine, w, ds):
    return pl.pallas_call(
        own_kernel,
        out_shape=(
            jax.ShapeDtypeStruct((CHIPS, ROWS, 2 * HD), F32),
            jax.ShapeDtypeStruct((HD, HEADS * HD), F32),
        ),
        in_specs=[VMEM] * 5,
        out_specs=(VMEM, VMEM),
        compiler_params=limit(12),
        name="own_keys",
    )(q_rows, go_rows, mine, w, ds)


def low_half(shape, axis):
    return lax.broadcasted_iota(jnp.int32, shape, axis) < 4


def halves(keys):
    rows = keys.T.reshape(PLANE // 2, 2, 8, ROWS)
    even, odd = rows[:, 0], rows[:, 1]
    low = low_half(even.shape, 1)
    first = jnp.where(low, even, pltpu.roll(odd, 4, axis=1))
    second = jnp.where(low, pltpu.roll(even, 4, axis=1), odd)
    return first.reshape(HD // 2, ROWS), second.reshape(HD // 2, ROWS)


def half_tiles(k_t, hidden_ref, out_ref):
    shape = (PLANE // 2, 8, TILE)
    low = low_half(shape, 1)
    for quad in range(TILES // 4):
        hidden = hidden_ref[:, pl.ds(quad * 4 * TILE, 4 * TILE)]
        grad_t = jnp.dot(k_t, hidden, preferred_element_type=F32)
        tiles = [grad_t[:, i * TILE : (i + 1) * TILE].reshape(shape) for i in range(4)]
        evens, odds = [], []
        for even, odd in (tiles[:2], tiles[2:]):
            evens.append(jnp.where(low, even, pltpu.roll(odd, 4, axis=1)))
            odds.append(jnp.where(low, pltpu.roll(even, 4, axis=1), odd))
        rows = pl.ds(quad * 16, 16)
        out_ref[:, 0, rows, :] = jnp.concatenate(evens, axis=1).astype(out_ref.dtype)
        out_ref[:, 1, rows, :] = jnp.concatenate(odds, axis=1).astype(out_ref.dtype)


def position_sums(parts_ref, part):
    return jnp.sum(parts_ref[:, :, part * HD : (part + 1) * HD].astype(F32), axis=0).astype(BF16)


def weight_send_kernel(parts_ref, hidden_ref, low_ref, k_ref, out_ref):
    core = lax.axis_index("core")
    low = position_sums(parts_ref, 0)
    low_ref[...] = low
    first, second = halves(low.astype(F32))
    k_ref[...] = jnp.where(core == 0, first, second).astype(BF16)
    half_tiles(jnp.where(core == 0, second, first).astype(BF16), hidden_ref, out_ref)


def weight_keep_kernel(
    k_ref, hidden_ref, dq_t, ds_other, other_ref, low_ref, parts_ref, out_ref, dq_ref, kv_ref, dq_all
):
    kv_ref[:, :HD] = low_ref[...]
    kv_ref[:, HD:] = position_sums(parts_ref, 1)
    half_tiles(k_ref[...], hidden_ref, out_ref)
    dq_all[...] = dq_t[...] + query_part(ds_other, other_ref)
    for h in range(HEADS):
        cols = pl.ds(h * HD, HD)
        dq_ref[:, cols] = (dq_all[:, cols].T * SCALE).astype(BF16)


def weight_send(parts, hidden):
    return pl.pallas_call(
        weight_send_kernel,
        out_shape=(
            jax.ShapeDtypeStruct((ROWS, HD), BF16),
            jax.ShapeDtypeStruct((HD // 2, ROWS), BF16),
            jax.ShapeDtypeStruct((PLANE // 2, 2, TILES * 4, TILE), BF16),
        ),
        in_specs=[VMEM, VMEM],
        out_specs=(VMEM, VMEM, VMEM),
        compiler_params=limit(10),
        name="weight_tiles_to_send",
    )(parts, hidden)


def weight_keep(k_t, hidden, dq_t, ds_other, other, low, parts):
    return pl.pallas_call(
        weight_keep_kernel,
        out_shape=(
            jax.ShapeDtypeStruct((PLANE // 2, 2, TILES * 4, TILE), F32),
            jax.ShapeDtypeStruct((ROWS, HEADS * HD), BF16),
            jax.ShapeDtypeStruct((ROWS, 2 * HD), BF16),
        ),
        in_specs=[VMEM] * 7,
        out_specs=(VMEM,) * 3,
        scratch_shapes=[pltpu.VMEM((HD, HEADS * HD), F32)],
        compiler_params=limit(12),
        name="weight_tiles_to_keep",
    )(k_t, hidden, dq_t, ds_other, other, low, parts)


def owner_kernel(place_ref, parts_ref, out_ref, sums, placed):
    rows = TILES * 4
    own = jnp.sum(parts_ref[...].astype(F32), axis=0)
    sums[:rows, :] = own
    sums[rows:, :] = pltpu.roll(own.reshape(rows // 8, 8, TILE), 4, axis=1).reshape(rows, TILE)
    placed[...] = jnp.zeros(placed.shape, F32)
    for t in range(TILES):
        place = place_ref[0, t]
        at = pl.ds(pl.multiple_of(place * 8, 8), 8)
        source = pl.multiple_of(((place & 1) ^ (t & 1)) * rows + (t // 2) * 8, 8)
        placed[at, :] = sums[pl.ds(source, 8), :]
    pairs = placed[...].reshape(N_DP * CAP // 2, 2, 8, TILE)
    low = low_half((N_DP * CAP // 2, 8, TILE), 1)
    merged = jnp.where(low, pairs[:, 0], pairs[:, 1])
    out_ref[...] = merged.reshape(out_ref.shape).astype(BF16)


def to_owners(place, parts):
    return pl.pallas_call(
        owner_kernel,
        out_shape=jax.ShapeDtypeStruct((N_Z, OWNED, TILE), BF16),
        in_specs=[pl.BlockSpec(memory_space=pltpu.SMEM), VMEM],
        out_specs=VMEM,
        scratch_shapes=[
            pltpu.VMEM((2 * TILES * 4, TILE), F32),
            pltpu.VMEM((N_DP * CAP * 8, TILE), F32),
        ],
        compiler_params=limit(12),
        name="owner_slots",
    )(place, parts)


def sum_kernel(parts_ref, out_ref):
    gradient = jnp.sum(parts_ref[...].astype(F32), axis=0) * (1.0 / math.sqrt(N_DP * SEQ))
    gradient = gradient.astype(BF16)
    rows = OWNED // N_YL
    some = 2 * N_YH
    for yl in range(N_YL):
        piece = gradient[yl * rows : (yl + 1) * rows]
        piece = jnp.broadcast_to(piece[None], (some, rows, TILE))
        for x in range(N_X):
            at = (x * N_YL + yl) * some
            out_ref[at : at + some] = piece


def owned_sum(parts):
    return pl.pallas_call(
        sum_kernel,
        out_shape=jax.ShapeDtypeStruct((2 * PLANE, OWNED // N_YL, TILE), BF16),
        in_specs=[VMEM],
        out_specs=VMEM,
        compiler_params=limit(8),
        name="owned_sum",
    )(parts)


def factor_kernel(pieces_ref, out_hbm, out_ref, sems):
    pieces = pieces_ref[...].astype(F32)
    low = low_half((PLANE, 8, TILE), 1)
    copies = []
    for two in range(CAP // 2):
        pair = pieces[:, two * 8 : (two + 1) * 8, :].reshape(PLANE, 2, 8, TILE)
        even, odd = pair[:, 0], pair[:, 1]
        both = (
            jnp.where(low, even, pltpu.roll(odd, 4, axis=1)),
            jnp.where(low, pltpu.roll(even, 4, axis=1), odd),
        )
        for i in range(2):
            grad_t = both[i].reshape(TILE, TILE)
            flat = grad_t.astype(BF16)
            flat_t = flat.T
            s = 2 * two + i
            out_ref[s, 0] = jnp.dot(flat_t, flat, preferred_element_type=F32) * (1.0 / TILE)
            out_ref[s, 1] = jnp.dot(flat, flat_t, preferred_element_type=F32) * (1.0 / TILE)
            copy = pltpu.make_async_copy(out_ref.at[s], out_hbm.at[s], sems.at[s])
            copy.start()
            copies.append(copy)
    for copy in copies:
        copy.wait()


def factors_of(pieces):
    return pl.pallas_call(
        factor_kernel,
        out_shape=jax.ShapeDtypeStruct((CAP, 2, TILE, TILE), F32),
        in_specs=[VMEM],
        out_specs=pl.BlockSpec(memory_space=pltpu.HBM),
        scratch_shapes=[
            pltpu.VMEM((CAP, 2, TILE, TILE), F32),
            pltpu.SemaphoreType.DMA((CAP,)),
        ],
        compiler_params=limit(8),
        name="factors",
    )(pieces)


SWAP = ((0, 1), (1, 0))
CHIP_AXES = ("x", "yh")
PLANE_AXES = ("x", "yl", "yh")


def body(hidden_in, query, key_value, grad_out, lengths, owner):
    mine = lax.all_to_all(
        jnp.broadcast_to(key_value, (CHIPS, ROWS, 2 * HD)), CHIP_AXES, 0, 0, tiled=True
    )
    other = lax.ppermute(mine, "core", SWAP)
    q_rows, go_rows, row_low, place = prepare(
        lengths, owner.reshape(1, TILES), query[0], grad_out[0]
    )
    send, w, ds, ds_other = attention(q_rows, go_rows, row_low, mine, other)
    arrived = lax.ppermute(send, "core", SWAP)
    keep, dq_t = own_keys(q_rows, go_rows, mine, w, ds)
    dkv = (keep + arrived.astype(F32)).astype(BF16)
    dkv = lax.all_to_all(dkv, CHIP_AXES, 0, 0, tiled=True)
    hidden = hidden_in[0]
    low, k_t, send = weight_send(dkv, hidden)
    arrived = lax.ppermute(send, "core", SWAP)
    keep, grad_query, grad_kv = weight_keep(k_t, hidden, dq_t, ds_other, other, low, dkv)
    wg = (keep + arrived.astype(F32)).astype(BF16).reshape(PLANE, TILES * 4, TILE)
    wg = lax.all_to_all(wg, PLANE_AXES, 0, 0, tiled=True)
    outgoing = to_owners(place, wg)
    incoming = lax.all_to_all(outgoing, "z", 0, 0, tiled=True)
    pieces = lax.all_to_all(owned_sum(incoming), PLANE_AXES + ("core",), 0, 0, tiled=True)
    return grad_query[None], grad_kv[None], factors_of(pieces)[None]


def solution(mesh):
    fine = Mesh(
        mesh.devices.reshape(N_YL, N_Z, N_X, N_YH, 2), ("yl", "z", "x", "yh", "core")
    )
    dp, ctx = ("yl", "z"), ("x", "yh", "core")
    split = P(dp, ctx, None)
    return jax.shard_map(
        body,
        mesh=fine,
        in_specs=(split, split, split, split, P(dp, None), P()),
        out_specs=(split, split, P(dp, None, None, None, None)),
        check_vma=False,
    )
```

```python
import math

import jax
import jax.numpy as jnp
from jax import lax
from jax.experimental import pallas as pl
from jax.experimental.pallas import tpu as pltpu
from jax.sharding import Mesh
from jax.sharding import PartitionSpec as P

HEADS = 8
HD = 128
TILE = 128
ROWS = 128
CHIPS = 8
SEQ = 2048
HALF = SEQ // 2
TILES = 64
CAP = 4
N_DP = 32
MODEL = 8192
N_YL = 2
N_Z = 16
N_X = 4
N_YH = 2
PLANE = N_YL * CHIPS
OWNED = N_YL * CAP * 4
GROUP = 2
HIDDEN_NEG = -1e30
SCALE = 1.0 / math.sqrt(HD)
EXP2_SCALE = SCALE * math.log2(math.e)
F32 = jnp.float32
BF16 = jnp.bfloat16


def first_position():
    chip = N_YH * lax.axis_index("x") + lax.axis_index("yh")
    return (2 * chip + lax.axis_index("core")) * ROWS


def slot_table(owner):
    across = jnp.broadcast_to(owner.astype(F32), (TILES, TILES))
    earlier = lax.broadcasted_iota(jnp.int32, (TILES, TILES), 0) < lax.broadcasted_iota(
        jnp.int32, (TILES, TILES), 1
    )
    same = jnp.where((across.T == across) & earlier, 1.0, 0.0)
    slot = jnp.sum(same, axis=0, keepdims=True).astype(jnp.int32)
    return ((owner & (N_Z - 1)) * N_YL + (owner >> 4)) * CAP + slot


def prepare_kernel(
    lengths_hbm, owner_hbm, q_hbm, go_hbm,
    q_rows, go_rows, low_ref, place_ref,
    lengths_ref, owner_ref, q_ref, go_ref, sems,
):
    copies = [
        pltpu.make_async_copy(lengths_hbm, lengths_ref, sems.at[0]),
        pltpu.make_async_copy(owner_hbm, owner_ref, sems.at[1]),
        pltpu.make_async_copy(q_hbm, q_ref, sems.at[2]),
        pltpu.make_async_copy(go_hbm, go_ref, sems.at[3]),
    ]
    for copy in copies:
        copy.start()
    first = first_position()
    row_pos = first + lax.broadcasted_iota(jnp.int32, low_ref.shape, 1)
    row_low = jnp.zeros(low_ref.shape, jnp.int32)
    end = jnp.int32(0)
    copies[0].wait()
    for d in range(lengths_ref.shape[1]):
        end = end + lengths_ref[0, d]
        row_low = jnp.maximum(row_low, jnp.where(row_pos >= end, end, 0))
    low_ref[...] = row_low
    copies[1].wait()
    place_ref[...] = slot_table(owner_ref[...])
    for copy, rows, ref in ((copies[2], q_rows, q_ref), (copies[3], go_rows, go_ref)):
        copy.wait()
        for h in range(HEADS):
            cols = pl.ds(h * HD, HD)
            rows[cols, :] = ref[:, cols]


def side_of(ref, part):
    return ref[:, :, part * HD : (part + 1) * HD].reshape(HALF, HD)


def products(w, ds, q_rows, go_rows):
    dk = jnp.dot(ds[...], q_rows[...], preferred_element_type=F32) * SCALE
    dv = jnp.dot(w[...], go_rows[...], preferred_element_type=F32)
    return dk.reshape(CHIPS, ROWS, HD), dv.reshape(CHIPS, ROWS, HD)


def query_part(ds, ref):
    return lax.dot_general(
        side_of(ref, 0), ds[...], (((0,), (0,)), ((), ())), preferred_element_type=F32
    )


def attention_kernel(
    q_rows, go_rows, low_ref, mine_ref, other_ref,
    send_ref, w_mine, ds_mine, ds_other,
    w_other, probs, top, total, delta,
):
    core = lax.axis_index("core")
    first = first_position()
    row_pos = first + lax.broadcasted_iota(jnp.int32, (1, ROWS), 1)
    row_low = low_ref[0:1, :]
    groups = [pl.ds(g * GROUP * HD, GROUP * HD) for g in range(HEADS // GROUP)]
    sides = (
        (0, other_ref, 1 - core, w_other, ds_other),
        (1, mine_ref, core, w_mine, ds_mine),
    )

    def fold(values, op):
        return op(values.reshape(values.shape[0] // 8, 8, values.shape[1]), axis=0)

    def against(rows, ref, cols):
        return lax.dot_general(
            rows, ref[cols, :], (((1,), (1,)), ((), ())), preferred_element_type=F32
        )

    def scores_of(ref, side):
        shape = (CHIPS, ROWS, ROWS)
        chip = lax.broadcasted_iota(jnp.int32, shape, 0)
        pos = (2 * chip + side) * ROWS + lax.broadcasted_iota(jnp.int32, shape, 1)
        pos = pos.reshape(HALF, ROWS)
        seen = (pos >= row_low) & (pos <= row_pos)
        seen = jnp.concatenate([seen] * GROUP, axis=1)
        keys = side_of(ref, 0)
        return lambda cols: jnp.where(seen, against(keys, q_rows, cols), HIDDEN_NEG)

    for i, ref, side, _, _ in sides:
        scores = scores_of(ref, side)
        for cols in groups:
            best = fold(scores(cols), jnp.max)
            top[:, cols] = best if i == 0 else jnp.maximum(top[:, cols], best)
    top[0:1, :] = jnp.max(top[...], axis=0, keepdims=True)
    for i, ref, side, _, _ in sides:
        scores = scores_of(ref, side)
        values = side_of(ref, 1)
        for cols in groups:
            pg = against(values, go_rows, cols)
            p = jnp.exp2((scores(cols) - top[0:1, cols]) * EXP2_SCALE)
            probs[pl.ds(i * HALF, HALF), cols] = p
            p_sum, pg_sum = fold(p, jnp.sum), fold(p * pg, jnp.sum)
            total[:, cols] = p_sum if i == 0 else total[:, cols] + p_sum
            delta[:, cols] = pg_sum if i == 0 else delta[:, cols] + pg_sum
    inverse = 1.0 / jnp.sum(total[...], axis=0, keepdims=True)
    total[0:1, :] = inverse
    delta[0:1, :] = jnp.sum(delta[...], axis=0, keepdims=True) * inverse
    for i, ref, _, w_ref, ds_ref in sides:
        values = side_of(ref, 1)
        for cols in groups:
            w = probs[pl.ds(i * HALF, HALF), cols] * total[0:1, cols]
            w_ref[:, cols] = w.astype(BF16)
            pg = against(values, go_rows, cols)
            ds_ref[:, cols] = (w * (pg - delta[0:1, cols])).astype(BF16)
    dk, dv = products(w_other, ds_other, q_rows, go_rows)
    send_ref[:, :, :HD] = dk.astype(BF16)
    send_ref[:, :, HD:] = dv.astype(BF16)


def own_kernel(q_rows, go_rows, mine_ref, w_mine, ds_mine, keep_ref, dq_t):
    dk, dv = products(w_mine, ds_mine, q_rows, go_rows)
    keep_ref[:, :, :HD] = dk
    keep_ref[:, :, HD:] = dv
    dq_t[...] = query_part(ds_mine, mine_ref)


VMEM = pl.BlockSpec(memory_space=pltpu.VMEM)
SMEM = pl.BlockSpec(memory_space=pltpu.SMEM)


def in_hbm(x):
    return pltpu.with_memory_space_constraint(x, pltpu.HBM)


def limit(mib):
    return pltpu.CompilerParams(vmem_limit_bytes=mib * 1024 * 1024)


def spread_kernel(kv_hbm, out_ref, sems):
    copies = [
        pltpu.make_async_copy(kv_hbm.at[0], out_ref.at[i], sems.at[i]) for i in range(CHIPS)
    ]
    for copy in copies:
        copy.start()
    for copy in copies:
        copy.wait()


def spread(key_value):
    return pl.pallas_call(
        spread_kernel,
        out_shape=jax.ShapeDtypeStruct((CHIPS, ROWS, 2 * HD), BF16),
        in_specs=[pl.BlockSpec(memory_space=pltpu.HBM)],
        out_specs=VMEM,
        scratch_shapes=[pltpu.SemaphoreType.DMA((CHIPS,))],
        compiler_params=limit(8),
        name="spread_kv",
    )(in_hbm(key_value))


def prepare(lengths, owner, query, grad_out):
    hbm = pl.BlockSpec(memory_space=pltpu.HBM)
    wide = HEADS * HD
    return pl.pallas_call(
        prepare_kernel,
        out_shape=(
            jax.ShapeDtypeStruct((wide, HD), BF16),
            jax.ShapeDtypeStruct((wide, HD), BF16),
            jax.ShapeDtypeStruct((8, ROWS), jnp.int32),
            jax.ShapeDtypeStruct((1, TILES), jnp.int32),
        ),
        in_specs=[hbm] * 4,
        out_specs=(VMEM,) * 4,
        scratch_shapes=[
            pltpu.SMEM((1, 8), jnp.int32),
            pltpu.VMEM((1, TILES), jnp.int32),
            pltpu.VMEM((ROWS, wide), BF16),
            pltpu.VMEM((ROWS, wide), BF16),
            pltpu.SemaphoreType.DMA((4,)),
        ],
        compiler_params=limit(8),
        name="prepare_rows",
    )(in_hbm(lengths), in_hbm(owner), in_hbm(query), in_hbm(grad_out))


def attention(q_rows, go_rows, row_low, mine, other):
    wide = HEADS * HD
    half = jax.ShapeDtypeStruct((HALF, wide), BF16)
    return pl.pallas_call(
        attention_kernel,
        out_shape=(
            jax.ShapeDtypeStruct((CHIPS, ROWS, 2 * HD), BF16),
            half,
            half,
            half,
        ),
        in_specs=[VMEM] * 5,
        out_specs=(VMEM,) * 4,
        scratch_shapes=[
            pltpu.VMEM((HALF, wide), BF16),
            pltpu.VMEM((SEQ, wide), F32),
            pltpu.VMEM((8, wide), F32),
            pltpu.VMEM((8, wide), F32),
            pltpu.VMEM((8, wide), F32),
        ],
        compiler_params=limit(24),
        name="attention_backward",
    )(q_rows, go_rows, row_low, mine, other)


def own_keys(q_rows, go_rows, mine, w, ds):
    return pl.pallas_call(
        own_kernel,
        out_shape=(
            jax.ShapeDtypeStruct((CHIPS, ROWS, 2 * HD), F32),
            jax.ShapeDtypeStruct((HD, HEADS * HD), F32),
        ),
        in_specs=[VMEM] * 5,
        out_specs=(VMEM, VMEM),
        compiler_params=limit(12),
        name="own_keys",
    )(q_rows, go_rows, mine, w, ds)


def low_half(shape, axis):
    return lax.broadcasted_iota(jnp.int32, shape, axis) < 4


def halves(keys):
    rows = keys.T.reshape(PLANE // 2, 2, 8, ROWS)
    even, odd = rows[:, 0], rows[:, 1]
    low = low_half(even.shape, 1)
    first = jnp.where(low, even, pltpu.roll(odd, 4, axis=1))
    second = jnp.where(low, pltpu.roll(even, 4, axis=1), odd)
    return first.reshape(HD // 2, ROWS), second.reshape(HD // 2, ROWS)


def half_tiles(k_t, hidden_ref, out_ref):
    shape = (PLANE // 2, 8, TILE)
    low = low_half(shape, 1)
    for quad in range(TILES // 4):
        hidden = hidden_ref[:, pl.ds(quad * 4 * TILE, 4 * TILE)]
        grad_t = jnp.dot(k_t, hidden, preferred_element_type=F32)
        tiles = [grad_t[:, i * TILE : (i + 1) * TILE].reshape(shape) for i in range(4)]
        evens, odds = [], []
        for even, odd in (tiles[:2], tiles[2:]):
            evens.append(jnp.where(low, even, pltpu.roll(odd, 4, axis=1)))
            odds.append(jnp.where(low, pltpu.roll(even, 4, axis=1), odd))
        rows = pl.ds(quad * 16, 16)
        out_ref[:, 0, rows, :] = jnp.concatenate(evens, axis=1).astype(out_ref.dtype)
        out_ref[:, 1, rows, :] = jnp.concatenate(odds, axis=1).astype(out_ref.dtype)


def position_sums(parts_ref, part):
    return jnp.sum(parts_ref[:, :, part * HD : (part + 1) * HD].astype(F32), axis=0).astype(BF16)


def weight_send_kernel(parts_ref, hidden_ref, low_ref, k_ref, out_ref):
    core = lax.axis_index("core")
    low = position_sums(parts_ref, 0)
    low_ref[...] = low
    first, second = halves(low.astype(F32))
    k_ref[...] = jnp.where(core == 0, first, second).astype(BF16)
    half_tiles(jnp.where(core == 0, second, first).astype(BF16), hidden_ref, out_ref)


def weight_keep_kernel(
    k_ref, hidden_ref, dq_t, ds_other, other_ref, low_ref, parts_ref, out_ref, dq_ref, kv_ref, dq_all
):
    kv_ref[:, :HD] = low_ref[...]
    kv_ref[:, HD:] = position_sums(parts_ref, 1)
    half_tiles(k_ref[...], hidden_ref, out_ref)
    dq_all[...] = dq_t[...] + query_part(ds_other, other_ref)
    for h in range(HEADS):
        cols = pl.ds(h * HD, HD)
        dq_ref[:, cols] = (dq_all[:, cols].T * SCALE).astype(BF16)


def weight_send(parts, hidden):
    return pl.pallas_call(
        weight_send_kernel,
        out_shape=(
            jax.ShapeDtypeStruct((ROWS, HD), BF16),
            jax.ShapeDtypeStruct((HD // 2, ROWS), BF16),
            jax.ShapeDtypeStruct((PLANE // 2, 2, TILES * 4, TILE), BF16),
        ),
        in_specs=[VMEM, VMEM],
        out_specs=(VMEM, VMEM, VMEM),
        compiler_params=limit(10),
        name="weight_tiles_to_send",
    )(parts, hidden)


def weight_keep(k_t, hidden, dq_t, ds_other, other, low, parts):
    return pl.pallas_call(
        weight_keep_kernel,
        out_shape=(
            jax.ShapeDtypeStruct((PLANE // 2, 2, TILES * 4, TILE), F32),
            jax.ShapeDtypeStruct((ROWS, HEADS * HD), BF16),
            jax.ShapeDtypeStruct((ROWS, 2 * HD), BF16),
        ),
        in_specs=[VMEM] * 7,
        out_specs=(VMEM,) * 3,
        scratch_shapes=[pltpu.VMEM((HD, HEADS * HD), F32)],
        compiler_params=limit(12),
        name="weight_tiles_to_keep",
    )(k_t, hidden, dq_t, ds_other, other, low, parts)


def owner_kernel(place_ref, parts_ref, out_ref, sums, placed):
    rows = TILES * 4
    own = jnp.sum(parts_ref[...].astype(F32), axis=0)
    sums[:rows, :] = own
    sums[rows:, :] = pltpu.roll(own.reshape(rows // 8, 8, TILE), 4, axis=1).reshape(rows, TILE)
    placed[...] = jnp.zeros(placed.shape, F32)
    for t in range(TILES):
        place = place_ref[0, t]
        at = pl.ds(pl.multiple_of(place * 8, 8), 8)
        source = pl.multiple_of(((place & 1) ^ (t & 1)) * rows + (t // 2) * 8, 8)
        placed[at, :] = sums[pl.ds(source, 8), :]
    pairs = placed[...].reshape(N_DP * CAP // 2, 2, 8, TILE)
    low = low_half((N_DP * CAP // 2, 8, TILE), 1)
    merged = jnp.where(low, pairs[:, 0], pairs[:, 1])
    out_ref[...] = merged.reshape(out_ref.shape).astype(BF16)


def to_owners(place, parts):
    return pl.pallas_call(
        owner_kernel,
        out_shape=jax.ShapeDtypeStruct((N_Z, OWNED, TILE), BF16),
        in_specs=[pl.BlockSpec(memory_space=pltpu.SMEM), VMEM],
        out_specs=VMEM,
        scratch_shapes=[
            pltpu.VMEM((2 * TILES * 4, TILE), F32),
            pltpu.VMEM((N_DP * CAP * 8, TILE), F32),
        ],
        compiler_params=limit(12),
        name="owner_slots",
    )(place, parts)


def sum_kernel(parts_ref, out_ref):
    gradient = jnp.sum(parts_ref[...].astype(F32), axis=0) * (1.0 / math.sqrt(N_DP * SEQ))
    gradient = gradient.astype(BF16)
    rows = OWNED // N_YL
    some = 2 * N_YH
    for yl in range(N_YL):
        piece = gradient[yl * rows : (yl + 1) * rows]
        piece = jnp.broadcast_to(piece[None], (some, rows, TILE))
        for x in range(N_X):
            at = (x * N_YL + yl) * some
            out_ref[at : at + some] = piece


def owned_sum(parts):
    return pl.pallas_call(
        sum_kernel,
        out_shape=jax.ShapeDtypeStruct((2 * PLANE, OWNED // N_YL, TILE), BF16),
        in_specs=[VMEM],
        out_specs=VMEM,
        compiler_params=limit(8),
        name="owned_sum",
    )(parts)


def factor_kernel(pieces_ref, out_hbm, out_ref, sems):
    pieces = pieces_ref[...].astype(F32)
    low = low_half((PLANE, 8, TILE), 1)
    copies = []
    for two in range(CAP // 2):
        pair = pieces[:, two * 8 : (two + 1) * 8, :].reshape(PLANE, 2, 8, TILE)
        even, odd = pair[:, 0], pair[:, 1]
        both = (
            jnp.where(low, even, pltpu.roll(odd, 4, axis=1)),
            jnp.where(low, pltpu.roll(even, 4, axis=1), odd),
        )
        for i in range(2):
            grad_t = both[i].reshape(TILE, TILE)
            flat = grad_t.astype(BF16)
            flat_t = flat.T
            s = 2 * two + i
            out_ref[s, 0] = jnp.dot(flat_t, flat, preferred_element_type=F32) * (1.0 / TILE)
            out_ref[s, 1] = jnp.dot(flat, flat_t, preferred_element_type=F32) * (1.0 / TILE)
            copy = pltpu.make_async_copy(out_ref.at[s], out_hbm.at[s], sems.at[s])
            copy.start()
            copies.append(copy)
    for copy in copies:
        copy.wait()


def factors_of(pieces):
    return pl.pallas_call(
        factor_kernel,
        out_shape=jax.ShapeDtypeStruct((CAP, 2, TILE, TILE), F32),
        in_specs=[VMEM],
        out_specs=pl.BlockSpec(memory_space=pltpu.HBM),
        scratch_shapes=[
            pltpu.VMEM((CAP, 2, TILE, TILE), F32),
            pltpu.SemaphoreType.DMA((CAP,)),
        ],
        compiler_params=limit(8),
        name="factors",
    )(pieces)


SWAP = ((0, 1), (1, 0))
CHIP_AXES = ("x", "yh")
PLANE_AXES = ("x", "yl", "yh")


def body(hidden_in, query, key_value, grad_out, lengths, owner):
    mine = lax.all_to_all(
        spread(key_value), CHIP_AXES, 0, 0, tiled=True
    )
    other = lax.ppermute(mine, "core", SWAP)
    q_rows, go_rows, row_low, place = prepare(
        lengths, owner.reshape(1, TILES), query[0], grad_out[0]
    )
    send, w, ds, ds_other = attention(q_rows, go_rows, row_low, mine, other)
    arrived = lax.ppermute(send, "core", SWAP)
    keep, dq_t = own_keys(q_rows, go_rows, mine, w, ds)
    dkv = (keep + arrived.astype(F32)).astype(BF16)
    dkv = lax.all_to_all(dkv, CHIP_AXES, 0, 0, tiled=True)
    hidden = hidden_in[0]
    low, k_t, send = weight_send(dkv, hidden)
    arrived = lax.ppermute(send, "core", SWAP)
    keep, grad_query, grad_kv = weight_keep(k_t, hidden, dq_t, ds_other, other, low, dkv)
    wg = (keep + arrived.astype(F32)).astype(BF16).reshape(PLANE, TILES * 4, TILE)
    wg = lax.all_to_all(wg, PLANE_AXES, 0, 0, tiled=True)
    outgoing = to_owners(place, wg)
    incoming = lax.all_to_all(outgoing, "z", 0, 0, tiled=True)
    pieces = lax.all_to_all(owned_sum(incoming), PLANE_AXES + ("core",), 0, 0, tiled=True)
    return grad_query[None], grad_kv[None], factors_of(pieces)[None]


def solution(mesh):
    fine = Mesh(
        mesh.devices.reshape(N_YL, N_Z, N_X, N_YH, 2), ("yl", "z", "x", "yh", "core")
    )
    dp, ctx = ("yl", "z"), ("x", "yh", "core")
    split = P(dp, ctx, None)
    return jax.shard_map(
        body,
        mesh=fine,
        in_specs=(split, split, split, split, P(dp, None), P()),
        out_specs=(split, split, P(dp, None, None, None, None)),
        check_vma=False,
    )
```
